32 devices in a mesh: dp: 8 (over y, x, core), fsdp: 4 (over z).
Axes of the slice: x: 2, y: 2, z: 4, core: 2. Of those that a mesh axis runs over, the one named last changes fastest.
Arguments:
- tokens: bfloat16 [64, 512, 768], P(('dp', 'fsdp')), may hold values from -6 to 6
- segment_ids: int32 [64, 512], P(('dp', 'fsdp')), may hold values from 0 to 3, never falling along the last dimension, each value on 1 to 256 neighbouring positions
- bucket_ids: int32 [64, 512, 8], P(('dp', 'fsdp')), may hold values from 0 to 16383
- cotangent: bfloat16 [64, 512, 768], P(('dp', 'fsdp')), may hold values from -6 to 6
- qkv_weight: bfloat16 [768, 2304], P(('dp', 'fsdp')), may hold values from -0.21875 to 0.21875
- out_weight: bfloat16 [768, 768], P(('dp', 'fsdp')), may hold values from -1.75 to 1.75
- up_weight: bfloat16 [768, 3072], P(('dp', 'fsdp')), may hold values from -0.21875 to 0.21875
- down_weight: bfloat16 [3072, 768], P(('dp', 'fsdp')), may hold values from -0.21875 to 0.21875
- attn_gain: bfloat16 [768], P(('dp', 'fsdp')), may hold values from 0.25 to 1.75
- attn_bias: bfloat16 [768], P(('dp', 'fsdp')), may hold values from -3 to 3
- ffn_gain: bfloat16 [768], P(('dp', 'fsdp')), may hold values from 0.25 to 1.75
- ffn_bias: bfloat16 [768], P(('dp', 'fsdp')), may hold values from -3 to 3
Outputs:
- layer_output: bfloat16 [64, 512, 768], P(('dp', 'fsdp'))
- tokens_grad: bfloat16 [64, 512, 768], P(('dp', 'fsdp'))
- qkv_grad: float32 [768, 2304], P(('dp', 'fsdp'))
- out_grad: float32 [768, 768], P(('dp', 'fsdp'))
- up_grad: float32 [768, 3072], P(('dp', 'fsdp'))
- down_grad: float32 [3072, 768], P(('dp', 'fsdp'))
- attn_gain_grad: float32 [768], P(('dp', 'fsdp'))
- attn_bias_grad: float32 [768], P(('dp', 'fsdp'))
- ffn_gain_grad: float32 [768], P(('dp', 'fsdp'))
- ffn_bias_grad: float32 [768], P(('dp', 'fsdp'))
- bucket_counts: int32 [8, 16384], replicated
The draws below stay inside these ranges and needn't reach their ends.
Inputs may be any that keep to these rules, and one draw needn't show every extreme that they name: `segment_ids`: within each packed row the numbers never fall and start at 0; a document has at most 256 molecules.
All inputs are finite; a program needn't handle non-finite values.
Results may differ from the reference program's by a relative error of at most 0.014.
Values may be sent and summed in bfloat16 or wider, within the bound.
No kernel may reach another device: no remote copies, remote signals or barrier semaphores. Data moves between devices by JAX's collectives and lax.ppermute only.
A program may use at most 192 MiB of HBM per device.

```python
import math
import jax
import jax.numpy as jnp
import numpy as np
from jax import lax

D = 768
H = 12
HD = 64
FF = 3072
L = 512
TABLES = 8
BUCKETS = 16384
ROWS = 64


def touch_ends(values, stream_key, least, top_value):
    longest = values.shape.index(max(values.shape))
    spots = []
    for shift in (0, 1):
        where = [jax.random.randint(jax.random.fold_in(stream_key, axis), (), 0, length) for axis, length in enumerate(values.shape)]
        where[longest] = (where[longest] + shift) % values.shape[longest]
        spots.append(tuple(where))
    return values.at[spots[0]].set(least).at[spots[1]].set(top_value)


def level_of(own_key, extent, shards, low, top_value):
    loudness = 1.0
    for dim, blocks in shards:
        heights = jax.random.uniform(jax.random.fold_in(jax.random.fold_in(own_key, 6), dim), (blocks,), jnp.float32, low / len(shards), top_value / len(shards))
        loudness = loudness * jnp.repeat(jnp.exp(heights), extent[dim] // blocks).reshape((-1,) + (1,) * (len(extent) - 1 - dim))
    return loudness


def cumulative_ranks(amount, slope):
    weights = [(1 << 20) // math.isqrt(grade ** slope) + 1 for grade in range(1, amount + 1)]
    scale = 1 + sum(weights) // (1 << 30)
    return np.cumsum(np.array([max(1, weight // scale) for weight in weights]))


def ranked_ids(stream_key, extent, number_of, skew):
    grid = cumulative_ranks(number_of, skew)
    pick = jax.random.randint(jax.random.fold_in(stream_key, 1), extent, 0, int(grid[number_of - 1]))
    grade = jnp.searchsorted(jnp.asarray(grid, jnp.int32), pick, side="right")
    return jax.random.permutation(jax.random.fold_in(stream_key, 2), number_of)[grade].astype(jnp.int32)


def length_profile(number_of, total, limit, lean):
    loads = [(1 << 20) // math.isqrt(standing ** lean) + 1 for standing in range(2, number_of + 1)]
    surplus, holding = total - limit - (number_of - 1), [1] * (number_of - 1)
    while surplus > 0:
        free = [i for i in range(number_of - 1) if holding[i] < limit]
        pool, budget = sum([loads[i] for i in free]), surplus
        for i in free:
            addition = min(limit - holding[i], max(1, budget * loads[i] // pool), surplus)
            holding[i] = holding[i] + addition
            surplus = surplus - addition
    return np.array([limit] + holding)


def ragged(key, count, total, reach, skew):
    if count == 2:
        one = jax.random.randint(key, (), max(1, total - reach), min(reach, total - 1) + 1)
        return jnp.stack([one, total - one])
    tallies = jnp.asarray(length_profile(count, total, reach, skew), jnp.int32)
    twos = (count - 1) // 2
    source_of, taker = tallies[1:1 + 2 * twos:2], tallies[2:2 + 2 * twos:2]
    slack = jnp.minimum(source_of - 1, reach - taker)
    passed = jax.random.randint(jax.random.fold_in(key, 1), (twos,), 0, 1 << 20) % (slack + 1)
    tallies = tallies.at[1:1 + 2 * twos:2].set(source_of - passed).at[2:2 + 2 * twos:2].set(taker + passed)
    return tallies[jax.random.permutation(jax.random.fold_in(key, 2), count)]


def scatter_about(rng, shape, scale, bound, shards=(), kind=jnp.bfloat16):
    factor_of = level_of(rng, shape, shards, -0.22, 0.18) if shards else 1.0
    array = jax.random.normal(rng, shape, jnp.float32) * scale * factor_of
    return jnp.minimum(jnp.maximum(array, -bound), bound).astype(kind)


def setup_inputs(seed: int = 0) -> dict:
    seeds = jax.random.split(jax.random.key(seed), 13)
    tokens = scatter_about(seeds[0], (ROWS, L, D), 1.0, 6.0, ((0, 32),))
    segment_ids = jax.vmap(lambda own: jnp.searchsorted(jnp.cumsum(ragged(own, 4, L, L // 2, 0)), jnp.arange(L), side="right"))(jax.random.split(seeds[1], ROWS)).reshape((ROWS, L)).astype(jnp.int32)
    bucket_ids = touch_ends(ranked_ids(seeds[2], (ROWS, L, TABLES), BUCKETS, 2), jax.random.fold_in(seeds[2], 3), 0, BUCKETS - 1).astype(jnp.int32)
    cotangent = scatter_about(seeds[3], (ROWS, L, D), 1.0, 6.0, ((0, 32),))
    qkv_weight = scatter_about(seeds[4], (D, 3 * D), D ** -0.5, 0.21875, ((0, 32),))
    out_weight = scatter_about(seeds[5], (D, D), (D // 64) ** -0.5, 1.75, ((0, 32),))
    up_weight = scatter_about(seeds[6], (D, FF), D ** -0.5, 0.21875, ((0, 32),))
    down_weight = scatter_about(seeds[7], (FF, D), (FF // 4) ** -0.5, 0.21875, ((0, 32),))
    attn_gain = jnp.clip(1.0 + 0.15 * jax.random.normal(seeds[8], (D,), jnp.float32), 0.25, 1.75).astype(jnp.bfloat16)
    attn_bias = scatter_about(seeds[9], (D,), 0.5, 3.0, ((0, 32),))
    ffn_gain = jnp.clip(1.0 + 0.15 * jax.random.normal(seeds[10], (D,), jnp.float32), 0.25, 1.75).astype(jnp.bfloat16)
    ffn_bias = scatter_about(seeds[11], (D,), 0.5, 3.0, ((0, 32),))
    return {"tokens": tokens, "segment_ids": segment_ids, "bucket_ids": bucket_ids, "cotangent": cotangent, "qkv_weight": qkv_weight, "out_weight": out_weight, "up_weight": up_weight, "down_weight": down_weight, "attn_gain": attn_gain, "attn_bias": attn_bias, "ffn_gain": ffn_gain, "ffn_bias": ffn_bias}


@jax.custom_vjp
def low(v):
    return lax.optimization_barrier(v.astype(jnp.bfloat16)).astype(jnp.float32)

@jax.custom_vjp
def low_back(v):
    return v

def low_keep(v):
    return (low(v), None)

def low_pass(kept, grad):
    return (grad,)

def back_keep(v):
    return (v, None)

def back_low(kept, grad):
    return (low(grad),)
low.defvjp(low_keep, low_pass)
low_back.defvjp(back_keep, back_low)
HIGH = lax.Precision.HIGHEST

def layer_norm(values, gain, bias):
    centered = values - lax.optimization_barrier(jnp.mean(values, axis=-1, keepdims=True))
    spread = lax.optimization_barrier(jnp.mean(centered * centered, axis=-1, keepdims=True))
    return centered * lax.rsqrt(spread + 1e-12) * gain + bias

def layer_row(x_row, seg_row, weights):
    qkv_weight, out_weight, up_weight, down_weight, attn_gain, attn_bias, ffn_gain, ffn_bias = weights
    length = x_row.shape[0]
    h1 = low(layer_norm(x_row, attn_gain, attn_bias))
    qkv = low(low_back(jnp.dot(h1, qkv_weight, precision=HIGH)))
    queries = qkv[:, :D].reshape(length, H, HD)
    keys = qkv[:, D:2 * D].reshape(length, H, HD)
    values = qkv[:, 2 * D:].reshape(length, H, HD)
    raw = low_back(jnp.einsum('qhd,khd->hqk', queries, keys, precision=HIGH) * (1.0 / HD ** 0.5))
    same = seg_row[:, None] == seg_row[None, :]
    scores = jnp.where(same[None], raw, -1e+30)
    top = lax.optimization_barrier(jnp.max(scores, axis=-1, keepdims=True))
    expo = jnp.exp(scores - top)
    probs = low(expo / lax.optimization_barrier(jnp.sum(expo, axis=-1, keepdims=True)))
    mixed = jnp.einsum('hqk,khd->qhd', probs, values, precision=HIGH).reshape(length, D)
    mixed = low(low_back(mixed))
    y1 = x_row + low_back(jnp.dot(mixed, out_weight, precision=HIGH))
    h2 = low(layer_norm(y1, ffn_gain, ffn_bias))
    upper = low_back(jnp.dot(h2, up_weight, precision=HIGH))
    act = low(jax.nn.gelu(upper, approximate=True))
    return y1 + low_back(jnp.dot(act, down_weight, precision=HIGH))

def reference(tokens, segment_ids, bucket_ids, cotangent, qkv_weight, out_weight, up_weight, down_weight, attn_gain, attn_bias, ffn_gain, ffn_bias):
    weights = tuple((w.astype(jnp.float32) for w in (qkv_weight, out_weight, up_weight, down_weight, attn_gain, attn_bias, ffn_gain, ffn_bias)))
    x_all = tokens.astype(jnp.float32)

    def forward(x_in, *wts):
        row_fn = jax.checkpoint(layer_row)
        return lax.map(lambda pair: row_fn(pair[0], pair[1], wts), (x_in, segment_ids))
    result, pullback = jax.vjp(forward, x_all, *weights)
    grads = pullback(cotangent.astype(jnp.float32))
    flat = bucket_ids.reshape(-1, TABLES)
    ones = jnp.ones((flat.shape[0],), jnp.int32)
    counts = jax.vmap(lambda column: jax.ops.segment_sum(ones, column, num_segments=BUCKETS), in_axes=1)(flat)
    return (result.astype(jnp.bfloat16), grads[0].astype(jnp.bfloat16), grads[1], grads[2], grads[3], grads[4], grads[5], grads[6], grads[7], grads[8], counts.astype(jnp.int32))
```

```python
import functools

import jax
import jax.numpy as jnp
from jax import lax
from jax.experimental import pallas as pl
from jax.experimental.pallas import tpu as pltpu
from jax.sharding import PartitionSpec as P

H = 12
BUCKETS = 16384
LOW = 256
BLOCKS = 8
CORE, NEAR_X, NEAR_Y = 1, 2, 4
PLACES = (0, NEAR_X, NEAR_Y, NEAR_X + NEAR_Y)
BOTH = ("dp", "fsdp")


def swap(value, bit):
    return lax.ppermute(value, "dp", [(i, i ^ bit) for i in range(BLOCKS)])


def swap_inner(value, bit, size):
    return lax.ppermute(value, "fsdp", [(i, i ^ bit) for i in range(size)])


def by_bits(parts, index):
    bit = 1
    while bit < len(parts):
        odd = (index & bit) != 0
        parts = [jnp.where(odd, parts[j ^ bit], parts[j]) for j in range(len(parts))]
        bit *= 2
    return parts


def direct(ranks, inner):
    return ranks == BLOCKS and inner & (inner - 1) == 0


def gather_whole(shard):
    near = lax.all_gather(shard, "fsdp", axis=0, tiled=True)
    whole = lax.all_gather(near, "dp", axis=0, tiled=True)
    whole = whole.reshape(4, 2, -1, whole.shape[1])
    return [whole[:, 0], whole[:, 1]], [0, CORE]


def gather_inner(shard, inner):
    parts = [shard] + [swap_inner(shard, k, inner) for k in range(1, inner)]
    return jnp.concatenate(by_bits(parts, lax.axis_index("fsdp")), axis=0)


def gather_sides(own):
    return [own] + [swap(own, bits) for bits in PLACES[1:]]


def with_core(pieces):
    joined = jnp.stack(pieces)
    return [joined, swap(joined, CORE)], [0, CORE]


def after(value, *others):
    return lax.optimization_barrier((value, *others))[0]


def together(values, *others):
    return list(lax.optimization_barrier((*values, *others)))[: len(values)]


def gather_first(shards, inner, counts):
    own = gather_inner(shards[0], inner)
    own, second = together([own, shards[1]])
    sides = gather_sides(own)
    parts = [second] + [swap_inner(second, k, inner) for k in range(1, inner)]
    values = together([*sides, *parts])
    sides, parts = values[:4], values[4:]
    keep, other = halve_tables(counts, CORE)
    own_second = jnp.concatenate(by_bits(parts, lax.axis_index("fsdp")), axis=0)
    first = with_core(sides)
    own_second, third, other = together([own_second, shards[2], other], *first[0])
    parts = [swap_inner(third, k, inner) for k in range(1, inner - 1)]
    return first, gather_sides(own_second), [third] + parts, keep, other


def halve_tables(counts, bit):
    tables = counts.shape[0] // 2
    upper = (lax.axis_index("dp") & bit) != 0
    keep = jnp.where(upper, counts[tables:], counts[:tables])
    send = jnp.where(upper, counts[:tables], counts[tables:])
    return keep, swap(send, bit)


def double_tables(counts, other, bit):
    upper = (lax.axis_index("dp") & bit) != 0
    return jnp.concatenate(
        [jnp.where(upper, other, counts), jnp.where(upper, counts, other)], axis=0
    )


def add(*terms):
    total = terms[0].astype(jnp.float32)
    for term in terms[1:]:
        total = total + term.astype(jnp.float32)
    return total.astype(jnp.bfloat16)


def scatter_core(keep, send):
    other = swap(send, CORE)
    return [add(keep[place], other[place]) for place in range(4)]


def scatter_sides(parts):
    return [swap(part, bits) for part, bits in zip(parts[1:], PLACES[1:])]


def scatter_corner(parts):
    half = parts[3].shape[0] // 2
    return [swap(parts[3][:half], NEAR_Y), swap(parts[3][half:], NEAR_X)]


def scatter_rest(parts, corners):
    half = parts[3].shape[0] // 2
    first, second = corners
    to_x = jnp.concatenate([add(parts[1][:half], first), parts[1][half:]], axis=0)
    to_y = jnp.concatenate([parts[2][:half], add(parts[2][half:], second)], axis=0)
    return [swap(to_x, NEAR_X), swap(to_y, NEAR_Y)]


def scatter_inner(mine, inner):
    part = mine.shape[0] // inner
    parts = [mine[j * part : (j + 1) * part] for j in range(inner)]
    parts = by_bits(parts, lax.axis_index("fsdp"))
    return parts[:1] + [swap_inner(parts[k], k, inner) for k in range(1, inner)]


def sum_parts(parts):
    total = parts[0].astype(jnp.float32)
    for part in parts[1:]:
        total = total + part.astype(jnp.float32)
    return total


def scatter_whole(keep, send):
    whole = jnp.stack([keep, send], axis=1).reshape(-1, keep.shape[2])
    near = lax.psum_scatter(whole, "dp", scatter_dimension=0, tiled=True)
    return lax.psum_scatter(near, "fsdp", scatter_dimension=0, tiled=True).astype(jnp.float32)


def piece_pairs(refs, plan, me, block, target, sems, column=0):
    pairs = []
    for ref, first in zip(refs, plan):
        for place, bits in enumerate(PLACES):
            start = pl.multiple_of((me ^ first ^ bits) * block, 16)
            pairs.append(
                (
                    ref.at[place, :, column : column + target.shape[1]],
                    target.at[pl.ds(start, block), :],
                    sems.at[len(pairs)],
                )
            )
    return pairs


def load_pieces(*details):
    copies = [pltpu.make_async_copy(*pair) for pair in piece_pairs(*details)]
    for copy in copies:
        copy.start()
    return copies


def count_kernel(ids_ref, counts_ref):
    _, high_count, low_count = counts_ref.shape
    tables, length = ids_ref.shape
    high_at = lax.broadcasted_iota(jnp.int32, (high_count, length), 0)
    low_at = lax.broadcasted_iota(jnp.int32, (low_count, length), 0)
    for table in range(tables):
        ids = ids_ref[table : table + 1, :]
        upper = lax.shift_right_logical(ids, 8)
        lower = jnp.bitwise_and(ids, low_count - 1)
        counts_ref[table] = dot_nt(
            jnp.where(high_at == upper, 1.0, 0.0).astype(jnp.bfloat16),
            jnp.where(low_at == lower, 1.0, 0.0).astype(jnp.bfloat16),
        ).astype(jnp.int32)


def count_buckets(ids):
    tables = ids.shape[0]
    counts = pl.pallas_call(
        count_kernel,
        out_shape=jax.ShapeDtypeStruct((tables, BUCKETS // LOW, LOW), jnp.int32),
        cost_estimate=pl.CostEstimate(flops=3 * 10**9, bytes_accessed=10**6, transcendentals=0),
    )(ids)
    return counts.reshape(tables, BUCKETS)


def norm_parts(values):
    centered = values - jnp.mean(values, axis=-1, keepdims=True)
    spread = jnp.mean(centered * centered, axis=-1, keepdims=True)
    factor = lax.rsqrt(spread + 1e-12)
    return centered * factor, factor


def dot_nn(first, second):
    return jnp.dot(first, second, preferred_element_type=jnp.float32)


def dot_nt(first, second):
    return lax.dot_general(
        first, second, (((1,), (1,)), ((), ())), preferred_element_type=jnp.float32
    )


def flip_axes(matrix):
    return matrix.T


def attend_kernel(plan, count, me_ref, x_ref, seg_ref, *rest):
    pieces = rest[:count]
    qkv_ref, expo_ref, inv_ref, mixed_ref, ht_ref, o_ref, vec_ref, w_ref, sems = rest[count:]
    length, width = x_ref.shape[1:]
    head_dim = width // H

    @pl.when(pl.program_id(0) == 0)
    def _():
        for copy in load_pieces(pieces, plan, me_ref[0], width // BLOCKS, w_ref, sems):
            copy.wait()
        vec_ref[...] = w_ref[:, 3 * width :].astype(jnp.float32).T[:8]

    normed, _ = norm_parts(x_ref[0].astype(jnp.float32))
    h_one = (normed * vec_ref[0:1] + vec_ref[1:2]).astype(jnp.bfloat16)
    ht_ref[0] = flip_axes(h_one)
    qkv = dot_nn(h_one, w_ref[:, : 3 * width]).astype(jnp.bfloat16)
    qkv_ref[0, :, :width] = qkv[:, :width] * (1.0 / head_dim**0.5)
    qkv_ref[0, :, width:] = qkv[:, width:]
    lane = lax.broadcasted_iota(jnp.int32, (length, 128), 1)
    seg = seg_ref[0]
    key_seg = jnp.where(seg == lane, 1.0, 0.0).astype(jnp.bfloat16)
    query_seg = jnp.where(seg == lane, 0.0, -1e30).astype(jnp.bfloat16)
    for pair in range(H // 2):
        cols = slice(pair * 128, pair * 128 + 128)
        queries = qkv_ref[0, :, cols]
        keys = qkv_ref[0, :, width + pair * 128 : width + pair * 128 + 128]
        values = qkv_ref[0, :, 2 * width + pair * 128 : 2 * width + pair * 128 + 128]
        key_wide = jnp.concatenate([keys, key_seg], axis=1)
        values_t = flip_axes(values)
        parts = []
        for half in range(2):
            inside = (lane < head_dim) if half == 0 else (lane >= head_dim)
            query_half = jnp.where(inside, queries, jnp.zeros_like(queries))
            scores = dot_nt(key_wide, jnp.concatenate([query_half, query_seg], axis=1))
            top = jnp.max(scores, axis=0, keepdims=True)
            expo = jnp.exp(scores - top)
            inverse = 1.0 / jnp.sum(expo, axis=0, keepdims=True)
            expo = expo.astype(jnp.bfloat16)
            expo_ref[0, 2 * pair + half] = expo
            inv_ref[0, 2 * pair + half] = inverse
            out = dot_nn(values_t, expo)
            parts.append(out[half * head_dim : (half + 1) * head_dim] * inverse)
        mixed = jnp.concatenate(parts, axis=0)
        mixed_ref[0, cols, :] = mixed.astype(jnp.bfloat16)
        o_ref[0, :, cols] = mixed.T.astype(jnp.bfloat16)


def whole_spec(shape):
    zeros = (0,) * len(shape)
    return pl.BlockSpec(shape, lambda *_: zeros, pipeline_mode=pl.Buffered(1))


def row_spec(shape):
    rest = (0,) * (len(shape) - 1)
    return pl.BlockSpec((1,) + shape[1:], lambda r, *_: (r,) + rest)


def any_specs(pieces):
    return [pl.BlockSpec(memory_space=pl.ANY) for _ in pieces]


def kernel_params(mebibytes):
    return pltpu.CompilerParams(vmem_limit_bytes=mebibytes * 1024 * 1024)


def attend(tokens, segments, me, pieces, plan):
    rows, length, width = tokens.shape
    shapes = (
        jax.ShapeDtypeStruct((rows, length, 3 * width), jnp.bfloat16),
        jax.ShapeDtypeStruct((rows, H, length, length), jnp.bfloat16),
        jax.ShapeDtypeStruct((rows, H, 1, length), jnp.float32),
        jax.ShapeDtypeStruct((rows, width, length), jnp.bfloat16),
        jax.ShapeDtypeStruct((rows, width, length), jnp.bfloat16),
        jax.ShapeDtypeStruct((rows, length, width), jnp.bfloat16),
        jax.ShapeDtypeStruct((8, width), jnp.float32),
    )
    return list(pl.pallas_call(
        functools.partial(attend_kernel, plan, len(pieces)),
        grid=(rows,),
        in_specs=[
            pl.BlockSpec(memory_space=pltpu.SMEM),
            row_spec(tokens.shape),
            row_spec(segments.shape),
        ]
        + any_specs(pieces),
        out_specs=[row_spec(s.shape) for s in shapes[:-1]] + [whole_spec((8, width))],
        out_shape=shapes,
        scratch_shapes=[
            pltpu.VMEM((width, 3 * width + 128), jnp.bfloat16),
            pltpu.SemaphoreType.DMA((BLOCKS,)),
        ],
        compiler_params=kernel_params(58),
        cost_estimate=pl.CostEstimate(
            flops=10**9, bytes_accessed=10**6, transcendentals=0
        ),
    )(me, tokens, segments, *pieces))


def split_blocks(source, me, block, keep_ref, send_ref):
    for place, bits in enumerate(PLACES):
        start = pl.multiple_of((me ^ bits) * block, 16)
        keep_ref[place] = source[pl.ds(start, block), :].astype(jnp.bfloat16)
        start = pl.multiple_of((me ^ bits ^ CORE) * block, 16)
        send_ref[place] = source[pl.ds(start, block), :].astype(jnp.bfloat16)


def split_shapes(block, columns):
    return [jax.ShapeDtypeStruct((4, block, columns), jnp.bfloat16)] * 2


def forward_kernel(
    plan, count, me_ref, x_ref, o_ref, cot_ref, vec_ref, *rest
):
    pieces = rest[:count]
    (
        y_ref, ht_ref, keep_ref, send_ref, rise_ref, act_ref, h_ref, w_ref, sems,
    ) = rest[count:]
    step = pl.program_id(0)
    width = y_ref.shape[1]
    chunk = act_ref.shape[1]
    hidden = w_ref.shape[1] - width

    @pl.when(step == 0)
    def _():
        for copy in load_pieces(pieces, plan, me_ref[0], width // BLOCKS, w_ref, sems):
            copy.wait()
        y_ref[...] = x_ref[...].astype(jnp.float32) + dot_nn(o_ref[...], w_ref[:, hidden:])
        normed, _ = norm_parts(y_ref[...])
        h_ref[...] = (normed * vec_ref[2:3] + vec_ref[3:4]).astype(jnp.bfloat16)
        ht_ref[...] = flip_axes(h_ref[...])

    span = pl.ds(pl.multiple_of(step * chunk, chunk), chunk)
    slope = (2.0 / 3.141592653589793) ** 0.5
    upper = dot_nn(h_ref[...], w_ref[:, span])
    square = upper * upper
    half = 0.5 + 0.5 * jnp.tanh(upper * (slope + (slope * 0.044715) * square))
    active = upper * half
    inner = (2.0 * slope) + (6.0 * 0.044715 * slope) * square
    rise_ref[...] = (half + active * (1.0 - half) * inner).astype(jnp.bfloat16)
    active = active.astype(jnp.bfloat16)
    act_ref[...] = active
    down_grad = dot_nn(flip_axes(active), cot_ref[...]).astype(jnp.bfloat16)
    block = keep_ref.shape[1]
    for odd in range(2):

        @pl.when((me_ref[0] & 1) == odd)
        def _():
            keep_ref[0] = down_grad[odd * block : (odd + 1) * block]
            send_ref[0] = down_grad[(1 - odd) * block : (2 - odd) * block]


def feed_forward(tokens, mixed, cotangent, vec, me, pieces, plan):
    count, width = cotangent.shape
    hidden = pieces[0].shape[2] - width
    chunk = hidden // 4
    shapes = (
        jax.ShapeDtypeStruct((count, width), jnp.float32),
        jax.ShapeDtypeStruct((width, count), jnp.bfloat16),
        *split_shapes(hidden // BLOCKS, width),
        jax.ShapeDtypeStruct((count, hidden), jnp.bfloat16),
        jax.ShapeDtypeStruct((count, hidden), jnp.bfloat16),
    )
    half_spec = pl.BlockSpec((1, hidden // BLOCKS, width), lambda j, me: (j ^ (me[0] // 2), 0, 0))
    return pl.pallas_call(
        functools.partial(forward_kernel, plan, len(pieces)),
        grid_spec=pltpu.PrefetchScalarGridSpec(
            num_scalar_prefetch=1,
            grid=(hidden // chunk,),
            in_specs=[whole_spec((count, width))] * 3
            + [whole_spec(vec.shape)]
            + any_specs(pieces),
            out_specs=[whole_spec(s.shape) for s in shapes[:2]]
            + [half_spec] * 2
            + [pl.BlockSpec((count, chunk), lambda j, me: (0, j))] * 2,
            scratch_shapes=[
                pltpu.VMEM((count, width), jnp.bfloat16),
                pltpu.VMEM((width, hidden + width), jnp.bfloat16),
                pltpu.SemaphoreType.DMA((BLOCKS,)),
            ],
        ),
        out_shape=shapes,
        compiler_params=kernel_params(60),
        cost_estimate=pl.CostEstimate(flops=10**9, bytes_accessed=10**6, transcendentals=0),
    )(me, tokens, mixed, cotangent, vec, *pieces)


def norm_back(back, normed, factor, gain):
    scaled = back * gain
    inner = scaled - jnp.mean(scaled, axis=-1, keepdims=True)
    inner = inner - normed * jnp.mean(scaled * normed, axis=-1, keepdims=True)
    gain_grad = jnp.sum(back * normed, axis=0, keepdims=True)
    return factor * inner, gain_grad, jnp.sum(back, axis=0, keepdims=True)


def return_kernel(
    plan, count, me_ref, y_ref, cot_ref, vec_ref, ht_ref, mixed_ref, rise_ref, act_ref, down_ref,
    *rest
):
    pieces = rest[:count]
    (
        grad_ref, out_ref, keep_ref, send_ref, sums_ref,
        acc_ref, du_ref, w_ref, part_ref, out_grad_ref, sems,
    ) = rest[count:]
    step = pl.program_id(0)
    width = y_ref.shape[1]
    chunk = act_ref.shape[1]
    block = width // BLOCKS
    copies = [
        pltpu.make_async_copy(*pair)
        for pair in piece_pairs(pieces, plan, me_ref[0], block, w_ref, sems)
    ]

    @pl.when(step == 0)
    def _():
        for copy in copies:
            copy.start()
        acc_ref[...] = y_ref[...]
        out_grad_ref[...] = jnp.zeros_like(out_grad_ref)
        sums_ref[...] = jnp.zeros_like(sums_ref)

    @pl.when(step < pl.num_programs(0) - 1)
    def _():
        start = pl.multiple_of(step * chunk, chunk)
        down = down_ref[...]
        grad_upper = (
            dot_nt(cot_ref[...], down) * rise_ref[...].astype(jnp.float32)
        ).astype(jnp.bfloat16)
        du_ref[:, pl.ds(start, chunk)] = grad_upper
        acc_ref[...] += dot_nn(act_ref[...], down)
        part_ref[...] = dot_nn(ht_ref[...], grad_upper)
        split_blocks(part_ref, me_ref[0], block, keep_ref, send_ref)

    @pl.when(step == pl.num_programs(0) - 1)
    def _():
        out_ref[...] = acc_ref[...].astype(jnp.bfloat16)
        for copy in copies:
            copy.wait()
        size = mixed_ref.shape[2]

        def body(place, carry):
            rows = pl.ds(pl.multiple_of(place * size, size), size)
            back = dot_nt(du_ref[rows, :], w_ref[...])
            normed, factor = norm_parts(y_ref[rows, :])
            through, gain_grad, bias_grad = norm_back(back, normed, factor, vec_ref[2:3])
            sums_ref[0:1] += gain_grad
            sums_ref[1:2] += bias_grad
            grad = cot_ref[rows, :].astype(jnp.float32) + through
            grad_ref[rows, :] = grad
            out_grad_ref[...] += dot_nn(mixed_ref[place], grad.astype(jnp.bfloat16))
            return carry

        lax.fori_loop(0, mixed_ref.shape[0], body, 0)
        split_blocks(out_grad_ref, me_ref[0], block, keep_ref, send_ref)


def feed_return(y_one, cotangent, vec, h_t, mixed, rise, active, w_down, me, pieces, plan):
    count, width = cotangent.shape
    hidden = active.shape[1]
    chunk = hidden // 4
    shapes = (
        jax.ShapeDtypeStruct((count, width), jnp.float32),
        jax.ShapeDtypeStruct((count, width), jnp.bfloat16),
        *split_shapes(width // BLOCKS, hidden + width),
        jax.ShapeDtypeStruct((8, width), jnp.float32),
    )
    return pl.pallas_call(
        functools.partial(return_kernel, plan, len(pieces)),
        grid=(hidden // chunk + 1,),
        in_specs=[pl.BlockSpec(memory_space=pltpu.SMEM)]
        + [whole_spec(v.shape) for v in (y_one, cotangent, vec, h_t, mixed)]
        + [
            pl.BlockSpec((count, chunk), lambda j: (0, jnp.minimum(j, 3))),
            pl.BlockSpec((count, chunk), lambda j: (0, jnp.minimum(j, 3))),
            pl.BlockSpec((chunk, width), lambda j: (jnp.minimum(j, 3), 0)),
        ]
        + any_specs(pieces),
        out_specs=[whole_spec(s.shape) for s in shapes[:2]]
        + [pl.BlockSpec((4, width // BLOCKS, width), lambda j: (0, 0, j))] * 2
        + [whole_spec((8, width))],
        out_shape=shapes,
        scratch_shapes=[
            pltpu.VMEM((count, width), jnp.float32),
            pltpu.VMEM((count, hidden), jnp.bfloat16),
            pltpu.VMEM((width, hidden), jnp.bfloat16),
            pltpu.VMEM((width, chunk), jnp.float32),
            pltpu.VMEM((width, width), jnp.float32),
            pltpu.SemaphoreType.DMA((BLOCKS,)),
        ],
        compiler_params=kernel_params(60),
        cost_estimate=pl.CostEstimate(
            flops=10**9, bytes_accessed=10**6, transcendentals=0
        ),
    )(me, y_one, cotangent, vec, h_t, mixed, rise, active, w_down, *pieces)


def heads_back(queries, keys, values, grads_t, mixed_t, expos, inverses, head_dim):
    length = queries.shape[0]
    lane = lax.broadcasted_iota(jnp.int32, (length, 128), 1)
    inside = lane < head_dim
    one_lane = jnp.where(lane < 2, 1.0, 0.0).astype(jnp.bfloat16)
    pad_rows = jnp.zeros((126, length), jnp.bfloat16)
    gap_rows = jnp.zeros((head_dim, length), jnp.bfloat16)
    keys_t = flip_axes(keys)
    value_wide = jnp.concatenate([values, one_lane], axis=1)
    grad_pair = grads_t.astype(jnp.float32)
    product = grad_pair * mixed_t.astype(jnp.float32)
    spans = [slice(half * head_dim, (half + 1) * head_dim) for half in range(2)]
    scaled = [
        (grad_pair[span] * inverse).astype(jnp.bfloat16)
        for span, inverse in zip(spans, inverses)
    ]
    scaled_pair = jnp.concatenate(scaled, axis=0)
    dv = []
    dk = []
    dq = []
    for half, span in enumerate(spans):
        delta = -jnp.sum(product[span], axis=0, keepdims=True) * inverses[half]
        high = delta.astype(jnp.bfloat16)
        low = (delta - high.astype(jnp.float32)).astype(jnp.bfloat16)
        first = [scaled[0], gap_rows] if half == 0 else [gap_rows, scaled[1]]
        grad_wide = jnp.concatenate(first + [high, low, pad_rows], axis=0)
        expo = expos[half]
        grad_scores = (expo.astype(jnp.float32) * dot_nn(value_wide, grad_wide)).astype(
            jnp.bfloat16
        )
        dv.append(dot_nt(expo, scaled_pair))
        dk.append(dot_nn(grad_scores, queries))
        dq.append(dot_nn(keys_t, grad_scores)[span] * (1.0 / head_dim**0.5))
    return (
        jnp.concatenate(dq, axis=0).T.astype(jnp.bfloat16),
        jnp.where(inside, dk[0], dk[1]).astype(jnp.bfloat16),
        jnp.where(inside, dv[0], dv[1]).astype(jnp.bfloat16),
    )


def backward_kernel(
    plans, counts, groups, first_group, me_ref, grad_ref, q_ref, k_ref, v_ref, expo_ref, inv_ref,
    mixed_ref, ht_ref, *rest
):
    out_pieces, rest = rest[: counts[0]], rest[counts[0] :]
    last = first_group > 0
    if last:
        x_ref, vec_ref, early_ref, ffn_sums_ref, *rest = rest
        qkv_pieces, rest = rest[: counts[1]], rest[counts[1] :]
        tokens_grad_ref, *rest = rest
    else:
        dqkv_ref, *rest = rest
    keep_ref, send_ref, dot_ref, acc_ref, wout_ref, out_sems, *rest = rest
    if last:
        w_ref, vec_acc, sems = rest
    row = pl.program_id(0)
    group = pl.program_id(1)
    length, width = grad_ref.shape[1:]
    head_dim = width // H
    block = width // BLOCKS
    wide = q_ref.shape[2]
    part = wide * groups
    me = me_ref[0]

    @pl.when((row == 0) & (group == 0))
    def _():
        copies = load_pieces(
            out_pieces, plans[0], me, block, wout_ref, out_sems, out_pieces[0].shape[2] - width
        )
        if last:
            copies += load_pieces(qkv_pieces, plans[1], me, block, w_ref, sems)
            vec_acc[...] = jnp.zeros_like(vec_acc)
            vec_acc[2:4] = ffn_sums_ref[0:2]
        acc_ref[...] = jnp.zeros_like(acc_ref)
        for copy in copies:
            copy.wait()

    @pl.when(group == 0)
    def _():
        attn_in = grad_ref[0].astype(jnp.bfloat16)
        weights = wout_ref[first_group * wide : first_group * wide + part, :]
        dot_ref[...] = dot_nt(weights, attn_in).astype(jnp.bfloat16)

    results = []
    for pair in range(wide // 128):
        cols = slice(pair * 128, pair * 128 + 128)
        start = pl.multiple_of(group * wide + pair * 128, 128)
        results.append(
            heads_back(
                q_ref[0, :, cols], k_ref[0, :, cols], v_ref[0, :, cols],
                dot_ref[pl.ds(start, 128), :], mixed_ref[0, cols, :],
                [expo_ref[0, 2 * pair + half] for half in range(2)],
                [inv_ref[0, 2 * pair + half] for half in range(2)],
                head_dim,
            )
        )
    joined = [jnp.concatenate(list(values), axis=1) for values in zip(*results)]
    for place, value in enumerate(joined):
        start = pl.multiple_of(place * part + group * wide, 128)
        acc_ref[:, pl.ds(start, wide)] += dot_nn(ht_ref[0], value)
        if not last:
            dqkv_ref[0, :, pl.ds(start, wide)] = value
    if last:
        before = first_group * wide
        back = None
        for place, value in enumerate(joined):
            old = early_ref[0, :, place * before : (place + 1) * before]
            start = place * width
            term = dot_nt(old, w_ref[:, start : start + before])
            term = term + dot_nt(value, w_ref[:, start + before : start + width])
            back = term if back is None else back + term
        normed, factor = norm_parts(x_ref[0].astype(jnp.float32))
        through, gain_grad, bias_grad = norm_back(back, normed, factor, vec_ref[0:1])
        vec_acc[0:1] += gain_grad
        vec_acc[1:2] += bias_grad
        tokens_grad_ref[0] = (grad_ref[0] + through).astype(jnp.bfloat16)

    @pl.when((row == pl.num_programs(0) - 1) & (group == groups - 1))
    def _():
        if last:
            acc_ref[:, 3 * part :] = vec_acc[...].T
        split_blocks(acc_ref, me, block, keep_ref, send_ref)


def backward(grad_y, saved, me, groups, first_group, out_group, extra=None):
    rows, length, width = grad_y.shape
    qkv, expo, inverse, mixed, h_t = saved
    wide = 256
    heads = wide * H // width
    part = wide * groups
    per = width // wide

    def column_spec(kind):
        return pl.BlockSpec(
            (1, length, wide), lambda r, g: (r, 0, kind * per + first_group + g)
        )

    out_pieces, plan_out = out_group
    inputs = [me, grad_y, qkv, qkv, qkv, expo, inverse, mixed, h_t, *out_pieces]
    in_specs = [
        pl.BlockSpec(memory_space=pltpu.SMEM),
        row_spec(grad_y.shape),
        column_spec(0),
        column_spec(1),
        column_spec(2),
        pl.BlockSpec((1, heads, length, length), lambda r, g: (r, first_group + g, 0, 0)),
        pl.BlockSpec((1, heads, 1, length), lambda r, g: (r, first_group + g, 0, 0)),
        pl.BlockSpec((1, wide, length), lambda r, g: (r, first_group + g, 0)),
        row_spec(h_t.shape),
    ] + any_specs(out_pieces)
    plans = [plan_out]
    counts = [len(out_pieces)]
    if extra is None:
        columns = 3 * part
        shapes = [jax.ShapeDtypeStruct((rows, length, 3 * part), jnp.bfloat16)]
    else:
        columns = 3 * part + 128
        tokens, vec, early, ffn_sums, (pieces, plan) = extra
        inputs += [tokens, vec, early, ffn_sums, *pieces]
        in_specs += [row_spec(tokens.shape), whole_spec(vec.shape)]
        in_specs += [row_spec(early.shape), whole_spec(ffn_sums.shape)] + any_specs(pieces)
        shapes = [jax.ShapeDtypeStruct(tokens.shape, jnp.bfloat16)]
        plans += [plan]
        counts += [len(pieces)]
    out_specs = [row_spec(shapes[0].shape)]
    shapes += split_shapes(width // BLOCKS, columns)
    out_specs += [whole_spec(s.shape) for s in shapes[1:]]
    scratch = [
        pltpu.VMEM((part, length), jnp.bfloat16),
        pltpu.VMEM((width, columns), jnp.float32),
        pltpu.VMEM((width, width), jnp.bfloat16),
        pltpu.SemaphoreType.DMA((BLOCKS,)),
    ]
    if extra is not None:
        scratch += [
            pltpu.VMEM((width, 3 * width), jnp.bfloat16),
            pltpu.VMEM((128, width), jnp.float32),
            pltpu.SemaphoreType.DMA((BLOCKS,)),
        ]
    return pl.pallas_call(
        functools.partial(backward_kernel, plans, counts, groups, first_group),
        grid=(rows, groups),
        in_specs=in_specs,
        out_specs=out_specs,
        out_shape=shapes,
        scratch_shapes=scratch,
        compiler_params=kernel_params(58),
        cost_estimate=pl.CostEstimate(flops=10**9, bytes_accessed=10**6, transcendentals=0),
    )(*inputs)


def layer(ranks, inner, tokens, segment_ids, cotangent, me, front, counts):
    rows, length, width = tokens.shape
    flat_shape = (rows * length, width)
    flat_cot = cotangent.reshape(flat_shape)
    first = front[0]
    near = direct(ranks, inner)
    *saved, o, vec = attend(tokens, segment_ids[:, :, None], me, *first)
    if near:
        _, sides, third, keep, other = front
        *values, o, other = together([*sides, *third, o, other])
        sides, third = values[:4], values[4:]
        third.append(swap_inner(third[0], inner - 1, inner))
        own_third = jnp.concatenate(by_bits(third, lax.axis_index("fsdp")), axis=0)
        w_down = lax.all_gather(own_third, "dp", axis=0, tiled=True)
        second = with_core(sides)
        keep, other = halve_tables(keep + other, NEAR_X)
        second = with_core(sides)
    else:
        second, w_down = front[1:]
    y_one, h_t, *down_parts, rise, active = feed_forward(
        tokens.reshape(flat_shape), o.reshape(flat_shape), flat_cot, vec, me, *second
    )
    if near:
        y_one, down_parts[1], other = together([y_one, down_parts[1], other])
        keep, other = halve_tables(keep + other, NEAR_Y)
        down_parts = scatter_core(*down_parts)
        y_one, *down_parts = together([y_one, *down_parts])
        down_received = scatter_sides(down_parts)
    grad_y, layer_output, *up_parts, ffn_sums = feed_return(
        y_one, flat_cot, vec, h_t, saved[3], rise, active, w_down, me, *second
    )
    groups = 2
    if near:
        *down_received, up_parts[1], grad_y, other = together(
            [*down_received, up_parts[1], grad_y, other]
        )
        counts = keep + other
        others = [swap_inner(counts, k, inner) for k in range(1, inner)]
        parts = scatter_core(*up_parts)
        down_mine = add(down_parts[0], *down_received)
        down_sum = lax.psum_scatter(down_mine, "fsdp", scatter_dimension=0, tiled=True)
        *parts, grad_y = together([*parts, grad_y])
        received = scatter_sides(parts)
    grad_y = grad_y.reshape(tokens.shape)
    dqkv, *early = backward(grad_y, saved, me, groups, 0, second)
    if near:
        received[0], received[1], dqkv, early[1], *others = together(
            [received[0], received[1], dqkv, early[1], *others]
        )
        counts = sum(others, counts)
        other = swap(counts, NEAR_Y)
        early_parts = scatter_core(*early)
        dqkv, *early_parts = together([dqkv, *early_parts])
        early_received = scatter_sides(early_parts)
    tokens_grad, *late = backward(
        grad_y, saved, me, 1, groups, second, (tokens, vec, dqkv, ffn_sums, first)
    )
    if near:
        *values, tokens_grad, late[1], down_sum, other = together(
            [*received, *early_received, tokens_grad, late[1], down_sum, other]
        )
        received, early_received = values[:3], values[3:]
        late_parts = scatter_core(*late)
        up_mine = add(parts[0], *received)
        up_sum = lax.psum_scatter(up_mine, "fsdp", scatter_dimension=0, tiled=True)
        early_mine = add(early_parts[0], *early_received)
        early_mine, *late_parts = together([early_mine, *late_parts])
        late_received = scatter_sides(late_parts)
        early_inner = scatter_inner(early_mine, inner)
        late_inner = scatter_inner(add(late_parts[0], *late_received), inner)
        for bit, following in ((NEAR_Y, NEAR_X), (NEAR_X, CORE), (CORE, None)):
            counts = double_tables(counts, other, bit)
            if following is not None:
                other = swap(counts, following)
        early_sum, late_sum = sum_parts(early_inner), sum_parts(late_inner)
        up_sum, down_sum = up_sum.astype(jnp.float32), down_sum.astype(jnp.float32)
    else:
        up_sum, down_sum, early_sum, late_sum = [
            scatter_whole(*v) for v in (up_parts, down_parts, early, late)
        ]
    part = width * groups // 3
    grads = []
    for place in range(3):
        grads.append(early_sum[:, place * part : (place + 1) * part])
        grads.append(late_sum[:, place * (width - part) : (place + 1) * (width - part)])
    hidden = active.shape[1]
    return (
        layer_output.reshape(tokens.shape),
        tokens_grad,
        jnp.concatenate(grads, axis=1),
        up_sum[:, hidden:],
        up_sum[:, :hidden],
        down_sum,
        late_sum[:, 3 * (width - part) :],
        counts,
    )


def per_device(
    ranks,
    inner,
    tokens,
    segment_ids,
    bucket_ids,
    cotangent,
    qkv_weight,
    out_weight,
    up_weight,
    down_weight,
    attn_gain,
    attn_bias,
    ffn_gain,
    ffn_bias,
):
    vectors = jnp.stack([attn_gain, attn_bias, ffn_gain, ffn_bias], axis=1)
    vectors = jnp.pad(vectors, ((0, 0), (0, 124)))
    ids = bucket_ids.reshape(-1, bucket_ids.shape[2]).T
    counts = count_buckets(ids)
    shards = (
        jnp.concatenate([qkv_weight, vectors], axis=1),
        jnp.concatenate([up_weight, out_weight], axis=1),
        down_weight,
    )
    if direct(ranks, inner):
        me = lax.axis_index("dp").reshape(1).astype(jnp.int32)
        front = gather_first(shards, inner, counts)
    else:
        me = jnp.zeros((1,), jnp.int32)
        front = [gather_whole(shard) for shard in shards[:2]]
        front.append(lax.all_gather(shards[2], BOTH, axis=0, tiled=True))
        counts = lax.psum(counts, BOTH)
    *results, vec_sums, counts = layer(
        ranks, inner, tokens, segment_ids, cotangent, me, front, counts
    )
    return (*results, *[vec_sums[:, place] for place in range(4)], counts)


def solution(mesh):
    placed = (
        P(("dp", "fsdp"), None, None),
        P(("dp", "fsdp"), None),
        P(("dp", "fsdp"), None, None),
        P(("dp", "fsdp"), None, None),
        P(("dp", "fsdp"), None),
        P(("dp", "fsdp"), None),
        P(("dp", "fsdp"), None),
        P(("dp", "fsdp"), None),
        P(("dp", "fsdp")),
        P(("dp", "fsdp")),
        P(("dp", "fsdp")),
        P(("dp", "fsdp")),
    )
    return jax.shard_map(
        functools.partial(per_device, mesh.shape["dp"], mesh.shape["fsdp"]),
        mesh=mesh,
        in_specs=placed,
        out_specs=(
            P(("dp", "fsdp"), None, None),
            P(("dp", "fsdp"), None, None),
            P(("dp", "fsdp"), None),
            P(("dp", "fsdp"), None),
            P(("dp", "fsdp"), None),
            P(("dp", "fsdp"), None),
            P(("dp", "fsdp")),
            P(("dp", "fsdp")),
            P(("dp", "fsdp")),
            P(("dp", "fsdp")),
            P(),
        ),
        check_vma=False,
    )
```

```python
import functools

import jax
import jax.numpy as jnp
from jax import lax
from jax.experimental import pallas as pl
from jax.experimental.pallas import tpu as pltpu
from jax.sharding import PartitionSpec as P

H = 12
BUCKETS = 16384
LOW = 256
BLOCKS = 8
CORE, NEAR_X, NEAR_Y = 1, 2, 4
PLACES = (0, NEAR_X, NEAR_Y, NEAR_X + NEAR_Y)
BOTH = ("dp", "fsdp")


def swap(value, bit):
    return lax.ppermute(value, "dp", [(i, i ^ bit) for i in range(BLOCKS)])


def swap_inner(value, bit, size):
    return lax.ppermute(value, "fsdp", [(i, i ^ bit) for i in range(size)])


def by_bits(parts, index):
    bit = 1
    while bit < len(parts):
        odd = (index & bit) != 0
        parts = [jnp.where(odd, parts[j ^ bit], parts[j]) for j in range(len(parts))]
        bit *= 2
    return parts


def direct(ranks, inner):
    return ranks == BLOCKS and inner & (inner - 1) == 0


def gather_whole(shard):
    near = lax.all_gather(shard, "fsdp", axis=0, tiled=True)
    whole = lax.all_gather(near, "dp", axis=0, tiled=True)
    whole = whole.reshape(4, 2, -1, whole.shape[1])
    return [whole[:, 0], whole[:, 1]], [0, CORE]


def gather_inner(shard, inner):
    parts = [shard] + [swap_inner(shard, k, inner) for k in range(1, inner)]
    return jnp.concatenate(by_bits(parts, lax.axis_index("fsdp")), axis=0)


def gather_sides(own):
    return [own] + [swap(own, bits) for bits in PLACES[1:]]


def with_core(pieces):
    joined = jnp.stack(pieces)
    return [joined, swap(joined, CORE)], [0, CORE]


def after(value, *others):
    return lax.optimization_barrier((value, *others))[0]


def together(values, *others):
    return list(lax.optimization_barrier((*values, *others)))[: len(values)]


def gather_first(shards, inner, counts):
    own = gather_inner(shards[0], inner)
    own, second = together([own, shards[1]])
    sides = gather_sides(own)
    parts = [second] + [swap_inner(second, k, inner) for k in range(1, inner)]
    values = together([*sides, *parts])
    sides, parts = values[:4], values[4:]
    keep, other = halve_tables(counts, CORE)
    own_second = jnp.concatenate(by_bits(parts, lax.axis_index("fsdp")), axis=0)
    first = with_core(sides)
    own_second, third, other = together([own_second, shards[2], other], *first[0])
    parts = [swap_inner(third, k, inner) for k in range(1, inner - 1)]
    return first, gather_sides(own_second), [third] + parts, keep, other


def halve_tables(counts, bit):
    tables = counts.shape[0] // 2
    upper = (lax.axis_index("dp") & bit) != 0
    keep = jnp.where(upper, counts[tables:], counts[:tables])
    send = jnp.where(upper, counts[:tables], counts[tables:])
    return keep, swap(send, bit)


def double_tables(counts, other, bit):
    upper = (lax.axis_index("dp") & bit) != 0
    return jnp.concatenate(
        [jnp.where(upper, other, counts), jnp.where(upper, counts, other)], axis=0
    )


def add(*terms):
    total = terms[0].astype(jnp.float32)
    for term in terms[1:]:
        total = total + term.astype(jnp.float32)
    return total.astype(jnp.bfloat16)


def scatter_core(keep, send):
    other = swap(send, CORE)
    return [add(keep[place], other[place]) for place in range(4)]


def scatter_sides(parts):
    return [swap(part, bits) for part, bits in zip(parts[1:], PLACES[1:])]


def scatter_corner(parts):
    half = parts[3].shape[0] // 2
    return [swap(parts[3][:half], NEAR_Y), swap(parts[3][half:], NEAR_X)]


def scatter_rest(parts, corners):
    half = parts[3].shape[0] // 2
    first, second = corners
    to_x = jnp.concatenate([add(parts[1][:half], first), parts[1][half:]], axis=0)
    to_y = jnp.concatenate([parts[2][:half], add(parts[2][half:], second)], axis=0)
    return [swap(to_x, NEAR_X), swap(to_y, NEAR_Y)]


def scatter_inner(mine, inner):
    part = mine.shape[0] // inner
    parts = [mine[j * part : (j + 1) * part] for j in range(inner)]
    parts = by_bits(parts, lax.axis_index("fsdp"))
    return parts[:1] + [swap_inner(parts[k], k, inner) for k in range(1, inner)]


def sum_parts(parts):
    total = parts[0].astype(jnp.float32)
    for part in parts[1:]:
        total = total + part.astype(jnp.float32)
    return total


def scatter_whole(keep, send):
    whole = jnp.stack([keep, send], axis=1).reshape(-1, keep.shape[2])
    near = lax.psum_scatter(whole, "dp", scatter_dimension=0, tiled=True)
    return lax.psum_scatter(near, "fsdp", scatter_dimension=0, tiled=True).astype(jnp.float32)


def piece_pairs(refs, plan, me, block, target, sems, column=0):
    pairs = []
    for ref, first in zip(refs, plan):
        for place, bits in enumerate(PLACES):
            start = pl.multiple_of((me ^ first ^ bits) * block, 16)
            pairs.append(
                (
                    ref.at[place, :, column : column + target.shape[1]],
                    target.at[pl.ds(start, block), :],
                    sems.at[len(pairs)],
                )
            )
    return pairs


def load_pieces(*details):
    copies = [pltpu.make_async_copy(*pair) for pair in piece_pairs(*details)]
    for copy in copies:
        copy.start()
    return copies


def count_kernel(ids_ref, counts_ref):
    _, high_count, low_count = counts_ref.shape
    tables, length = ids_ref.shape
    high_at = lax.broadcasted_iota(jnp.int32, (high_count, length), 0)
    low_at = lax.broadcasted_iota(jnp.int32, (low_count, length), 0)
    for table in range(tables):
        ids = ids_ref[table : table + 1, :]
        upper = lax.shift_right_logical(ids, 8)
        lower = jnp.bitwise_and(ids, low_count - 1)
        counts_ref[table] = dot_nt(
            jnp.where(high_at == upper, 1.0, 0.0).astype(jnp.bfloat16),
            jnp.where(low_at == lower, 1.0, 0.0).astype(jnp.bfloat16),
        ).astype(jnp.int32)


def count_buckets(ids):
    tables = ids.shape[0]
    counts = pl.pallas_call(
        count_kernel,
        out_shape=jax.ShapeDtypeStruct((tables, BUCKETS // LOW, LOW), jnp.int32),
        cost_estimate=pl.CostEstimate(flops=3 * 10**9, bytes_accessed=10**6, transcendentals=0),
    )(ids)
    return counts.reshape(tables, BUCKETS)


def norm_parts(values):
    centered = values - jnp.mean(values, axis=-1, keepdims=True)
    spread = jnp.mean(centered * centered, axis=-1, keepdims=True)
    factor = lax.rsqrt(spread + 1e-12)
    return centered * factor, factor


def dot_nn(first, second):
    return jnp.dot(first, second, preferred_element_type=jnp.float32)


def dot_nt(first, second):
    return lax.dot_general(
        first, second, (((1,), (1,)), ((), ())), preferred_element_type=jnp.float32
    )


def flip_axes(matrix):
    return matrix.T


def attend_kernel(plan, count, me_ref, x_ref, seg_ref, *rest):
    pieces = rest[:count]
    qkv_ref, expo_ref, inv_ref, mixed_ref, ht_ref, o_ref, vec_ref, w_ref, sems = rest[count:]
    length, width = x_ref.shape[1:]
    head_dim = width // H

    @pl.when(pl.program_id(0) == 0)
    def _():
        for copy in load_pieces(pieces, plan, me_ref[0], width // BLOCKS, w_ref, sems):
            copy.wait()
        vec_ref[...] = w_ref[:, 3 * width :].astype(jnp.float32).T[:8]

    normed, _ = norm_parts(x_ref[0].astype(jnp.float32))
    h_one = (normed * vec_ref[0:1] + vec_ref[1:2]).astype(jnp.bfloat16)
    ht_ref[0] = flip_axes(h_one)
    qkv = dot_nn(h_one, w_ref[:, : 3 * width]).astype(jnp.bfloat16)
    qkv_ref[0, :, :width] = qkv[:, :width] * (1.0 / head_dim**0.5)
    qkv_ref[0, :, width:] = qkv[:, width:]
    lane = lax.broadcasted_iota(jnp.int32, (length, 128), 1)
    seg = seg_ref[0]
    key_seg = jnp.where(seg == lane, 1.0, 0.0).astype(jnp.bfloat16)
    query_seg = jnp.where(seg == lane, 0.0, -1e30).astype(jnp.bfloat16)
    for pair in range(H // 2):
        cols = slice(pair * 128, pair * 128 + 128)
        queries = qkv_ref[0, :, cols]
        keys = qkv_ref[0, :, width + pair * 128 : width + pair * 128 + 128]
        values = qkv_ref[0, :, 2 * width + pair * 128 : 2 * width + pair * 128 + 128]
        key_wide = jnp.concatenate([keys, key_seg], axis=1)
        values_t = flip_axes(values)
        parts = []
        for half in range(2):
            inside = (lane < head_dim) if half == 0 else (lane >= head_dim)
            query_half = jnp.where(inside, queries, jnp.zeros_like(queries))
            scores = dot_nt(key_wide, jnp.concatenate([query_half, query_seg], axis=1))
            top = jnp.max(scores, axis=0, keepdims=True)
            expo = jnp.exp(scores - top)
            inverse = 1.0 / jnp.sum(expo, axis=0, keepdims=True)
            expo = expo.astype(jnp.bfloat16)
            expo_ref[0, 2 * pair + half] = expo
            inv_ref[0, 2 * pair + half] = inverse
            out = dot_nn(values_t, expo)
            parts.append(out[half * head_dim : (half + 1) * head_dim] * inverse)
        mixed = jnp.concatenate(parts, axis=0)
        mixed_ref[0, cols, :] = mixed.astype(jnp.bfloat16)
        o_ref[0, :, cols] = mixed.T.astype(jnp.bfloat16)


def whole_spec(shape):
    zeros = (0,) * len(shape)
    return pl.BlockSpec(shape, lambda *_: zeros, pipeline_mode=pl.Buffered(1))


def row_spec(shape):
    rest = (0,) * (len(shape) - 1)
    return pl.BlockSpec((1,) + shape[1:], lambda r, *_: (r,) + rest)


def any_specs(pieces):
    return [pl.BlockSpec(memory_space=pl.ANY) for _ in pieces]


def kernel_params(mebibytes):
    return pltpu.CompilerParams(vmem_limit_bytes=mebibytes * 1024 * 1024)


def attend(tokens, segments, me, pieces, plan):
    rows, length, width = tokens.shape
    shapes = (
        jax.ShapeDtypeStruct((rows, length, 3 * width), jnp.bfloat16),
        jax.ShapeDtypeStruct((rows, H, length, length), jnp.bfloat16),
        jax.ShapeDtypeStruct((rows, H, 1, length), jnp.float32),
        jax.ShapeDtypeStruct((rows, width, length), jnp.bfloat16),
        jax.ShapeDtypeStruct((rows, width, length), jnp.bfloat16),
        jax.ShapeDtypeStruct((rows, length, width), jnp.bfloat16),
        jax.ShapeDtypeStruct((8, width), jnp.float32),
    )
    return list(pl.pallas_call(
        functools.partial(attend_kernel, plan, len(pieces)),
        grid=(rows,),
        in_specs=[
            pl.BlockSpec(memory_space=pltpu.SMEM),
            row_spec(tokens.shape),
            row_spec(segments.shape),
        ]
        + any_specs(pieces),
        out_specs=[row_spec(s.shape) for s in shapes[:-1]] + [whole_spec((8, width))],
        out_shape=shapes,
        scratch_shapes=[
            pltpu.VMEM((width, 3 * width + 128), jnp.bfloat16),
            pltpu.SemaphoreType.DMA((BLOCKS,)),
        ],
        compiler_params=kernel_params(58),
        cost_estimate=pl.CostEstimate(
            flops=10**9, bytes_accessed=10**6, transcendentals=0
        ),
    )(me, tokens, segments, *pieces))


def split_blocks(source, me, block, keep_ref, send_ref):
    for place, bits in enumerate(PLACES):
        start = pl.multiple_of((me ^ bits) * block, 16)
        keep_ref[place] = source[pl.ds(start, block), :].astype(jnp.bfloat16)
        start = pl.multiple_of((me ^ bits ^ CORE) * block, 16)
        send_ref[place] = source[pl.ds(start, block), :].astype(jnp.bfloat16)


def split_shapes(block, columns):
    return [jax.ShapeDtypeStruct((4, block, columns), jnp.bfloat16)] * 2


def forward_kernel(
    plan, count, me_ref, x_ref, o_ref, cot_ref, vec_ref, *rest
):
    pieces = rest[:count]
    (
        y_ref, ht_ref, keep_ref, send_ref, rise_ref, act_ref, h_ref, w_ref, sems,
    ) = rest[count:]
    step = pl.program_id(0)
    width = y_ref.shape[1]
    chunk = act_ref.shape[1]
    hidden = w_ref.shape[1] - width

    @pl.when(step == 0)
    def _():
        for copy in load_pieces(pieces, plan, me_ref[0], width // BLOCKS, w_ref, sems):
            copy.wait()
        y_ref[...] = x_ref[...].astype(jnp.float32) + dot_nn(o_ref[...], w_ref[:, hidden:])
        normed, _ = norm_parts(y_ref[...])
        h_ref[...] = (normed * vec_ref[2:3] + vec_ref[3:4]).astype(jnp.bfloat16)
        ht_ref[...] = flip_axes(h_ref[...])

    span = pl.ds(pl.multiple_of(step * chunk, chunk), chunk)
    slope = (2.0 / 3.141592653589793) ** 0.5
    upper = dot_nn(h_ref[...], w_ref[:, span])
    square = upper * upper
    half = 0.5 + 0.5 * jnp.tanh(upper * (slope + (slope * 0.044715) * square))
    active = upper * half
    inner = (2.0 * slope) + (6.0 * 0.044715 * slope) * square
    rise_ref[...] = (half + active * (1.0 - half) * inner).astype(jnp.bfloat16)
    active = active.astype(jnp.bfloat16)
    act_ref[...] = active
    down_grad = dot_nn(flip_axes(active), cot_ref[...]).astype(jnp.bfloat16)
    block = keep_ref.shape[1]
    for odd in range(2):

        @pl.when((me_ref[0] & 1) == odd)
        def _():
            keep_ref[0] = down_grad[odd * block : (odd + 1) * block]
            send_ref[0] = down_grad[(1 - odd) * block : (2 - odd) * block]


def feed_forward(tokens, mixed, cotangent, vec, me, pieces, plan):
    count, width = cotangent.shape
    hidden = pieces[0].shape[2] - width
    chunk = hidden // 4
    shapes = (
        jax.ShapeDtypeStruct((count, width), jnp.float32),
        jax.ShapeDtypeStruct((width, count), jnp.bfloat16),
        *split_shapes(hidden // BLOCKS, width),
        jax.ShapeDtypeStruct((count, hidden), jnp.bfloat16),
        jax.ShapeDtypeStruct((count, hidden), jnp.bfloat16),
    )
    half_spec = pl.BlockSpec((1, hidden // BLOCKS, width), lambda j, me: (j ^ (me[0] // 2), 0, 0))
    return pl.pallas_call(
        functools.partial(forward_kernel, plan, len(pieces)),
        grid_spec=pltpu.PrefetchScalarGridSpec(
            num_scalar_prefetch=1,
            grid=(hidden // chunk,),
            in_specs=[whole_spec((count, width))] * 3
            + [whole_spec(vec.shape)]
            + any_specs(pieces),
            out_specs=[whole_spec(s.shape) for s in shapes[:2]]
            + [half_spec] * 2
            + [pl.BlockSpec((count, chunk), lambda j, me: (0, j))] * 2,
            scratch_shapes=[
                pltpu.VMEM((count, width), jnp.bfloat16),
                pltpu.VMEM((width, hidden + width), jnp.bfloat16),
                pltpu.SemaphoreType.DMA((BLOCKS,)),
            ],
        ),
        out_shape=shapes,
        compiler_params=kernel_params(60),
        cost_estimate=pl.CostEstimate(flops=10**9, bytes_accessed=10**6, transcendentals=0),
    )(me, tokens, mixed, cotangent, vec, *pieces)


def norm_back(back, normed, factor, gain):
    scaled = back * gain
    inner = scaled - jnp.mean(scaled, axis=-1, keepdims=True)
    inner = inner - normed * jnp.mean(scaled * normed, axis=-1, keepdims=True)
    gain_grad = jnp.sum(back * normed, axis=0, keepdims=True)
    return factor * inner, gain_grad, jnp.sum(back, axis=0, keepdims=True)


def return_kernel(
    plan, count, plan_down, count_down, me_ref, y_ref, cot_ref, vec_ref, ht_ref, mixed_ref,
    rise_ref, act_ref, *rest
):
    pieces = rest[:count]
    down_pieces = rest[count : count + count_down]
    (
        grad_ref, out_ref, keep_ref, send_ref, sums_ref,
        acc_ref, du_ref, w_ref, wd_ref, part_ref, out_grad_ref, sems, down_sems,
    ) = rest[count + count_down :]
    step = pl.program_id(0)
    width = y_ref.shape[1]
    chunk = act_ref.shape[1]
    block = width // BLOCKS
    copies = [
        pltpu.make_async_copy(*pair)
        for pair in piece_pairs(pieces, plan, me_ref[0], block, w_ref, sems)
    ]

    @pl.when(step == 0)
    def _():
        down_copies = load_pieces(
            down_pieces, plan_down, me_ref[0], wd_ref.shape[0] // BLOCKS, wd_ref, down_sems
        )
        for copy in copies:
            copy.start()
        acc_ref[...] = y_ref[...]
        out_grad_ref[...] = jnp.zeros_like(out_grad_ref)
        sums_ref[...] = jnp.zeros_like(sums_ref)
        for copy in down_copies:
            copy.wait()

    @pl.when(step < pl.num_programs(0) - 1)
    def _():
        start = pl.multiple_of(step * chunk, chunk)
        down = wd_ref[pl.ds(start, chunk), :]
        grad_upper = (
            dot_nt(cot_ref[...], down) * rise_ref[...].astype(jnp.float32)
        ).astype(jnp.bfloat16)
        du_ref[:, pl.ds(start, chunk)] = grad_upper
        acc_ref[...] += dot_nn(act_ref[...], down)
        part_ref[...] = dot_nn(ht_ref[...], grad_upper)
        split_blocks(part_ref, me_ref[0], block, keep_ref, send_ref)

    @pl.when(step == pl.num_programs(0) - 1)
    def _():
        out_ref[...] = acc_ref[...].astype(jnp.bfloat16)
        for copy in copies:
            copy.wait()
        size = mixed_ref.shape[2]

        def body(place, carry):
            rows = pl.ds(pl.multiple_of(place * size, size), size)
            back = dot_nt(du_ref[rows, :], w_ref[...])
            normed, factor = norm_parts(y_ref[rows, :])
            through, gain_grad, bias_grad = norm_back(back, normed, factor, vec_ref[2:3])
            sums_ref[0:1] += gain_grad
            sums_ref[1:2] += bias_grad
            grad = cot_ref[rows, :].astype(jnp.float32) + through
            grad_ref[rows, :] = grad
            out_grad_ref[...] += dot_nn(mixed_ref[place], grad.astype(jnp.bfloat16))
            return carry

        lax.fori_loop(0, mixed_ref.shape[0], body, 0)
        split_blocks(out_grad_ref, me_ref[0], block, keep_ref, send_ref)


def feed_return(y_one, cotangent, vec, h_t, mixed, rise, active, me, pieces, plan, down_pieces, plan_down):
    count, width = cotangent.shape
    hidden = active.shape[1]
    chunk = hidden // 4
    shapes = (
        jax.ShapeDtypeStruct((count, width), jnp.float32),
        jax.ShapeDtypeStruct((count, width), jnp.bfloat16),
        *split_shapes(width // BLOCKS, hidden + width),
        jax.ShapeDtypeStruct((8, width), jnp.float32),
    )
    return pl.pallas_call(
        functools.partial(
            return_kernel, plan, len(pieces), plan_down, len(down_pieces)
        ),
        grid=(hidden // chunk + 1,),
        in_specs=[pl.BlockSpec(memory_space=pltpu.SMEM)]
        + [whole_spec(v.shape) for v in (y_one, cotangent, vec, h_t, mixed)]
        + [
            pl.BlockSpec((count, chunk), lambda j: (0, jnp.minimum(j, 3))),
            pl.BlockSpec((count, chunk), lambda j: (0, jnp.minimum(j, 3))),
        ]
        + any_specs(pieces)
        + any_specs(down_pieces),
        out_specs=[whole_spec(s.shape) for s in shapes[:2]]
        + [pl.BlockSpec((4, width // BLOCKS, width), lambda j: (0, 0, j))] * 2
        + [whole_spec((8, width))],
        out_shape=shapes,
        scratch_shapes=[
            pltpu.VMEM((count, width), jnp.float32),
            pltpu.VMEM((count, hidden), jnp.bfloat16),
            pltpu.VMEM((width, hidden), jnp.bfloat16),
            pltpu.VMEM((hidden, width), jnp.bfloat16),
            pltpu.VMEM((width, chunk), jnp.float32),
            pltpu.VMEM((width, width), jnp.float32),
            pltpu.SemaphoreType.DMA((BLOCKS,)),
            pltpu.SemaphoreType.DMA((BLOCKS,)),
        ],
        compiler_params=kernel_params(60),
        cost_estimate=pl.CostEstimate(
            flops=10**9, bytes_accessed=10**6, transcendentals=0
        ),
    )(me, y_one, cotangent, vec, h_t, mixed, rise, active, *pieces, *down_pieces)


def heads_back(queries, keys, values, grads_t, mixed_t, expos, inverses, head_dim):
    length = queries.shape[0]
    lane = lax.broadcasted_iota(jnp.int32, (length, 128), 1)
    inside = lane < head_dim
    one_lane = jnp.where(lane < 2, 1.0, 0.0).astype(jnp.bfloat16)
    pad_rows = jnp.zeros((126, length), jnp.bfloat16)
    gap_rows = jnp.zeros((head_dim, length), jnp.bfloat16)
    keys_t = flip_axes(keys)
    value_wide = jnp.concatenate([values, one_lane], axis=1)
    grad_pair = grads_t.astype(jnp.float32)
    product = grad_pair * mixed_t.astype(jnp.float32)
    spans = [slice(half * head_dim, (half + 1) * head_dim) for half in range(2)]
    scaled = [
        (grad_pair[span] * inverse).astype(jnp.bfloat16)
        for span, inverse in zip(spans, inverses)
    ]
    scaled_pair = jnp.concatenate(scaled, axis=0)
    dv = []
    dk = []
    dq = []
    for half, span in enumerate(spans):
        delta = -jnp.sum(product[span], axis=0, keepdims=True) * inverses[half]
        high = delta.astype(jnp.bfloat16)
        low = (delta - high.astype(jnp.float32)).astype(jnp.bfloat16)
        first = [scaled[0], gap_rows] if half == 0 else [gap_rows, scaled[1]]
        grad_wide = jnp.concatenate(first + [high, low, pad_rows], axis=0)
        expo = expos[half]
        grad_scores = (expo.astype(jnp.float32) * dot_nn(value_wide, grad_wide)).astype(
            jnp.bfloat16
        )
        dv.append(dot_nt(expo, scaled_pair))
        dk.append(dot_nn(grad_scores, queries))
        dq.append(dot_nn(keys_t, grad_scores)[span] * (1.0 / head_dim**0.5))
    return (
        jnp.concatenate(dq, axis=0).T.astype(jnp.bfloat16),
        jnp.where(inside, dk[0], dk[1]).astype(jnp.bfloat16),
        jnp.where(inside, dv[0], dv[1]).astype(jnp.bfloat16),
    )


def backward_kernel(
    plans, counts, groups, first_group, me_ref, grad_ref, q_ref, k_ref, v_ref, expo_ref, inv_ref,
    mixed_ref, ht_ref, *rest
):
    out_pieces, rest = rest[: counts[0]], rest[counts[0] :]
    last = first_group > 0
    if last:
        x_ref, vec_ref, early_ref, ffn_sums_ref, *rest = rest
        qkv_pieces, rest = rest[: counts[1]], rest[counts[1] :]
        tokens_grad_ref, *rest = rest
    else:
        dqkv_ref, *rest = rest
    keep_ref, send_ref, dot_ref, acc_ref, wout_ref, out_sems, *rest = rest
    if last:
        w_ref, vec_acc, sems = rest
    row = pl.program_id(0)
    group = pl.program_id(1)
    length, width = grad_ref.shape[1:]
    head_dim = width // H
    block = width // BLOCKS
    wide = q_ref.shape[2]
    part = wide * groups
    me = me_ref[0]

    @pl.when((row == 0) & (group == 0))
    def _():
        copies = load_pieces(
            out_pieces, plans[0], me, block, wout_ref, out_sems, out_pieces[0].shape[2] - width
        )
        if last:
            copies += load_pieces(qkv_pieces, plans[1], me, block, w_ref, sems)
            vec_acc[...] = jnp.zeros_like(vec_acc)
            vec_acc[2:4] = ffn_sums_ref[0:2]
        acc_ref[...] = jnp.zeros_like(acc_ref)
        for copy in copies:
            copy.wait()

    @pl.when(group == 0)
    def _():
        attn_in = grad_ref[0].astype(jnp.bfloat16)
        weights = wout_ref[first_group * wide : first_group * wide + part, :]
        dot_ref[...] = dot_nt(weights, attn_in).astype(jnp.bfloat16)

    results = []
    for pair in range(wide // 128):
        cols = slice(pair * 128, pair * 128 + 128)
        start = pl.multiple_of(group * wide + pair * 128, 128)
        results.append(
            heads_back(
                q_ref[0, :, cols], k_ref[0, :, cols], v_ref[0, :, cols],
                dot_ref[pl.ds(start, 128), :], mixed_ref[0, cols, :],
                [expo_ref[0, 2 * pair + half] for half in range(2)],
                [inv_ref[0, 2 * pair + half] for half in range(2)],
                head_dim,
            )
        )
    joined = [jnp.concatenate(list(values), axis=1) for values in zip(*results)]
    for place, value in enumerate(joined):
        start = pl.multiple_of(place * part + group * wide, 128)
        acc_ref[:, pl.ds(start, wide)] += dot_nn(ht_ref[0], value)
        if not last:
            dqkv_ref[0, :, pl.ds(start, wide)] = value
    if last:
        before = first_group * wide
        back = None
        for place, value in enumerate(joined):
            old = early_ref[0, :, place * before : (place + 1) * before]
            start = place * width
            term = dot_nt(old, w_ref[:, start : start + before])
            term = term + dot_nt(value, w_ref[:, start + before : start + width])
            back = term if back is None else back + term
        normed, factor = norm_parts(x_ref[0].astype(jnp.float32))
        through, gain_grad, bias_grad = norm_back(back, normed, factor, vec_ref[0:1])
        vec_acc[0:1] += gain_grad
        vec_acc[1:2] += bias_grad
        tokens_grad_ref[0] = (grad_ref[0] + through).astype(jnp.bfloat16)

    @pl.when((row == pl.num_programs(0) - 1) & (group == groups - 1))
    def _():
        if last:
            acc_ref[:, 3 * part :] = vec_acc[...].T
        split_blocks(acc_ref, me, block, keep_ref, send_ref)


def backward(grad_y, saved, me, groups, first_group, out_group, extra=None):
    rows, length, width = grad_y.shape
    qkv, expo, inverse, mixed, h_t = saved
    wide = 256
    heads = wide * H // width
    part = wide * groups
    per = width // wide

    def column_spec(kind):
        return pl.BlockSpec(
            (1, length, wide), lambda r, g: (r, 0, kind * per + first_group + g)
        )

    out_pieces, plan_out = out_group
    inputs = [me, grad_y, qkv, qkv, qkv, expo, inverse, mixed, h_t, *out_pieces]
    in_specs = [
        pl.BlockSpec(memory_space=pltpu.SMEM),
        row_spec(grad_y.shape),
        column_spec(0),
        column_spec(1),
        column_spec(2),
        pl.BlockSpec((1, heads, length, length), lambda r, g: (r, first_group + g, 0, 0)),
        pl.BlockSpec((1, heads, 1, length), lambda r, g: (r, first_group + g, 0, 0)),
        pl.BlockSpec((1, wide, length), lambda r, g: (r, first_group + g, 0)),
        row_spec(h_t.shape),
    ] + any_specs(out_pieces)
    plans = [plan_out]
    counts = [len(out_pieces)]
    if extra is None:
        columns = 3 * part
        shapes = [jax.ShapeDtypeStruct((rows, length, 3 * part), jnp.bfloat16)]
    else:
        columns = 3 * part + 128
        tokens, vec, early, ffn_sums, (pieces, plan) = extra
        inputs += [tokens, vec, early, ffn_sums, *pieces]
        in_specs += [row_spec(tokens.shape), whole_spec(vec.shape)]
        in_specs += [row_spec(early.shape), whole_spec(ffn_sums.shape)] + any_specs(pieces)
        shapes = [jax.ShapeDtypeStruct(tokens.shape, jnp.bfloat16)]
        plans += [plan]
        counts += [len(pieces)]
    out_specs = [row_spec(shapes[0].shape)]
    shapes += split_shapes(width // BLOCKS, columns)
    out_specs += [whole_spec(s.shape) for s in shapes[1:]]
    scratch = [
        pltpu.VMEM((part, length), jnp.bfloat16),
        pltpu.VMEM((width, columns), jnp.float32),
        pltpu.VMEM((width, width), jnp.bfloat16),
        pltpu.SemaphoreType.DMA((BLOCKS,)),
    ]
    if extra is not None:
        scratch += [
            pltpu.VMEM((width, 3 * width), jnp.bfloat16),
            pltpu.VMEM((128, width), jnp.float32),
            pltpu.SemaphoreType.DMA((BLOCKS,)),
        ]
    return pl.pallas_call(
        functools.partial(backward_kernel, plans, counts, groups, first_group),
        grid=(rows, groups),
        in_specs=in_specs,
        out_specs=out_specs,
        out_shape=shapes,
        scratch_shapes=scratch,
        compiler_params=kernel_params(58),
        cost_estimate=pl.CostEstimate(flops=10**9, bytes_accessed=10**6, transcendentals=0),
    )(*inputs)


def layer(ranks, inner, tokens, segment_ids, cotangent, me, front, counts):
    rows, length, width = tokens.shape
    flat_shape = (rows * length, width)
    flat_cot = cotangent.reshape(flat_shape)
    first = front[0]
    near = direct(ranks, inner)
    *saved, o, vec = attend(tokens, segment_ids[:, :, None], me, *first)
    if near:
        _, sides, parts, keep, other = front
        *values, o, other = together([*sides, *parts, o, other])
        sides, parts = values[:4], values[4:]
        parts.append(swap_inner(parts[0], inner - 1, inner))
        own_third = jnp.concatenate(by_bits(parts, lax.axis_index("fsdp")), axis=0)
        second = with_core(sides)
        keep, other = halve_tables(keep + other, NEAR_X)
        own_third, second[0][1] = together([own_third, second[0][1]])
        sides = gather_sides(own_third)
    else:
        second, third = front[1:]
    y_one, h_t, *down_parts, rise, active = feed_forward(
        tokens.reshape(flat_shape), o.reshape(flat_shape), flat_cot, vec, me, *second
    )
    if near:
        *sides, y_one, down_parts[1], other = together([*sides, y_one, down_parts[1], other])
        keep, other = halve_tables(keep + other, NEAR_Y)
        third = with_core(sides)
        down_parts = scatter_core(*down_parts)
        y_one, *down_parts = together([y_one, *down_parts])
        down_received = scatter_sides(down_parts)
    grad_y, layer_output, *up_parts, ffn_sums = feed_return(
        y_one, flat_cot, vec, h_t, saved[3], rise, active, me, *second, *third
    )
    groups = 2
    if near:
        *down_received, up_parts[1], grad_y, other = together(
            [*down_received, up_parts[1], grad_y, other]
        )
        counts = keep + other
        others = [swap_inner(counts, k, inner) for k in range(1, inner)]
        parts = scatter_core(*up_parts)
        down_mine = add(down_parts[0], *down_received)
        *values, grad_y = together([*parts, *others, grad_y])
        parts, others = values[:4], values[4:]
        received = scatter_sides(parts)
        down_inner = scatter_inner(down_mine, inner)
    grad_y = grad_y.reshape(tokens.shape)
    dqkv, *early = backward(grad_y, saved, me, groups, 0, second)
    if near:
        received[0], received[1], dqkv, early[1], *down_inner = together(
            [received[0], received[1], dqkv, early[1], *down_inner]
        )
        counts = sum(others, counts)
        other = swap(counts, NEAR_Y)
        early_parts = scatter_core(*early)
        dqkv, *early_parts = together([dqkv, *early_parts])
        early_received = scatter_sides(early_parts)
    tokens_grad, *late = backward(
        grad_y, saved, me, 1, groups, second, (tokens, vec, dqkv, ffn_sums, first)
    )
    if near:
        *values, tokens_grad, late[1], other = together(
            [*received, *early_received, tokens_grad, late[1], other]
        )
        received, early_received = values[:3], values[3:]
        late_parts = scatter_core(*late)
        up_mine = add(parts[0], *received)
        early_mine = add(early_parts[0], *early_received)
        joined = jnp.concatenate([up_mine, early_mine], axis=1)
        late_received = scatter_sides(late_parts)
        *joined, late_mine = together(
            [*scatter_inner(joined, inner), add(late_parts[0], *late_received)]
        )
        joined_sum = sum_parts(joined)
        up_sum, early_sum = joined_sum[:, : up_mine.shape[1]], joined_sum[:, up_mine.shape[1] :]
        down_sum = sum_parts(down_inner)
        late_sum = sum_parts(scatter_inner(late_mine, inner))
        for bit, following in ((NEAR_Y, NEAR_X), (NEAR_X, CORE), (CORE, None)):
            counts = double_tables(counts, other, bit)
            if following is not None:
                other = swap(counts, following)
    else:
        up_sum, down_sum, early_sum, late_sum = [
            scatter_whole(*v) for v in (up_parts, down_parts, early, late)
        ]
    part = width * groups // 3
    grads = []
    for place in range(3):
        grads.append(early_sum[:, place * part : (place + 1) * part])
        grads.append(late_sum[:, place * (width - part) : (place + 1) * (width - part)])
    hidden = active.shape[1]
    return (
        layer_output.reshape(tokens.shape),
        tokens_grad,
        jnp.concatenate(grads, axis=1),
        up_sum[:, hidden:],
        up_sum[:, :hidden],
        down_sum,
        late_sum[:, 3 * (width - part) :],
        counts,
    )


def per_device(
    ranks,
    inner,
    tokens,
    segment_ids,
    bucket_ids,
    cotangent,
    qkv_weight,
    out_weight,
    up_weight,
    down_weight,
    attn_gain,
    attn_bias,
    ffn_gain,
    ffn_bias,
):
    vectors = jnp.stack([attn_gain, attn_bias, ffn_gain, ffn_bias], axis=1)
    vectors = jnp.pad(vectors, ((0, 0), (0, 124)))
    ids = bucket_ids.reshape(-1, bucket_ids.shape[2]).T
    counts = count_buckets(ids)
    shards = (
        jnp.concatenate([qkv_weight, vectors], axis=1),
        jnp.concatenate([up_weight, out_weight], axis=1),
        down_weight,
    )
    if direct(ranks, inner):
        me = lax.axis_index("dp").reshape(1).astype(jnp.int32)
        front = gather_first(shards, inner, counts)
    else:
        me = jnp.zeros((1,), jnp.int32)
        front = [gather_whole(shard) for shard in shards]
        counts = lax.psum(counts, BOTH)
    *results, vec_sums, counts = layer(
        ranks, inner, tokens, segment_ids, cotangent, me, front, counts
    )
    return (*results, *[vec_sums[:, place] for place in range(4)], counts)


def solution(mesh):
    placed = (
        P(("dp", "fsdp"), None, None),
        P(("dp", "fsdp"), None),
        P(("dp", "fsdp"), None, None),
        P(("dp", "fsdp"), None, None),
        P(("dp", "fsdp"), None),
        P(("dp", "fsdp"), None),
        P(("dp", "fsdp"), None),
        P(("dp", "fsdp"), None),
        P(("dp", "fsdp")),
        P(("dp", "fsdp")),
        P(("dp", "fsdp")),
        P(("dp", "fsdp")),
    )
    return jax.shard_map(
        functools.partial(per_device, mesh.shape["dp"], mesh.shape["fsdp"]),
        mesh=mesh,
        in_specs=placed,
        out_specs=(
            P(("dp", "fsdp"), None, None),
            P(("dp", "fsdp"), None, None),
            P(("dp", "fsdp"), None),
            P(("dp", "fsdp"), None),
            P(("dp", "fsdp"), None),
            P(("dp", "fsdp"), None),
            P(("dp", "fsdp")),
            P(("dp", "fsdp")),
            P(("dp", "fsdp")),
            P(("dp", "fsdp")),
            P(),
        ),
        check_vma=False,
    )
```

```python
import functools

import jax
import jax.numpy as jnp
from jax import lax
from jax.experimental import pallas as pl
from jax.experimental.pallas import tpu as pltpu
from jax.sharding import PartitionSpec as P

H = 12
BUCKETS = 16384
LOW = 256
BLOCKS = 8
CORE, NEAR_X, NEAR_Y = 1, 2, 4
PLACES = (0, NEAR_X, NEAR_Y, NEAR_X + NEAR_Y)
BOTH = ("dp", "fsdp")


def swap(value, bit):
    return lax.ppermute(value, "dp", [(i, i ^ bit) for i in range(BLOCKS)])


def swap_inner(value, bit, size):
    return lax.ppermute(value, "fsdp", [(i, i ^ bit) for i in range(size)])


def by_bits(parts, index):
    bit = 1
    while bit < len(parts):
        odd = (index & bit) != 0
        parts = [jnp.where(odd, parts[j ^ bit], parts[j]) for j in range(len(parts))]
        bit *= 2
    return parts


def direct(ranks, inner):
    return ranks == BLOCKS and inner & (inner - 1) == 0


def gather_whole(shard):
    near = lax.all_gather(shard, "fsdp", axis=0, tiled=True)
    whole = lax.all_gather(near, "dp", axis=0, tiled=True)
    whole = whole.reshape(4, 2, -1, whole.shape[1])
    return [whole[:, 0], whole[:, 1]], [0, CORE]


def gather_inner(shard, inner):
    parts = [shard] + [swap_inner(shard, k, inner) for k in range(1, inner)]
    return jnp.concatenate(by_bits(parts, lax.axis_index("fsdp")), axis=0)


def gather_sides(own):
    return [own] + [swap(own, bits) for bits in PLACES[1:]]


def with_core(pieces):
    joined = jnp.stack(pieces)
    return [joined, swap(joined, CORE)], [0, CORE]


def after(value, *others):
    return lax.optimization_barrier((value, *others))[0]


def together(values, *others):
    return list(lax.optimization_barrier((*values, *others)))[: len(values)]


def gather_first(shards, inner, counts, segments):
    own = gather_inner(shards[0], inner)
    own, second, counts, segments = together([own, shards[1], counts, segments])
    sides = gather_sides(own)
    parts = [second] + [swap_inner(second, k, inner) for k in range(1, inner)]
    values = together([*sides, *parts])
    sides, parts = values[:4], values[4:]
    keep, other = halve_tables(counts, CORE)
    own_second = jnp.concatenate(by_bits(parts, lax.axis_index("fsdp")), axis=0)
    first = with_core(sides)
    own_second, third, other = together([own_second, shards[2], other], *first[0])
    parts = [swap_inner(third, k, inner) for k in range(1, inner - 1)]
    return first, gather_sides(own_second), [third] + parts, keep, other, segments


def halve_tables(counts, bit):
    tables = counts.shape[0] // 2
    upper = (lax.axis_index("dp") & bit) != 0
    keep = jnp.where(upper, counts[tables:], counts[:tables])
    send = jnp.where(upper, counts[:tables], counts[tables:])
    return keep, swap(send, bit)


def double_tables(counts, other, bit):
    upper = (lax.axis_index("dp") & bit) != 0
    return jnp.concatenate(
        [jnp.where(upper, other, counts), jnp.where(upper, counts, other)], axis=0
    )


def add(*terms):
    total = terms[0].astype(jnp.float32)
    for term in terms[1:]:
        total = total + term.astype(jnp.float32)
    return total.astype(jnp.bfloat16)


def scatter_core(keep, send):
    other = swap(send, CORE)
    return [add(keep[place], other[place]) for place in range(4)]


def scatter_sides(parts):
    return [swap(part, bits) for part, bits in zip(parts[1:], PLACES[1:])]


def scatter_corner(parts):
    half = parts[3].shape[0] // 2
    return [swap(parts[3][:half], NEAR_Y), swap(parts[3][half:], NEAR_X)]


def scatter_rest(parts, corners):
    half = parts[3].shape[0] // 2
    first, second = corners
    to_x = jnp.concatenate([add(parts[1][:half], first), parts[1][half:]], axis=0)
    to_y = jnp.concatenate([parts[2][:half], add(parts[2][half:], second)], axis=0)
    return [swap(to_x, NEAR_X), swap(to_y, NEAR_Y)]


def scatter_inner(mine, inner):
    part = mine.shape[0] // inner
    parts = [mine[j * part : (j + 1) * part] for j in range(inner)]
    parts = by_bits(parts, lax.axis_index("fsdp"))
    return parts[:1] + [swap_inner(parts[k], k, inner) for k in range(1, inner)]


def sum_parts(parts):
    total = parts[0].astype(jnp.float32)
    for part in parts[1:]:
        total = total + part.astype(jnp.float32)
    return total


def scatter_whole(keep, send):
    whole = jnp.stack([keep, send], axis=1).reshape(-1, keep.shape[2])
    near = lax.psum_scatter(whole, "dp", scatter_dimension=0, tiled=True)
    return lax.psum_scatter(near, "fsdp", scatter_dimension=0, tiled=True).astype(jnp.float32)


def piece_pairs(refs, plan, me, block, target, sems, column=0):
    pairs = []
    for ref, first in zip(refs, plan):
        for place, bits in enumerate(PLACES):
            start = pl.multiple_of((me ^ first ^ bits) * block, 16)
            pairs.append(
                (
                    ref.at[place, :, column : column + target.shape[1]],
                    target.at[pl.ds(start, block), :],
                    sems.at[len(pairs)],
                )
            )
    return pairs


def load_pieces(*details):
    copies = [pltpu.make_async_copy(*pair) for pair in piece_pairs(*details)]
    for copy in copies:
        copy.start()
    return copies


def count_kernel(ids_ref, counts_ref):
    _, high_count, low_count = counts_ref.shape
    tables, length = ids_ref.shape
    high_at = lax.broadcasted_iota(jnp.int32, (high_count, length), 0)
    low_at = lax.broadcasted_iota(jnp.int32, (low_count, length), 0)
    for table in range(tables):
        ids = ids_ref[table : table + 1, :]
        upper = lax.shift_right_logical(ids, 8)
        lower = jnp.bitwise_and(ids, low_count - 1)
        counts_ref[table] = dot_nt(
            jnp.where(high_at == upper, 1.0, 0.0).astype(jnp.bfloat16),
            jnp.where(low_at == lower, 1.0, 0.0).astype(jnp.bfloat16),
        ).astype(jnp.int32)


def count_buckets(ids):
    tables = ids.shape[0]
    counts = pl.pallas_call(
        count_kernel,
        out_shape=jax.ShapeDtypeStruct((tables, BUCKETS // LOW, LOW), jnp.int32),
        cost_estimate=pl.CostEstimate(flops=3 * 10**9, bytes_accessed=10**6, transcendentals=0),
    )(ids)
    return counts.reshape(tables, BUCKETS)


def norm_parts(values):
    centered = values - jnp.mean(values, axis=-1, keepdims=True)
    spread = jnp.mean(centered * centered, axis=-1, keepdims=True)
    factor = lax.rsqrt(spread + 1e-12)
    return centered * factor, factor


def dot_nn(first, second):
    return jnp.dot(first, second, preferred_element_type=jnp.float32)


def dot_nt(first, second):
    return lax.dot_general(
        first, second, (((1,), (1,)), ((), ())), preferred_element_type=jnp.float32
    )


def flip_axes(matrix):
    return matrix.T


def attend_kernel(plan, count, me_ref, x_ref, seg_ref, *rest):
    pieces = rest[:count]
    qkv_ref, expo_ref, inv_ref, mixed_ref, ht_ref, o_ref, vec_ref, w_ref, sems = rest[count:]
    length, width = x_ref.shape[1:]
    head_dim = width // H

    @pl.when(pl.program_id(0) == 0)
    def _():
        for copy in load_pieces(pieces, plan, me_ref[0], width // BLOCKS, w_ref, sems):
            copy.wait()
        vec_ref[...] = w_ref[:, 3 * width :].astype(jnp.float32).T[:8]

    normed, _ = norm_parts(x_ref[0].astype(jnp.float32))
    h_one = (normed * vec_ref[0:1] + vec_ref[1:2]).astype(jnp.bfloat16)
    ht_ref[0] = flip_axes(h_one)
    qkv = dot_nn(h_one, w_ref[:, : 3 * width]).astype(jnp.bfloat16)
    qkv_ref[0, :, :width] = qkv[:, :width] * (1.0 / head_dim**0.5)
    qkv_ref[0, :, width:] = qkv[:, width:]
    lane = lax.broadcasted_iota(jnp.int32, (length, 128), 1)
    seg = seg_ref[0]
    key_seg = jnp.where(seg == lane, 1.0, 0.0).astype(jnp.bfloat16)
    query_seg = jnp.where(seg == lane, 0.0, -1e30).astype(jnp.bfloat16)
    for pair in range(H // 2):
        cols = slice(pair * 128, pair * 128 + 128)
        queries = qkv_ref[0, :, cols]
        keys = qkv_ref[0, :, width + pair * 128 : width + pair * 128 + 128]
        values = qkv_ref[0, :, 2 * width + pair * 128 : 2 * width + pair * 128 + 128]
        key_wide = jnp.concatenate([keys, key_seg], axis=1)
        values_t = flip_axes(values)
        parts = []
        for half in range(2):
            inside = (lane < head_dim) if half == 0 else (lane >= head_dim)
            query_half = jnp.where(inside, queries, jnp.zeros_like(queries))
            scores = dot_nt(key_wide, jnp.concatenate([query_half, query_seg], axis=1))
            top = jnp.max(scores, axis=0, keepdims=True)
            expo = jnp.exp(scores - top)
            inverse = 1.0 / jnp.sum(expo, axis=0, keepdims=True)
            expo = expo.astype(jnp.bfloat16)
            expo_ref[0, 2 * pair + half] = expo
            inv_ref[0, 2 * pair + half] = inverse
            out = dot_nn(values_t, expo)
            parts.append(out[half * head_dim : (half + 1) * head_dim] * inverse)
        mixed = jnp.concatenate(parts, axis=0)
        mixed_ref[0, cols, :] = mixed.astype(jnp.bfloat16)
        o_ref[0, :, cols] = mixed.T.astype(jnp.bfloat16)


def whole_spec(shape):
    zeros = (0,) * len(shape)
    return pl.BlockSpec(shape, lambda *_: zeros, pipeline_mode=pl.Buffered(1))


def row_spec(shape):
    rest = (0,) * (len(shape) - 1)
    return pl.BlockSpec((1,) + shape[1:], lambda r, *_: (r,) + rest)


def any_specs(pieces):
    return [pl.BlockSpec(memory_space=pl.ANY) for _ in pieces]


def kernel_params(mebibytes):
    return pltpu.CompilerParams(vmem_limit_bytes=mebibytes * 1024 * 1024)


def attend(tokens, segments, me, pieces, plan):
    rows, length, width = tokens.shape
    shapes = (
        jax.ShapeDtypeStruct((rows, length, 3 * width), jnp.bfloat16),
        jax.ShapeDtypeStruct((rows, H, length, length), jnp.bfloat16),
        jax.ShapeDtypeStruct((rows, H, 1, length), jnp.float32),
        jax.ShapeDtypeStruct((rows, width, length), jnp.bfloat16),
        jax.ShapeDtypeStruct((rows, width, length), jnp.bfloat16),
        jax.ShapeDtypeStruct((rows, length, width), jnp.bfloat16),
        jax.ShapeDtypeStruct((8, width), jnp.float32),
    )
    return list(pl.pallas_call(
        functools.partial(attend_kernel, plan, len(pieces)),
        grid=(rows,),
        in_specs=[
            pl.BlockSpec(memory_space=pltpu.SMEM),
            row_spec(tokens.shape),
            row_spec(segments.shape),
        ]
        + any_specs(pieces),
        out_specs=[row_spec(s.shape) for s in shapes[:-1]] + [whole_spec((8, width))],
        out_shape=shapes,
        scratch_shapes=[
            pltpu.VMEM((width, 3 * width + 128), jnp.bfloat16),
            pltpu.SemaphoreType.DMA((BLOCKS,)),
        ],
        compiler_params=kernel_params(58),
        cost_estimate=pl.CostEstimate(
            flops=10**9, bytes_accessed=10**6, transcendentals=0
        ),
    )(me, tokens, segments, *pieces))


def split_blocks(source, me, block, keep_ref, send_ref):
    for place, bits in enumerate(PLACES):
        start = pl.multiple_of((me ^ bits) * block, 16)
        keep_ref[place] = source[pl.ds(start, block), :].astype(jnp.bfloat16)
        start = pl.multiple_of((me ^ bits ^ CORE) * block, 16)
        send_ref[place] = source[pl.ds(start, block), :].astype(jnp.bfloat16)


def split_shapes(block, columns):
    return [jax.ShapeDtypeStruct((4, block, columns), jnp.bfloat16)] * 2


def forward_kernel(
    plan, count, me_ref, x_ref, o_ref, cot_ref, vec_ref, *rest
):
    pieces = rest[:count]
    (
        y_ref, ht_ref, keep_ref, send_ref, rise_ref, act_ref, h_ref, w_ref, sems,
    ) = rest[count:]
    step = pl.program_id(0)
    width = y_ref.shape[1]
    chunk = act_ref.shape[1]
    hidden = w_ref.shape[1] - width

    @pl.when(step == 0)
    def _():
        for copy in load_pieces(pieces, plan, me_ref[0], width // BLOCKS, w_ref, sems):
            copy.wait()
        y_ref[...] = x_ref[...].astype(jnp.float32) + dot_nn(o_ref[...], w_ref[:, hidden:])
        normed, _ = norm_parts(y_ref[...])
        h_ref[...] = (normed * vec_ref[2:3] + vec_ref[3:4]).astype(jnp.bfloat16)
        ht_ref[...] = flip_axes(h_ref[...])

    span = pl.ds(pl.multiple_of(step * chunk, chunk), chunk)
    slope = (2.0 / 3.141592653589793) ** 0.5
    upper = dot_nn(h_ref[...], w_ref[:, span])
    square = upper * upper
    half = 0.5 + 0.5 * jnp.tanh(upper * (slope + (slope * 0.044715) * square))
    active = upper * half
    inner = (2.0 * slope) + (6.0 * 0.044715 * slope) * square
    rise_ref[...] = (half + active * (1.0 - half) * inner).astype(jnp.bfloat16)
    active = active.astype(jnp.bfloat16)
    act_ref[...] = active
    down_grad = dot_nn(flip_axes(active), cot_ref[...]).astype(jnp.bfloat16)
    block = keep_ref.shape[1]
    for odd in range(2):

        @pl.when((me_ref[0] & 1) == odd)
        def _():
            keep_ref[0] = down_grad[odd * block : (odd + 1) * block]
            send_ref[0] = down_grad[(1 - odd) * block : (2 - odd) * block]


def feed_forward(tokens, mixed, cotangent, vec, me, pieces, plan):
    count, width = cotangent.shape
    hidden = pieces[0].shape[2] - width
    chunk = hidden // 4
    shapes = (
        jax.ShapeDtypeStruct((count, width), jnp.float32),
        jax.ShapeDtypeStruct((width, count), jnp.bfloat16),
        *split_shapes(hidden // BLOCKS, width),
        jax.ShapeDtypeStruct((count, hidden), jnp.bfloat16),
        jax.ShapeDtypeStruct((count, hidden), jnp.bfloat16),
    )
    half_spec = pl.BlockSpec((1, hidden // BLOCKS, width), lambda j, me: (j ^ (me[0] // 2), 0, 0))
    return pl.pallas_call(
        functools.partial(forward_kernel, plan, len(pieces)),
        grid_spec=pltpu.PrefetchScalarGridSpec(
            num_scalar_prefetch=1,
            grid=(hidden // chunk,),
            in_specs=[whole_spec((count, width))] * 3
            + [whole_spec(vec.shape)]
            + any_specs(pieces),
            out_specs=[whole_spec(s.shape) for s in shapes[:2]]
            + [half_spec] * 2
            + [pl.BlockSpec((count, chunk), lambda j, me: (0, j))] * 2,
            scratch_shapes=[
                pltpu.VMEM((count, width), jnp.bfloat16),
                pltpu.VMEM((width, hidden + width), jnp.bfloat16),
                pltpu.SemaphoreType.DMA((BLOCKS,)),
            ],
        ),
        out_shape=shapes,
        compiler_params=kernel_params(60),
        cost_estimate=pl.CostEstimate(flops=10**9, bytes_accessed=10**6, transcendentals=0),
    )(me, tokens, mixed, cotangent, vec, *pieces)


def norm_back(back, normed, factor, gain):
    scaled = back * gain
    inner = scaled - jnp.mean(scaled, axis=-1, keepdims=True)
    inner = inner - normed * jnp.mean(scaled * normed, axis=-1, keepdims=True)
    gain_grad = jnp.sum(back * normed, axis=0, keepdims=True)
    return factor * inner, gain_grad, jnp.sum(back, axis=0, keepdims=True)


def return_kernel(
    plan, count, plan_down, count_down, me_ref, y_ref, cot_ref, vec_ref, ht_ref, mixed_ref,
    rise_ref, act_ref, *rest
):
    pieces = rest[:count]
    down_pieces = rest[count : count + count_down]
    (
        grad_ref, out_ref, keep_ref, send_ref, sums_ref,
        acc_ref, du_ref, w_ref, wd_ref, part_ref, out_grad_ref, sems, down_sems,
    ) = rest[count + count_down :]
    step = pl.program_id(0)
    width = y_ref.shape[1]
    chunk = act_ref.shape[1]
    block = width // BLOCKS
    copies = [
        pltpu.make_async_copy(*pair)
        for pair in piece_pairs(pieces, plan, me_ref[0], block, w_ref, sems)
    ]

    @pl.when(step == 0)
    def _():
        down_copies = load_pieces(
            down_pieces, plan_down, me_ref[0], wd_ref.shape[0] // BLOCKS, wd_ref, down_sems
        )
        for copy in copies:
            copy.start()
        acc_ref[...] = y_ref[...]
        out_grad_ref[...] = jnp.zeros_like(out_grad_ref)
        sums_ref[...] = jnp.zeros_like(sums_ref)
        for copy in down_copies:
            copy.wait()

    @pl.when(step < pl.num_programs(0) - 1)
    def _():
        start = pl.multiple_of(step * chunk, chunk)
        down = wd_ref[pl.ds(start, chunk), :]
        grad_upper = (
            dot_nt(cot_ref[...], down) * rise_ref[...].astype(jnp.float32)
        ).astype(jnp.bfloat16)
        du_ref[:, pl.ds(start, chunk)] = grad_upper
        acc_ref[...] += dot_nn(act_ref[...], down)
        part_ref[...] = dot_nn(ht_ref[...], grad_upper)
        split_blocks(part_ref, me_ref[0], block, keep_ref, send_ref)

    @pl.when(step == pl.num_programs(0) - 1)
    def _():
        out_ref[...] = acc_ref[...].astype(jnp.bfloat16)
        for copy in copies:
            copy.wait()
        size = mixed_ref.shape[2]

        def body(place, carry):
            rows = pl.ds(pl.multiple_of(place * size, size), size)
            back = dot_nt(du_ref[rows, :], w_ref[...])
            normed, factor = norm_parts(y_ref[rows, :])
            through, gain_grad, bias_grad = norm_back(back, normed, factor, vec_ref[2:3])
            sums_ref[0:1] += gain_grad
            sums_ref[1:2] += bias_grad
            grad = cot_ref[rows, :].astype(jnp.float32) + through
            grad_ref[rows, :] = grad
            out_grad_ref[...] += dot_nn(mixed_ref[place], grad.astype(jnp.bfloat16))
            return carry

        lax.fori_loop(0, mixed_ref.shape[0], body, 0)
        split_blocks(out_grad_ref, me_ref[0], block, keep_ref, send_ref)


def feed_return(y_one, cotangent, vec, h_t, mixed, rise, active, me, pieces, plan, down_pieces, plan_down):
    count, width = cotangent.shape
    hidden = active.shape[1]
    chunk = hidden // 4
    shapes = (
        jax.ShapeDtypeStruct((count, width), jnp.float32),
        jax.ShapeDtypeStruct((count, width), jnp.bfloat16),
        *split_shapes(width // BLOCKS, hidden + width),
        jax.ShapeDtypeStruct((8, width), jnp.float32),
    )
    return pl.pallas_call(
        functools.partial(
            return_kernel, plan, len(pieces), plan_down, len(down_pieces)
        ),
        grid=(hidden // chunk + 1,),
        in_specs=[pl.BlockSpec(memory_space=pltpu.SMEM)]
        + [whole_spec(v.shape) for v in (y_one, cotangent, vec, h_t, mixed)]
        + [
            pl.BlockSpec((count, chunk), lambda j: (0, jnp.minimum(j, 3))),
            pl.BlockSpec((count, chunk), lambda j: (0, jnp.minimum(j, 3))),
        ]
        + any_specs(pieces)
        + any_specs(down_pieces),
        out_specs=[whole_spec(s.shape) for s in shapes[:2]]
        + [pl.BlockSpec((4, width // BLOCKS, width), lambda j: (0, 0, j))] * 2
        + [whole_spec((8, width))],
        out_shape=shapes,
        scratch_shapes=[
            pltpu.VMEM((count, width), jnp.float32),
            pltpu.VMEM((count, hidden), jnp.bfloat16),
            pltpu.VMEM((width, hidden), jnp.bfloat16),
            pltpu.VMEM((hidden, width), jnp.bfloat16),
            pltpu.VMEM((width, chunk), jnp.float32),
            pltpu.VMEM((width, width), jnp.float32),
            pltpu.SemaphoreType.DMA((BLOCKS,)),
            pltpu.SemaphoreType.DMA((BLOCKS,)),
        ],
        compiler_params=kernel_params(60),
        cost_estimate=pl.CostEstimate(
            flops=10**9, bytes_accessed=10**6, transcendentals=0
        ),
    )(me, y_one, cotangent, vec, h_t, mixed, rise, active, *pieces, *down_pieces)


def heads_back(queries, keys, values, grads_t, mixed_t, expos, inverses, head_dim):
    length = queries.shape[0]
    lane = lax.broadcasted_iota(jnp.int32, (length, 128), 1)
    inside = lane < head_dim
    one_lane = jnp.where(lane < 2, 1.0, 0.0).astype(jnp.bfloat16)
    pad_rows = jnp.zeros((126, length), jnp.bfloat16)
    gap_rows = jnp.zeros((head_dim, length), jnp.bfloat16)
    keys_t = flip_axes(keys)
    value_wide = jnp.concatenate([values, one_lane], axis=1)
    grad_pair = grads_t.astype(jnp.float32)
    product = grad_pair * mixed_t.astype(jnp.float32)
    spans = [slice(half * head_dim, (half + 1) * head_dim) for half in range(2)]
    scaled = [
        (grad_pair[span] * inverse).astype(jnp.bfloat16)
        for span, inverse in zip(spans, inverses)
    ]
    scaled_pair = jnp.concatenate(scaled, axis=0)
    dv = []
    dk = []
    dq = []
    for half, span in enumerate(spans):
        delta = -jnp.sum(product[span], axis=0, keepdims=True) * inverses[half]
        high = delta.astype(jnp.bfloat16)
        low = (delta - high.astype(jnp.float32)).astype(jnp.bfloat16)
        first = [scaled[0], gap_rows] if half == 0 else [gap_rows, scaled[1]]
        grad_wide = jnp.concatenate(first + [high, low, pad_rows], axis=0)
        expo = expos[half]
        grad_scores = (expo.astype(jnp.float32) * dot_nn(value_wide, grad_wide)).astype(
            jnp.bfloat16
        )
        dv.append(dot_nt(expo, scaled_pair))
        dk.append(dot_nn(grad_scores, queries))
        dq.append(dot_nn(keys_t, grad_scores)[span] * (1.0 / head_dim**0.5))
    return (
        jnp.concatenate(dq, axis=0).T.astype(jnp.bfloat16),
        jnp.where(inside, dk[0], dk[1]).astype(jnp.bfloat16),
        jnp.where(inside, dv[0], dv[1]).astype(jnp.bfloat16),
    )


def backward_kernel(
    plan, count, groups, me_ref, grad_ref, q_ref, k_ref, v_ref, expo_ref, inv_ref, mixed_ref, ht_ref,
    *rest
):
    pieces = rest[:count]
    dqkv_ref, keep_ref, send_ref, dot_ref, acc_ref, wout_ref, sems = rest[count:]
    row = pl.program_id(0)
    group = pl.program_id(1)
    length, width = grad_ref.shape[1:]
    head_dim = width // H
    block = width // BLOCKS
    wide = q_ref.shape[2]
    me = me_ref[0]

    @pl.when((row == 0) & (group == 0))
    def _():
        copies = load_pieces(
            pieces, plan, me, block, wout_ref, sems, pieces[0].shape[2] - width
        )
        acc_ref[...] = jnp.zeros_like(acc_ref)
        for copy in copies:
            copy.wait()

    @pl.when(group == 0)
    def _():
        attn_in = grad_ref[0].astype(jnp.bfloat16)
        dot_ref[...] = dot_nt(wout_ref[...], attn_in).astype(jnp.bfloat16)

    results = []
    for pair in range(wide // 128):
        cols = slice(pair * 128, pair * 128 + 128)
        start = pl.multiple_of(group * wide + pair * 128, 128)
        results.append(
            heads_back(
                q_ref[0, :, cols], k_ref[0, :, cols], v_ref[0, :, cols],
                dot_ref[pl.ds(start, 128), :], mixed_ref[0, cols, :],
                [expo_ref[0, 2 * pair + half] for half in range(2)],
                [inv_ref[0, 2 * pair + half] for half in range(2)],
                head_dim,
            )
        )
    joined = [jnp.concatenate(list(values), axis=1) for values in zip(*results)]
    for place, value in enumerate(joined):
        start = pl.multiple_of(place * width + group * wide, 128)
        acc_ref[:, pl.ds(start, wide)] += dot_nn(ht_ref[0], value)
        dqkv_ref[0, :, pl.ds(start, wide)] = value

    @pl.when((row == pl.num_programs(0) - 1) & (group == groups - 1))
    def _():
        split_blocks(acc_ref, me, block, keep_ref, send_ref)


def backward(grad_y, saved, me, pieces, plan):
    rows, length, width = grad_y.shape
    qkv, expo, inverse, mixed, h_t = saved
    wide = 256
    heads = wide * H // width
    groups = width // wide

    def column_spec(kind):
        return pl.BlockSpec((1, length, wide), lambda r, g: (r, 0, kind * groups + g))

    inputs = [me, grad_y, qkv, qkv, qkv, expo, inverse, mixed, h_t, *pieces]
    in_specs = [
        pl.BlockSpec(memory_space=pltpu.SMEM),
        row_spec(grad_y.shape),
        column_spec(0),
        column_spec(1),
        column_spec(2),
        pl.BlockSpec((1, heads, length, length), lambda r, g: (r, g, 0, 0)),
        pl.BlockSpec((1, heads, 1, length), lambda r, g: (r, g, 0, 0)),
        pl.BlockSpec((1, wide, length), lambda r, g: (r, g, 0)),
        row_spec(h_t.shape),
    ] + any_specs(pieces)
    shapes = [jax.ShapeDtypeStruct((rows, length, 3 * width), jnp.bfloat16)]
    shapes += split_shapes(width // BLOCKS, 3 * width)
    return pl.pallas_call(
        functools.partial(backward_kernel, plan, len(pieces), groups),
        grid=(rows, groups),
        in_specs=in_specs,
        out_specs=[row_spec(shapes[0].shape)] + [whole_spec(s.shape) for s in shapes[1:]],
        out_shape=shapes,
        scratch_shapes=[
            pltpu.VMEM((width, length), jnp.bfloat16),
            pltpu.VMEM((width, 3 * width), jnp.float32),
            pltpu.VMEM((width, width), jnp.bfloat16),
            pltpu.SemaphoreType.DMA((BLOCKS,)),
        ],
        compiler_params=kernel_params(58),
        cost_estimate=pl.CostEstimate(flops=10**9, bytes_accessed=10**6, transcendentals=0),
    )(*inputs)


def finish_kernel(
    plan, count, me_ref, grad_ref, x_ref, dqkv_ref, vec_ref, ffn_sums_ref, *rest
):
    pieces = rest[:count]
    tokens_grad_ref, keep_ref, send_ref, w_ref, vec_acc, sems = rest[count:]
    row = pl.program_id(0)
    block = w_ref.shape[0] // BLOCKS
    normed, factor = norm_parts(x_ref[0].astype(jnp.float32))

    @pl.when(row == 0)
    def _():
        copies = load_pieces(pieces, plan, me_ref[0], block, w_ref, sems)
        vec_acc[...] = jnp.zeros_like(vec_acc)
        vec_acc[2:4] = ffn_sums_ref[0:2]
        for copy in copies:
            copy.wait()

    back = dot_nt(dqkv_ref[0], w_ref[...])
    through, gain_grad, bias_grad = norm_back(back, normed, factor, vec_ref[0:1])
    vec_acc[0:1] += gain_grad
    vec_acc[1:2] += bias_grad
    tokens_grad_ref[0] = (grad_ref[0] + through).astype(jnp.bfloat16)

    @pl.when(row == pl.num_programs(0) - 1)
    def _():
        vec_t = vec_acc[...].T
        vec_acc[...] = jnp.zeros_like(vec_acc)
        w_ref[:, :128] = vec_t.astype(jnp.bfloat16)
        for place, bits in enumerate(PLACES):
            start = pl.multiple_of((me_ref[0] ^ bits) * block, 16)
            keep_ref[place] = w_ref[pl.ds(start, block), :128]
            start = pl.multiple_of((me_ref[0] ^ bits ^ CORE) * block, 16)
            send_ref[place] = w_ref[pl.ds(start, block), :128]


def finish(grad_y, tokens, dqkv, vec, ffn_sums, me, pieces, plan):
    rows, length, width = tokens.shape
    shapes = [jax.ShapeDtypeStruct(tokens.shape, jnp.bfloat16)]
    shapes += split_shapes(width // BLOCKS, 128)
    return pl.pallas_call(
        functools.partial(finish_kernel, plan, len(pieces)),
        grid=(rows,),
        in_specs=[pl.BlockSpec(memory_space=pltpu.SMEM)]
        + [row_spec(v.shape) for v in (grad_y, tokens, dqkv)]
        + [whole_spec(vec.shape), whole_spec(ffn_sums.shape)]
        + any_specs(pieces),
        out_specs=[row_spec(tokens.shape)] + [whole_spec(s.shape) for s in shapes[1:]],
        out_shape=shapes,
        scratch_shapes=[
            pltpu.VMEM((width, 3 * width), jnp.bfloat16),
            pltpu.VMEM((128, width), jnp.float32),
            pltpu.SemaphoreType.DMA((BLOCKS,)),
        ],
        compiler_params=kernel_params(58),
        cost_estimate=pl.CostEstimate(flops=10**9, bytes_accessed=10**6, transcendentals=0),
    )(me, grad_y, tokens, dqkv, vec, ffn_sums, *pieces)


def layer(ranks, inner, tokens, segments, cotangent, me, front, counts):
    rows, length, width = tokens.shape
    flat_shape = (rows * length, width)
    flat_cot = cotangent.reshape(flat_shape)
    first = front[0]
    near = direct(ranks, inner)
    *saved, o, vec = attend(tokens, segments, me, *first)
    if near:
        _, sides, parts, keep, other = front
        *values, o, other = together([*sides, *parts, o, other])
        sides, parts = values[:4], values[4:]
        parts.append(swap_inner(parts[0], inner - 1, inner))
        own_third = jnp.concatenate(by_bits(parts, lax.axis_index("fsdp")), axis=0)
        second = with_core(sides)
        keep, other = halve_tables(keep + other, NEAR_X)
        own_third, second[0][1] = together([own_third, second[0][1]])
        sides = gather_sides(own_third)
    else:
        second, third = front[1:]
    y_one, h_t, *down_parts, rise, active = feed_forward(
        tokens.reshape(flat_shape), o.reshape(flat_shape), flat_cot, vec, me, *second
    )
    if near:
        *sides, y_one, down_parts[1], other = together([*sides, y_one, down_parts[1], other])
        keep, other = halve_tables(keep + other, NEAR_Y)
        third = with_core(sides)
        down_parts = scatter_core(*down_parts)
        y_one, *down_parts = together([y_one, *down_parts])
        down_received = scatter_sides(down_parts)
    grad_y, layer_output, *up_parts, ffn_sums = feed_return(
        y_one, flat_cot, vec, h_t, saved[3], rise, active, me, *second, *third
    )
    if near:
        *down_received, up_parts[1], grad_y, other = together(
            [*down_received, up_parts[1], grad_y, other]
        )
        counts = keep + other
        others = [swap_inner(counts, k, inner) for k in range(1, inner)]
        parts = scatter_core(*up_parts)
        down_mine = add(down_parts[0], *down_received)
        *values, grad_y, down_mine = together([*parts, *others, grad_y, down_mine])
        parts, others = values[:4], values[4:]
        counts = sum(others, counts)
        received = scatter_sides(parts)
        size = down_mine.shape[0] // inner
        pieces = [down_mine[k * size : (k + 1) * size] for k in range(inner)]
        pieces = by_bits(pieces, lax.axis_index("fsdp"))
        down_inner = [swap_inner(pieces[k], k, inner) for k in range(1, inner - 1)]
    grad_y = grad_y.reshape(tokens.shape)
    dqkv, *early = backward(grad_y, saved, me, *second)
    if near:
        *values, dqkv, early[1], piece, counts = together(
            [*received, *down_inner, dqkv, early[1], pieces[-1], counts]
        )
        received, down_inner = values[:3], values[3:]
        other = swap(counts, NEAR_Y)
        down_inner.append(swap_inner(piece, inner - 1, inner))
        early_parts = scatter_core(*early)
        up_mine = add(parts[0], *received)
        size = up_mine.shape[0] // inner
        up_pieces = [up_mine[k * size : (k + 1) * size] for k in range(inner)]
        up_pieces = by_bits(up_pieces, lax.axis_index("fsdp"))
        *values, dqkv, other = together([*early_parts, *down_inner, *up_pieces, dqkv, other])
        early_parts, down_inner = values[:4], values[4 : 3 + inner]
        up_pieces = values[3 + inner :]
        counts = double_tables(counts, other, NEAR_Y)
        down_sum = sum_parts(pieces[:1] + down_inner)
        early_received = scatter_sides(early_parts)
        up_inner = [swap_inner(up_pieces[k], k, inner) for k in range(1, inner - 1)]
    tokens_grad, *late = finish(grad_y, tokens, dqkv, vec, ffn_sums, me, *first)
    if near:
        *values, tokens_grad, late[1], piece, counts = together(
            [*early_received, *up_inner, tokens_grad, late[1], up_pieces[-1], counts]
        )
        early_received, up_inner = values[:3], values[3:]
        late_parts = scatter_core(*late)
        other = swap(counts, NEAR_X)
        *late_parts, other = together([*late_parts, other])
        counts = double_tables(counts, other, NEAR_X)
        other = swap(counts, CORE)
        up_inner.append(swap_inner(piece, inner - 1, inner))
        early_mine = add(early_parts[0], *early_received)
        early_sum = sum_parts(scatter_inner(early_mine, inner))
        late_received = scatter_sides(late_parts)
        up_sum = sum_parts(up_pieces[:1] + up_inner)
        late_mine, other = together([add(late_parts[0], *late_received), other])
        late_sum = sum_parts(scatter_inner(late_mine, inner))
        counts = double_tables(counts, other, CORE)
    else:
        up_sum, down_sum, early_sum, late_sum = [
            scatter_whole(*v) for v in (up_parts, down_parts, early, late)
        ]
    hidden = active.shape[1]
    return (
        layer_output.reshape(tokens.shape),
        tokens_grad,
        early_sum,
        up_sum[:, hidden:],
        up_sum[:, :hidden],
        down_sum,
        late_sum,
        counts,
    )


def per_device(
    ranks,
    inner,
    tokens,
    segment_ids,
    bucket_ids,
    cotangent,
    qkv_weight,
    out_weight,
    up_weight,
    down_weight,
    attn_gain,
    attn_bias,
    ffn_gain,
    ffn_bias,
):
    vectors = jnp.stack([attn_gain, attn_bias, ffn_gain, ffn_bias], axis=1)
    vectors = jnp.pad(vectors, ((0, 0), (0, 124)))
    ids = bucket_ids.reshape(-1, bucket_ids.shape[2]).T
    counts = count_buckets(ids)
    segments = segment_ids[:, :, None]
    shards = (
        jnp.concatenate([qkv_weight, vectors], axis=1),
        jnp.concatenate([up_weight, out_weight], axis=1),
        down_weight,
    )
    if direct(ranks, inner):
        me = lax.axis_index("dp").reshape(1).astype(jnp.int32)
        *front, segments = gather_first(shards, inner, counts, segments)
    else:
        me = jnp.zeros((1,), jnp.int32)
        front = [gather_whole(shard) for shard in shards]
        counts = lax.psum(counts, BOTH)
    *results, vec_sums, counts = layer(
        ranks, inner, tokens, segments, cotangent, me, front, counts
    )
    return (*results, *[vec_sums[:, place] for place in range(4)], counts)


def solution(mesh):
    placed = (
        P(("dp", "fsdp"), None, None),
        P(("dp", "fsdp"), None),
        P(("dp", "fsdp"), None, None),
        P(("dp", "fsdp"), None, None),
        P(("dp", "fsdp"), None),
        P(("dp", "fsdp"), None),
        P(("dp", "fsdp"), None),
        P(("dp", "fsdp"), None),
        P(("dp", "fsdp")),
        P(("dp", "fsdp")),
        P(("dp", "fsdp")),
        P(("dp", "fsdp")),
    )
    return jax.shard_map(
        functools.partial(per_device, mesh.shape["dp"], mesh.shape["fsdp"]),
        mesh=mesh,
        in_specs=placed,
        out_specs=(
            P(("dp", "fsdp"), None, None),
            P(("dp", "fsdp"), None, None),
            P(("dp", "fsdp"), None),
            P(("dp", "fsdp"), None),
            P(("dp", "fsdp"), None),
            P(("dp", "fsdp"), None),
            P(("dp", "fsdp")),
            P(("dp", "fsdp")),
            P(("dp", "fsdp")),
            P(("dp", "fsdp")),
            P(),
        ),
        check_vma=False,
    )
```

```python
import functools

import jax
import jax.numpy as jnp
from jax import lax
from jax.experimental import pallas as pl
from jax.experimental.pallas import tpu as pltpu
from jax.sharding import PartitionSpec as P

H = 12
BUCKETS = 16384
LOW = 256
BLOCKS = 8
CORE, NEAR_X, NEAR_Y = 1, 2, 4
PLACES = (0, NEAR_X, NEAR_Y, NEAR_X + NEAR_Y)
BOTH = ("dp", "fsdp")


def swap(value, bit):
    return lax.ppermute(value, "dp", [(i, i ^ bit) for i in range(BLOCKS)])


def swap_inner(value, bit, size):
    return lax.ppermute(value, "fsdp", [(i, i ^ bit) for i in range(size)])


def by_bits(parts, index):
    bit = 1
    while bit < len(parts):
        odd = (index & bit) != 0
        parts = [jnp.where(odd, parts[j ^ bit], parts[j]) for j in range(len(parts))]
        bit *= 2
    return parts


def direct(ranks, inner):
    return ranks == BLOCKS and inner & (inner - 1) == 0


def gather_whole(shard):
    near = lax.all_gather(shard, "fsdp", axis=0, tiled=True)
    whole = lax.all_gather(near, "dp", axis=0, tiled=True)
    whole = whole.reshape(4, 2, -1, whole.shape[1])
    return [whole[:, 0], whole[:, 1]], [0, CORE]


def gather_inner(shard, inner):
    parts = [shard] + [swap_inner(shard, k, inner) for k in range(1, inner)]
    return jnp.concatenate(by_bits(parts, lax.axis_index("fsdp")), axis=0)


def gather_sides(own):
    return [own] + [swap(own, bits) for bits in PLACES[1:]]


def with_core(pieces):
    joined = jnp.stack(pieces)
    return [joined, swap(joined, CORE)], [0, CORE]


def after(value, *others):
    return lax.optimization_barrier((value, *others))[0]


def together(values, *others):
    return list(lax.optimization_barrier((*values, *others)))[: len(values)]


def gather_first(shards, inner, counts, segments):
    own = gather_inner(shards[0], inner)
    own, second, counts, segments = together([own, shards[1], counts, segments])
    sides = gather_sides(own)
    parts = [second] + [swap_inner(second, k, inner) for k in range(1, inner)]
    values = together([*sides, *parts])
    sides, parts = values[:4], values[4:]
    keep, other = halve_tables(counts, CORE)
    own_second = jnp.concatenate(by_bits(parts, lax.axis_index("fsdp")), axis=0)
    first = with_core(sides)
    own_second, third, other = together([own_second, shards[2], other], *first[0])
    parts = [swap_inner(third, k, inner) for k in range(1, inner - 1)]
    return first, gather_sides(own_second), [third] + parts, keep, other, segments


def halve_tables(counts, bit):
    tables = counts.shape[0] // 2
    upper = (lax.axis_index("dp") & bit) != 0
    keep = jnp.where(upper, counts[tables:], counts[:tables])
    send = jnp.where(upper, counts[:tables], counts[tables:])
    return keep, swap(send, bit)


def double_tables(counts, other, bit):
    upper = (lax.axis_index("dp") & bit) != 0
    return jnp.concatenate(
        [jnp.where(upper, other, counts), jnp.where(upper, counts, other)], axis=0
    )


def add(*terms):
    total = terms[0].astype(jnp.float32)
    for term in terms[1:]:
        total = total + term.astype(jnp.float32)
    return total.astype(jnp.bfloat16)


def scatter_core(keep, send):
    other = swap(send, CORE)
    return [add(keep[place], other[place]) for place in range(4)]


def scatter_sides(parts):
    return [swap(part, bits) for part, bits in zip(parts[1:], PLACES[1:])]


def scatter_corner(parts):
    half = parts[3].shape[0] // 2
    return [swap(parts[3][:half], NEAR_Y), swap(parts[3][half:], NEAR_X)]


def scatter_rest(parts, corners):
    half = parts[3].shape[0] // 2
    first, second = corners
    to_x = jnp.concatenate([add(parts[1][:half], first), parts[1][half:]], axis=0)
    to_y = jnp.concatenate([parts[2][:half], add(parts[2][half:], second)], axis=0)
    return [swap(to_x, NEAR_X), swap(to_y, NEAR_Y)]


def scatter_inner(mine, inner):
    part = mine.shape[0] // inner
    parts = [mine[j * part : (j + 1) * part] for j in range(inner)]
    parts = by_bits(parts, lax.axis_index("fsdp"))
    return parts[:1] + [swap_inner(parts[k], k, inner) for k in range(1, inner)]


def sum_parts(parts):
    total = parts[0].astype(jnp.float32)
    for part in parts[1:]:
        total = total + part.astype(jnp.float32)
    return total


def scatter_whole(keep, send):
    whole = jnp.stack([keep, send], axis=1).reshape(-1, keep.shape[2])
    near = lax.psum_scatter(whole, "dp", scatter_dimension=0, tiled=True)
    return lax.psum_scatter(near, "fsdp", scatter_dimension=0, tiled=True).astype(jnp.float32)


def piece_pairs(refs, plan, me, block, target, sems, column=0):
    pairs = []
    for ref, first in zip(refs, plan):
        for place, bits in enumerate(PLACES):
            start = pl.multiple_of((me ^ first ^ bits) * block, 16)
            pairs.append(
                (
                    ref.at[place, :, column : column + target.shape[1]],
                    target.at[pl.ds(start, block), :],
                    sems.at[len(pairs)],
                )
            )
    return pairs


def load_pieces(*details):
    copies = [pltpu.make_async_copy(*pair) for pair in piece_pairs(*details)]
    for copy in copies:
        copy.start()
    return copies


def count_kernel(ids_ref, counts_ref):
    _, high_count, low_count = counts_ref.shape
    tables, length = ids_ref.shape
    high_at = lax.broadcasted_iota(jnp.int32, (high_count, length), 0)
    low_at = lax.broadcasted_iota(jnp.int32, (low_count, length), 0)
    for table in range(tables):
        ids = ids_ref[table : table + 1, :]
        upper = lax.shift_right_logical(ids, 8)
        lower = jnp.bitwise_and(ids, low_count - 1)
        counts_ref[table] = dot_nt(
            jnp.where(high_at == upper, 1.0, 0.0).astype(jnp.bfloat16),
            jnp.where(low_at == lower, 1.0, 0.0).astype(jnp.bfloat16),
        ).astype(jnp.int32)


def count_buckets(ids):
    tables = ids.shape[0]
    counts = pl.pallas_call(
        count_kernel,
        out_shape=jax.ShapeDtypeStruct((tables, BUCKETS // LOW, LOW), jnp.int32),
        cost_estimate=pl.CostEstimate(flops=3 * 10**9, bytes_accessed=10**6, transcendentals=0),
    )(ids)
    return counts.reshape(tables, BUCKETS)


def norm_parts(values):
    centered = values - jnp.mean(values, axis=-1, keepdims=True)
    spread = jnp.mean(centered * centered, axis=-1, keepdims=True)
    factor = lax.rsqrt(spread + 1e-12)
    return centered * factor, factor


def dot_nn(first, second):
    return jnp.dot(first, second, preferred_element_type=jnp.float32)


def dot_nt(first, second):
    return lax.dot_general(
        first, second, (((1,), (1,)), ((), ())), preferred_element_type=jnp.float32
    )


def flip_axes(matrix):
    return matrix.T


def attend_kernel(plan, count, me_ref, x_ref, seg_ref, *rest):
    pieces = rest[:count]
    qkv_ref, expo_ref, inv_ref, mixed_ref, ht_ref, o_ref, vec_ref, w_ref, sems = rest[count:]
    length, width = x_ref.shape[1:]
    head_dim = width // H

    @pl.when(pl.program_id(0) == 0)
    def _():
        for copy in load_pieces(pieces, plan, me_ref[0], width // BLOCKS, w_ref, sems):
            copy.wait()
        vec_ref[...] = w_ref[:, 3 * width :].astype(jnp.float32).T[:8]

    normed, _ = norm_parts(x_ref[0].astype(jnp.float32))
    h_one = (normed * vec_ref[0:1] + vec_ref[1:2]).astype(jnp.bfloat16)
    ht_ref[0] = flip_axes(h_one)
    qkv = dot_nn(h_one, w_ref[:, : 3 * width]).astype(jnp.bfloat16)
    qkv_ref[0, :, :width] = qkv[:, :width] * (1.0 / head_dim**0.5)
    qkv_ref[0, :, width:] = qkv[:, width:]
    lane = lax.broadcasted_iota(jnp.int32, (length, 128), 1)
    seg = seg_ref[0]
    key_seg = jnp.where(seg == lane, 1.0, 0.0).astype(jnp.bfloat16)
    query_seg = jnp.where(seg == lane, 0.0, -1e30).astype(jnp.bfloat16)
    for pair in range(H // 2):
        cols = slice(pair * 128, pair * 128 + 128)
        queries = qkv_ref[0, :, cols]
        keys = qkv_ref[0, :, width + pair * 128 : width + pair * 128 + 128]
        values = qkv_ref[0, :, 2 * width + pair * 128 : 2 * width + pair * 128 + 128]
        key_wide = jnp.concatenate([keys, key_seg], axis=1)
        values_t = flip_axes(values)
        parts = []
        for half in range(2):
            inside = (lane < head_dim) if half == 0 else (lane >= head_dim)
            query_half = jnp.where(inside, queries, jnp.zeros_like(queries))
            scores = dot_nt(key_wide, jnp.concatenate([query_half, query_seg], axis=1))
            top = jnp.max(scores, axis=0, keepdims=True)
            expo = jnp.exp(scores - top)
            inverse = 1.0 / jnp.sum(expo, axis=0, keepdims=True)
            expo = expo.astype(jnp.bfloat16)
            expo_ref[0, 2 * pair + half] = expo
            inv_ref[0, 2 * pair + half] = inverse
            out = dot_nn(values_t, expo)
            parts.append(out[half * head_dim : (half + 1) * head_dim] * inverse)
        mixed = jnp.concatenate(parts, axis=0)
        mixed_ref[0, cols, :] = mixed.astype(jnp.bfloat16)
        o_ref[0, :, cols] = mixed.T.astype(jnp.bfloat16)


def whole_spec(shape):
    zeros = (0,) * len(shape)
    return pl.BlockSpec(shape, lambda *_: zeros, pipeline_mode=pl.Buffered(1))


def row_spec(shape):
    rest = (0,) * (len(shape) - 1)
    return pl.BlockSpec((1,) + shape[1:], lambda r, *_: (r,) + rest)


def any_specs(pieces):
    return [pl.BlockSpec(memory_space=pl.ANY) for _ in pieces]


def kernel_params(mebibytes):
    return pltpu.CompilerParams(vmem_limit_bytes=mebibytes * 1024 * 1024)


def attend(tokens, segments, me, pieces, plan):
    rows, length, width = tokens.shape
    shapes = (
        jax.ShapeDtypeStruct((rows, length, 3 * width), jnp.bfloat16),
        jax.ShapeDtypeStruct((rows, H, length, length), jnp.bfloat16),
        jax.ShapeDtypeStruct((rows, H, 1, length), jnp.float32),
        jax.ShapeDtypeStruct((rows, width, length), jnp.bfloat16),
        jax.ShapeDtypeStruct((rows, width, length), jnp.bfloat16),
        jax.ShapeDtypeStruct((rows, length, width), jnp.bfloat16),
        jax.ShapeDtypeStruct((8, width), jnp.float32),
    )
    return list(pl.pallas_call(
        functools.partial(attend_kernel, plan, len(pieces)),
        grid=(rows,),
        in_specs=[
            pl.BlockSpec(memory_space=pltpu.SMEM),
            row_spec(tokens.shape),
            row_spec(segments.shape),
        ]
        + any_specs(pieces),
        out_specs=[row_spec(s.shape) for s in shapes[:-1]] + [whole_spec((8, width))],
        out_shape=shapes,
        scratch_shapes=[
            pltpu.VMEM((width, 3 * width + 128), jnp.bfloat16),
            pltpu.SemaphoreType.DMA((BLOCKS,)),
        ],
        compiler_params=kernel_params(58),
        cost_estimate=pl.CostEstimate(
            flops=10**9, bytes_accessed=10**6, transcendentals=0
        ),
    )(me, tokens, segments, *pieces))


def split_blocks(source, me, block, keep_ref, send_ref):
    for place, bits in enumerate(PLACES):
        start = pl.multiple_of((me ^ bits) * block, 16)
        keep_ref[place] = source[pl.ds(start, block), :].astype(jnp.bfloat16)
        start = pl.multiple_of((me ^ bits ^ CORE) * block, 16)
        send_ref[place] = source[pl.ds(start, block), :].astype(jnp.bfloat16)


def split_shapes(block, columns):
    return [jax.ShapeDtypeStruct((4, block, columns), jnp.bfloat16)] * 2


def forward_kernel(
    plan, count, me_ref, x_ref, o_ref, cot_ref, vec_ref, *rest
):
    pieces = rest[:count]
    (
        y_ref, ht_ref, keep_ref, send_ref, rise_ref, act_ref, h_ref, w_ref, sems,
    ) = rest[count:]
    step = pl.program_id(0)
    width = y_ref.shape[1]
    chunk = act_ref.shape[1]
    hidden = w_ref.shape[1] - width

    @pl.when(step == 0)
    def _():
        for copy in load_pieces(pieces, plan, me_ref[0], width // BLOCKS, w_ref, sems):
            copy.wait()
        y_ref[...] = x_ref[...].astype(jnp.float32) + dot_nn(o_ref[...], w_ref[:, hidden:])
        normed, _ = norm_parts(y_ref[...])
        h_ref[...] = (normed * vec_ref[2:3] + vec_ref[3:4]).astype(jnp.bfloat16)
        ht_ref[...] = flip_axes(h_ref[...])

    span = pl.ds(pl.multiple_of(step * chunk, chunk), chunk)
    slope = (2.0 / 3.141592653589793) ** 0.5
    upper = dot_nn(h_ref[...], w_ref[:, span])
    square = upper * upper
    half = 0.5 + 0.5 * jnp.tanh(upper * (slope + (slope * 0.044715) * square))
    active = upper * half
    inner = (2.0 * slope) + (6.0 * 0.044715 * slope) * square
    rise_ref[...] = (half + active * (1.0 - half) * inner).astype(jnp.bfloat16)
    active = active.astype(jnp.bfloat16)
    act_ref[...] = active
    down_grad = dot_nn(flip_axes(active), cot_ref[...]).astype(jnp.bfloat16)
    block = keep_ref.shape[1]
    for odd in range(2):

        @pl.when((me_ref[0] & 1) == odd)
        def _():
            keep_ref[0] = down_grad[odd * block : (odd + 1) * block]
            send_ref[0] = down_grad[(1 - odd) * block : (2 - odd) * block]


def feed_forward(tokens, mixed, cotangent, vec, me, pieces, plan):
    count, width = cotangent.shape
    hidden = pieces[0].shape[2] - width
    chunk = hidden // 4
    shapes = (
        jax.ShapeDtypeStruct((count, width), jnp.float32),
        jax.ShapeDtypeStruct((width, count), jnp.bfloat16),
        *split_shapes(hidden // BLOCKS, width),
        jax.ShapeDtypeStruct((count, hidden), jnp.bfloat16),
        jax.ShapeDtypeStruct((count, hidden), jnp.bfloat16),
    )
    half_spec = pl.BlockSpec((1, hidden // BLOCKS, width), lambda j, me: (j ^ (me[0] // 2), 0, 0))
    return pl.pallas_call(
        functools.partial(forward_kernel, plan, len(pieces)),
        grid_spec=pltpu.PrefetchScalarGridSpec(
            num_scalar_prefetch=1,
            grid=(hidden // chunk,),
            in_specs=[whole_spec((count, width))] * 3
            + [whole_spec(vec.shape)]
            + any_specs(pieces),
            out_specs=[whole_spec(s.shape) for s in shapes[:2]]
            + [half_spec] * 2
            + [pl.BlockSpec((count, chunk), lambda j, me: (0, j))] * 2,
            scratch_shapes=[
                pltpu.VMEM((count, width), jnp.bfloat16),
                pltpu.VMEM((width, hidden + width), jnp.bfloat16),
                pltpu.SemaphoreType.DMA((BLOCKS,)),
            ],
        ),
        out_shape=shapes,
        compiler_params=kernel_params(60),
        cost_estimate=pl.CostEstimate(flops=10**9, bytes_accessed=10**6, transcendentals=0),
    )(me, tokens, mixed, cotangent, vec, *pieces)


def norm_back(back, normed, factor, gain):
    scaled = back * gain
    inner = scaled - jnp.mean(scaled, axis=-1, keepdims=True)
    inner = inner - normed * jnp.mean(scaled * normed, axis=-1, keepdims=True)
    gain_grad = jnp.sum(back * normed, axis=0, keepdims=True)
    return factor * inner, gain_grad, jnp.sum(back, axis=0, keepdims=True)


def return_kernel(
    plan, count, plan_down, count_down, me_ref, y_ref, cot_ref, vec_ref, ht_ref, mixed_ref,
    rise_ref, act_ref, *rest
):
    pieces = rest[:count]
    down_pieces = rest[count : count + count_down]
    (
        grad_ref, out_ref, keep_ref, send_ref, sums_ref,
        acc_ref, du_ref, w_ref, wd_ref, part_ref, out_grad_ref, sems, down_sems,
    ) = rest[count + count_down :]
    step = pl.program_id(0)
    width = y_ref.shape[1]
    chunk = act_ref.shape[1]
    block = width // BLOCKS
    copies = [
        pltpu.make_async_copy(*pair)
        for pair in piece_pairs(pieces, plan, me_ref[0], block, w_ref, sems)
    ]

    @pl.when(step == 0)
    def _():
        down_copies = load_pieces(
            down_pieces, plan_down, me_ref[0], wd_ref.shape[0] // BLOCKS, wd_ref, down_sems
        )
        for copy in copies:
            copy.start()
        acc_ref[...] = y_ref[...]
        out_grad_ref[...] = jnp.zeros_like(out_grad_ref)
        sums_ref[...] = jnp.zeros_like(sums_ref)
        for copy in down_copies:
            copy.wait()

    @pl.when(step < pl.num_programs(0) - 1)
    def _():
        start = pl.multiple_of(step * chunk, chunk)
        down = wd_ref[pl.ds(start, chunk), :]
        grad_upper = (
            dot_nt(cot_ref[...], down) * rise_ref[...].astype(jnp.float32)
        ).astype(jnp.bfloat16)
        du_ref[:, pl.ds(start, chunk)] = grad_upper
        acc_ref[...] += dot_nn(act_ref[...], down)
        part_ref[...] = dot_nn(ht_ref[...], grad_upper)
        split_blocks(part_ref, me_ref[0], block, keep_ref, send_ref)

    @pl.when(step == pl.num_programs(0) - 1)
    def _():
        out_ref[...] = acc_ref[...].astype(jnp.bfloat16)
        for copy in copies:
            copy.wait()
        size = mixed_ref.shape[2]

        def body(place, carry):
            rows = pl.ds(pl.multiple_of(place * size, size), size)
            back = dot_nt(du_ref[rows, :], w_ref[...])
            normed, factor = norm_parts(y_ref[rows, :])
            through, gain_grad, bias_grad = norm_back(back, normed, factor, vec_ref[2:3])
            sums_ref[0:1] += gain_grad
            sums_ref[1:2] += bias_grad
            grad = cot_ref[rows, :].astype(jnp.float32) + through
            grad_ref[rows, :] = grad
            out_grad_ref[...] += dot_nn(mixed_ref[place], grad.astype(jnp.bfloat16))
            return carry

        lax.fori_loop(0, mixed_ref.shape[0], body, 0)
        split_blocks(out_grad_ref, me_ref[0], block, keep_ref, send_ref)


def feed_return(y_one, cotangent, vec, h_t, mixed, rise, active, me, pieces, plan, down_pieces, plan_down):
    count, width = cotangent.shape
    hidden = active.shape[1]
    chunk = hidden // 4
    shapes = (
        jax.ShapeDtypeStruct((count, width), jnp.float32),
        jax.ShapeDtypeStruct((count, width), jnp.bfloat16),
        *split_shapes(width // BLOCKS, hidden + width),
        jax.ShapeDtypeStruct((8, width), jnp.float32),
    )
    return pl.pallas_call(
        functools.partial(
            return_kernel, plan, len(pieces), plan_down, len(down_pieces)
        ),
        grid=(hidden // chunk + 1,),
        in_specs=[pl.BlockSpec(memory_space=pltpu.SMEM)]
        + [whole_spec(v.shape) for v in (y_one, cotangent, vec, h_t, mixed)]
        + [
            pl.BlockSpec((count, chunk), lambda j: (0, jnp.minimum(j, 3))),
            pl.BlockSpec((count, chunk), lambda j: (0, jnp.minimum(j, 3))),
        ]
        + any_specs(pieces)
        + any_specs(down_pieces),
        out_specs=[whole_spec(s.shape) for s in shapes[:2]]
        + [pl.BlockSpec((4, width // BLOCKS, width), lambda j: (0, 0, j))] * 2
        + [whole_spec((8, width))],
        out_shape=shapes,
        scratch_shapes=[
            pltpu.VMEM((count, width), jnp.float32),
            pltpu.VMEM((count, hidden), jnp.bfloat16),
            pltpu.VMEM((width, hidden), jnp.bfloat16),
            pltpu.VMEM((hidden, width), jnp.bfloat16),
            pltpu.VMEM((width, chunk), jnp.float32),
            pltpu.VMEM((width, width), jnp.float32),
            pltpu.SemaphoreType.DMA((BLOCKS,)),
            pltpu.SemaphoreType.DMA((BLOCKS,)),
        ],
        compiler_params=kernel_params(60),
        cost_estimate=pl.CostEstimate(
            flops=10**9, bytes_accessed=10**6, transcendentals=0
        ),
    )(me, y_one, cotangent, vec, h_t, mixed, rise, active, *pieces, *down_pieces)


def heads_back(queries, keys, values, grads_t, mixed_t, expos, inverses, head_dim):
    length = queries.shape[0]
    lane = lax.broadcasted_iota(jnp.int32, (length, 128), 1)
    inside = lane < head_dim
    one_lane = jnp.where(lane < 2, 1.0, 0.0).astype(jnp.bfloat16)
    pad_rows = jnp.zeros((126, length), jnp.bfloat16)
    gap_rows = jnp.zeros((head_dim, length), jnp.bfloat16)
    keys_t = flip_axes(keys)
    value_wide = jnp.concatenate([values, one_lane], axis=1)
    grad_pair = grads_t.astype(jnp.float32)
    product = grad_pair * mixed_t.astype(jnp.float32)
    spans = [slice(half * head_dim, (half + 1) * head_dim) for half in range(2)]
    scaled = [
        (grad_pair[span] * inverse).astype(jnp.bfloat16)
        for span, inverse in zip(spans, inverses)
    ]
    scaled_pair = jnp.concatenate(scaled, axis=0)
    dv = []
    dk = []
    dq = []
    for half, span in enumerate(spans):
        delta = -jnp.sum(product[span], axis=0, keepdims=True) * inverses[half]
        high = delta.astype(jnp.bfloat16)
        low = (delta - high.astype(jnp.float32)).astype(jnp.bfloat16)
        first = [scaled[0], gap_rows] if half == 0 else [gap_rows, scaled[1]]
        grad_wide = jnp.concatenate(first + [high, low, pad_rows], axis=0)
        expo = expos[half]
        grad_scores = (expo.astype(jnp.float32) * dot_nn(value_wide, grad_wide)).astype(
            jnp.bfloat16
        )
        dv.append(dot_nt(expo, scaled_pair))
        dk.append(dot_nn(grad_scores, queries))
        dq.append(dot_nn(keys_t, grad_scores)[span] * (1.0 / head_dim**0.5))
    return (
        jnp.concatenate(dq, axis=0).T.astype(jnp.bfloat16),
        jnp.where(inside, dk[0], dk[1]).astype(jnp.bfloat16),
        jnp.where(inside, dv[0], dv[1]).astype(jnp.bfloat16),
    )


def backward_kernel(
    plan, count, groups, me_ref, grad_ref, q_ref, k_ref, v_ref, expo_ref, inv_ref, mixed_ref, ht_ref,
    *rest
):
    pieces = rest[:count]
    dqkv_ref, keep_ref, send_ref, dot_ref, acc_ref, wout_ref, sems = rest[count:]
    row = pl.program_id(0)
    group = pl.program_id(1)
    length, width = grad_ref.shape[1:]
    head_dim = width // H
    block = width // BLOCKS
    wide = q_ref.shape[2]
    me = me_ref[0]

    @pl.when((row == 0) & (group == 0))
    def _():
        copies = load_pieces(
            pieces, plan, me, block, wout_ref, sems, pieces[0].shape[2] - width
        )
        acc_ref[...] = jnp.zeros_like(acc_ref)
        for copy in copies:
            copy.wait()

    @pl.when(group == 0)
    def _():
        attn_in = grad_ref[0].astype(jnp.bfloat16)
        dot_ref[...] = dot_nt(wout_ref[...], attn_in).astype(jnp.bfloat16)

    results = []
    for pair in range(wide // 128):
        cols = slice(pair * 128, pair * 128 + 128)
        start = pl.multiple_of(group * wide + pair * 128, 128)
        results.append(
            heads_back(
                q_ref[0, :, cols], k_ref[0, :, cols], v_ref[0, :, cols],
                dot_ref[pl.ds(start, 128), :], mixed_ref[0, cols, :],
                [expo_ref[0, 2 * pair + half] for half in range(2)],
                [inv_ref[0, 2 * pair + half] for half in range(2)],
                head_dim,
            )
        )
    joined = [jnp.concatenate(list(values), axis=1) for values in zip(*results)]
    for place, value in enumerate(joined):
        start = pl.multiple_of(place * width + group * wide, 128)
        acc_ref[:, pl.ds(start, wide)] += dot_nn(ht_ref[0], value)
        dqkv_ref[0, :, pl.ds(start, wide)] = value

    @pl.when((row == pl.num_programs(0) - 1) & (group == groups - 1))
    def _():
        split_blocks(acc_ref, me, block, keep_ref, send_ref)


def backward(grad_y, saved, me, pieces, plan):
    rows, length, width = grad_y.shape
    qkv, expo, inverse, mixed, h_t = saved
    wide = 256
    heads = wide * H // width
    groups = width // wide

    def column_spec(kind):
        return pl.BlockSpec((1, length, wide), lambda r, g: (r, 0, kind * groups + g))

    inputs = [me, grad_y, qkv, qkv, qkv, expo, inverse, mixed, h_t, *pieces]
    in_specs = [
        pl.BlockSpec(memory_space=pltpu.SMEM),
        row_spec(grad_y.shape),
        column_spec(0),
        column_spec(1),
        column_spec(2),
        pl.BlockSpec((1, heads, length, length), lambda r, g: (r, g, 0, 0)),
        pl.BlockSpec((1, heads, 1, length), lambda r, g: (r, g, 0, 0)),
        pl.BlockSpec((1, wide, length), lambda r, g: (r, g, 0)),
        row_spec(h_t.shape),
    ] + any_specs(pieces)
    shapes = [jax.ShapeDtypeStruct((rows, length, 3 * width), jnp.bfloat16)]
    shapes += split_shapes(width // BLOCKS, 3 * width)
    return pl.pallas_call(
        functools.partial(backward_kernel, plan, len(pieces), groups),
        grid=(rows, groups),
        in_specs=in_specs,
        out_specs=[row_spec(shapes[0].shape)] + [whole_spec(s.shape) for s in shapes[1:]],
        out_shape=shapes,
        scratch_shapes=[
            pltpu.VMEM((width, length), jnp.bfloat16),
            pltpu.VMEM((width, 3 * width), jnp.float32),
            pltpu.VMEM((width, width), jnp.bfloat16),
            pltpu.SemaphoreType.DMA((BLOCKS,)),
        ],
        compiler_params=kernel_params(58),
        cost_estimate=pl.CostEstimate(flops=10**9, bytes_accessed=10**6, transcendentals=0),
    )(*inputs)


def finish_kernel(
    plan, count, me_ref, grad_ref, x_ref, dqkv_ref, vec_ref, ffn_sums_ref, *rest
):
    pieces = rest[:count]
    tokens_grad_ref, keep_ref, send_ref, w_ref, vec_acc, sems = rest[count:]
    row = pl.program_id(0)
    block = w_ref.shape[0] // BLOCKS
    normed, factor = norm_parts(x_ref[0].astype(jnp.float32))

    @pl.when(row == 0)
    def _():
        copies = load_pieces(pieces, plan, me_ref[0], block, w_ref, sems)
        vec_acc[...] = jnp.zeros_like(vec_acc)
        vec_acc[2:4] = ffn_sums_ref[0:2]
        for copy in copies:
            copy.wait()

    back = dot_nt(dqkv_ref[0], w_ref[...])
    through, gain_grad, bias_grad = norm_back(back, normed, factor, vec_ref[0:1])
    vec_acc[0:1] += gain_grad
    vec_acc[1:2] += bias_grad
    tokens_grad_ref[0] = (grad_ref[0] + through).astype(jnp.bfloat16)

    @pl.when(row == pl.num_programs(0) - 1)
    def _():
        vec_t = vec_acc[...].T
        vec_acc[...] = jnp.zeros_like(vec_acc)
        w_ref[:, :128] = vec_t.astype(jnp.bfloat16)
        for place, bits in enumerate(PLACES):
            start = pl.multiple_of((me_ref[0] ^ bits) * block, 16)
            keep_ref[place] = w_ref[pl.ds(start, block), :128]
            start = pl.multiple_of((me_ref[0] ^ bits ^ CORE) * block, 16)
            send_ref[place] = w_ref[pl.ds(start, block), :128]


def finish(grad_y, tokens, dqkv, vec, ffn_sums, me, pieces, plan):
    rows, length, width = tokens.shape
    shapes = [jax.ShapeDtypeStruct(tokens.shape, jnp.bfloat16)]
    shapes += split_shapes(width // BLOCKS, 128)
    return pl.pallas_call(
        functools.partial(finish_kernel, plan, len(pieces)),
        grid=(rows,),
        in_specs=[pl.BlockSpec(memory_space=pltpu.SMEM)]
        + [row_spec(v.shape) for v in (grad_y, tokens, dqkv)]
        + [whole_spec(vec.shape), whole_spec(ffn_sums.shape)]
        + any_specs(pieces),
        out_specs=[row_spec(tokens.shape)] + [whole_spec(s.shape) for s in shapes[1:]],
        out_shape=shapes,
        scratch_shapes=[
            pltpu.VMEM((width, 3 * width), jnp.bfloat16),
            pltpu.VMEM((128, width), jnp.float32),
            pltpu.SemaphoreType.DMA((BLOCKS,)),
        ],
        compiler_params=kernel_params(58),
        cost_estimate=pl.CostEstimate(flops=10**9, bytes_accessed=10**6, transcendentals=0),
    )(me, grad_y, tokens, dqkv, vec, ffn_sums, *pieces)


def layer(ranks, inner, tokens, segments, cotangent, me, front, counts):
    rows, length, width = tokens.shape
    flat_shape = (rows * length, width)
    flat_cot = cotangent.reshape(flat_shape)
    first = front[0]
    near = direct(ranks, inner)
    *saved, o, vec = attend(tokens, segments, me, *first)
    if near:
        _, sides, parts, keep, other = front
        *values, o, other = together([*sides, *parts, o, other])
        sides, parts = values[:4], values[4:]
        parts.append(swap_inner(parts[0], inner - 1, inner))
        own_third = jnp.concatenate(by_bits(parts, lax.axis_index("fsdp")), axis=0)
        second = with_core(sides)
        keep, other = halve_tables(keep + other, NEAR_X)
        own_third, second[0][1] = together([own_third, second[0][1]])
        sides = gather_sides(own_third)
    else:
        second, third = front[1:]
    y_one, h_t, *down_parts, rise, active = feed_forward(
        tokens.reshape(flat_shape), o.reshape(flat_shape), flat_cot, vec, me, *second
    )
    if near:
        *sides, y_one, down_parts[1], other = together([*sides, y_one, down_parts[1], other])
        keep, other = halve_tables(keep + other, NEAR_Y)
        third = with_core(sides)
        down_parts = scatter_core(*down_parts)
        y_one, *down_parts = together([y_one, *down_parts])
        down_received = scatter_sides(down_parts)
    grad_y, layer_output, *up_parts, ffn_sums = feed_return(
        y_one, flat_cot, vec, h_t, saved[3], rise, active, me, *second, *third
    )
    if near:
        *down_received, up_parts[1], grad_y, other = together(
            [*down_received, up_parts[1], grad_y, other]
        )
        counts = keep + other
        others = [swap_inner(counts, k, inner) for k in range(1, inner)]
        parts = scatter_core(*up_parts)
        down_mine = add(down_parts[0], *down_received)
        *values, grad_y, down_mine = together([*parts, *others, grad_y, down_mine])
        parts, others = values[:4], values[4:]
        counts = sum(others, counts)
        received = scatter_sides(parts)
        size = down_mine.shape[0] // inner
        pieces = [down_mine[k * size : (k + 1) * size] for k in range(inner)]
        pieces = by_bits(pieces, lax.axis_index("fsdp"))
        down_inner = [swap_inner(pieces[k], k, inner) for k in range(1, inner - 1)]
    grad_y = grad_y.reshape(tokens.shape)
    dqkv, *early = backward(grad_y, saved, me, *second)
    if near:
        *values, dqkv, early[1], piece, counts = together(
            [*received, *down_inner, dqkv, early[1], pieces[-1], counts]
        )
        received, down_inner = values[:3], values[3:]
        other = swap(counts, NEAR_Y)
        down_inner.append(swap_inner(piece, inner - 1, inner))
        early_parts = scatter_core(*early)
        up_mine = add(parts[0], *received)
        size = up_mine.shape[0] // inner
        up_pieces = [up_mine[k * size : (k + 1) * size] for k in range(inner)]
        up_pieces = by_bits(up_pieces, lax.axis_index("fsdp"))
        *values, dqkv, other = together([*early_parts, *down_inner, *up_pieces, dqkv, other])
        early_parts, down_inner = values[:4], values[4 : 3 + inner]
        up_pieces = values[3 + inner :]
        counts = double_tables(counts, other, NEAR_Y)
        other = swap(counts, NEAR_X)
        dqkv, other = together([dqkv, other])
        counts = double_tables(counts, other, NEAR_X)
        down_sum = sum_parts(pieces[:1] + down_inner)
        early_received = scatter_sides(early_parts)
        up_inner = [swap_inner(up_pieces[k], k, inner) for k in range(1, inner - 1)]
    tokens_grad, *late = finish(grad_y, tokens, dqkv, vec, ffn_sums, me, *first)
    if near:
        *up_inner, tokens_grad, late[1], piece, counts = together(
            [*up_inner, tokens_grad, late[1], up_pieces[-1], counts]
        )
        late_parts = scatter_core(*late)
        other = swap(counts, CORE)
        *late_parts, other = together([*late_parts, other])
        counts = double_tables(counts, other, CORE)
        late_received = scatter_sides(late_parts)
        *values, piece = together([*early_received, *late_received, piece])
        early_received, late_received = values[:3], values[3:]
        early_mine = add(early_parts[0], *early_received)
        up_inner.append(swap_inner(piece, inner - 1, inner))
        early_sum = sum_parts(scatter_inner(early_mine, inner))
        up_sum = sum_parts(up_pieces[:1] + up_inner)
        late_sum = sum_parts(scatter_inner(add(late_parts[0], *late_received), inner))
    else:
        up_sum, down_sum, early_sum, late_sum = [
            scatter_whole(*v) for v in (up_parts, down_parts, early, late)
        ]
    hidden = active.shape[1]
    return (
        layer_output.reshape(tokens.shape),
        tokens_grad,
        early_sum,
        up_sum[:, hidden:],
        up_sum[:, :hidden],
        down_sum,
        late_sum,
        counts,
    )


def per_device(
    ranks,
    inner,
    tokens,
    segment_ids,
    bucket_ids,
    cotangent,
    qkv_weight,
    out_weight,
    up_weight,
    down_weight,
    attn_gain,
    attn_bias,
    ffn_gain,
    ffn_bias,
):
    vectors = jnp.stack([attn_gain, attn_bias, ffn_gain, ffn_bias], axis=1)
    vectors = jnp.pad(vectors, ((0, 0), (0, 124)))
    ids = bucket_ids.reshape(-1, bucket_ids.shape[2]).T
    counts = count_buckets(ids)
    segments = segment_ids[:, :, None]
    shards = (
        jnp.concatenate([qkv_weight, vectors], axis=1),
        jnp.concatenate([up_weight, out_weight], axis=1),
        down_weight,
    )
    if direct(ranks, inner):
        me = lax.axis_index("dp").reshape(1).astype(jnp.int32)
        *front, segments = gather_first(shards, inner, counts, segments)
    else:
        me = jnp.zeros((1,), jnp.int32)
        front = [gather_whole(shard) for shard in shards]
        counts = lax.psum(counts, BOTH)
    *results, vec_sums, counts = layer(
        ranks, inner, tokens, segments, cotangent, me, front, counts
    )
    return (*results, *[vec_sums[:, place] for place in range(4)], counts)


def solution(mesh):
    placed = (
        P(("dp", "fsdp"), None, None),
        P(("dp", "fsdp"), None),
        P(("dp", "fsdp"), None, None),
        P(("dp", "fsdp"), None, None),
        P(("dp", "fsdp"), None),
        P(("dp", "fsdp"), None),
        P(("dp", "fsdp"), None),
        P(("dp", "fsdp"), None),
        P(("dp", "fsdp")),
        P(("dp", "fsdp")),
        P(("dp", "fsdp")),
        P(("dp", "fsdp")),
    )
    return jax.shard_map(
        functools.partial(per_device, mesh.shape["dp"], mesh.shape["fsdp"]),
        mesh=mesh,
        in_specs=placed,
        out_specs=(
            P(("dp", "fsdp"), None, None),
            P(("dp", "fsdp"), None, None),
            P(("dp", "fsdp"), None),
            P(("dp", "fsdp"), None),
            P(("dp", "fsdp"), None),
            P(("dp", "fsdp"), None),
            P(("dp", "fsdp")),
            P(("dp", "fsdp")),
            P(("dp", "fsdp")),
            P(("dp", "fsdp")),
            P(),
        ),
        check_vma=False,
    )
```

```python
import functools

import jax
import jax.numpy as jnp
from jax import lax
from jax.experimental import pallas as pl
from jax.experimental.pallas import tpu as pltpu
from jax.sharding import PartitionSpec as P

H = 12
BUCKETS = 16384
LOW = 256
BLOCKS = 8
CORE, NEAR_X, NEAR_Y = 1, 2, 4
PLACES = (0, NEAR_X, NEAR_Y, NEAR_X + NEAR_Y)
BOTH = ("dp", "fsdp")


def swap(value, bit):
    return lax.ppermute(value, "dp", [(i, i ^ bit) for i in range(BLOCKS)])


def swap_inner(value, bit, size):
    return lax.ppermute(value, "fsdp", [(i, i ^ bit) for i in range(size)])


def by_bits(parts, index):
    bit = 1
    while bit < len(parts):
        odd = (index & bit) != 0
        parts = [jnp.where(odd, parts[j ^ bit], parts[j]) for j in range(len(parts))]
        bit *= 2
    return parts


def direct(ranks, inner):
    return ranks == BLOCKS and inner & (inner - 1) == 0


def gather_whole(shard):
    near = lax.all_gather(shard, "fsdp", axis=0, tiled=True)
    whole = lax.all_gather(near, "dp", axis=0, tiled=True)
    whole = whole.reshape(4, 2, -1, whole.shape[1])
    return [whole[:, 0], whole[:, 1]], [0, CORE]


def gather_inner(shard, inner):
    parts = [shard] + [swap_inner(shard, k, inner) for k in range(1, inner)]
    return jnp.concatenate(by_bits(parts, lax.axis_index("fsdp")), axis=0)


def gather_sides(own):
    return [own] + [swap(own, bits) for bits in PLACES[1:]]


def with_core(pieces):
    joined = jnp.stack(pieces)
    return [joined, swap(joined, CORE)], [0, CORE]


def after(value, *others):
    return lax.optimization_barrier((value, *others))[0]


def together(values, *others):
    return list(lax.optimization_barrier((*values, *others)))[: len(values)]


def gather_first(shards, inner, counts, segments):
    own = gather_inner(shards[0], inner)
    own, second, counts, segments = together([own, shards[1], counts, segments])
    sides = gather_sides(own)
    parts = [second] + [swap_inner(second, k, inner) for k in range(1, inner)]
    values = together([*sides, *parts])
    sides, parts = values[:4], values[4:]
    keep, other = halve_tables(counts, CORE)
    own_second = jnp.concatenate(by_bits(parts, lax.axis_index("fsdp")), axis=0)
    first = with_core(sides)
    own_second, third, other = together([own_second, shards[2], other], *first[0])
    parts = [swap_inner(third, k, inner) for k in range(1, inner - 1)]
    return first, gather_sides(own_second), [third] + parts, keep, other, segments


def halve_tables(counts, bit):
    tables = counts.shape[0] // 2
    upper = (lax.axis_index("dp") & bit) != 0
    keep = jnp.where(upper, counts[tables:], counts[:tables])
    send = jnp.where(upper, counts[:tables], counts[tables:])
    return keep, swap(send, bit)


def double_tables(counts, other, bit):
    upper = (lax.axis_index("dp") & bit) != 0
    return jnp.concatenate(
        [jnp.where(upper, other, counts), jnp.where(upper, counts, other)], axis=0
    )


def add(*terms):
    total = terms[0].astype(jnp.float32)
    for term in terms[1:]:
        total = total + term.astype(jnp.float32)
    return total.astype(jnp.bfloat16)


def scatter_core(keep, send):
    other = swap(send, CORE)
    return [add(keep[place], other[place]) for place in range(4)]


def scatter_sides(parts):
    return [swap(part, bits) for part, bits in zip(parts[1:], PLACES[1:])]


def scatter_corner(parts):
    half = parts[3].shape[0] // 2
    return [swap(parts[3][:half], NEAR_Y), swap(parts[3][half:], NEAR_X)]


def scatter_rest(parts, corners):
    half = parts[3].shape[0] // 2
    first, second = corners
    to_x = jnp.concatenate([add(parts[1][:half], first), parts[1][half:]], axis=0)
    to_y = jnp.concatenate([parts[2][:half], add(parts[2][half:], second)], axis=0)
    return [swap(to_x, NEAR_X), swap(to_y, NEAR_Y)]


def scatter_inner(mine, inner):
    part = mine.shape[0] // inner
    parts = [mine[j * part : (j + 1) * part] for j in range(inner)]
    parts = by_bits(parts, lax.axis_index("fsdp"))
    return parts[:1] + [swap_inner(parts[k], k, inner) for k in range(1, inner)]


def sum_parts(parts):
    total = parts[0].astype(jnp.float32)
    for part in parts[1:]:
        total = total + part.astype(jnp.float32)
    return total


def scatter_whole(keep, send):
    whole = jnp.stack([keep, send], axis=1).reshape(-1, keep.shape[2])
    near = lax.psum_scatter(whole, "dp", scatter_dimension=0, tiled=True)
    return lax.psum_scatter(near, "fsdp", scatter_dimension=0, tiled=True).astype(jnp.float32)


def piece_pairs(refs, plan, me, block, target, sems, column=0):
    pairs = []
    for ref, first in zip(refs, plan):
        for place, bits in enumerate(PLACES):
            start = pl.multiple_of((me ^ first ^ bits) * block, 16)
            pairs.append(
                (
                    ref.at[place, :, column : column + target.shape[1]],
                    target.at[pl.ds(start, block), :],
                    sems.at[len(pairs)],
                )
            )
    return pairs


def load_pieces(*details):
    copies = [pltpu.make_async_copy(*pair) for pair in piece_pairs(*details)]
    for copy in copies:
        copy.start()
    return copies


def count_kernel(ids_ref, counts_ref):
    _, high_count, low_count = counts_ref.shape
    tables, length = ids_ref.shape
    high_at = lax.broadcasted_iota(jnp.int32, (high_count, length), 0)
    low_at = lax.broadcasted_iota(jnp.int32, (low_count, length), 0)
    for table in range(tables):
        ids = ids_ref[table : table + 1, :]
        upper = lax.shift_right_logical(ids, 8)
        lower = jnp.bitwise_and(ids, low_count - 1)
        counts_ref[table] = dot_nt(
            jnp.where(high_at == upper, 1.0, 0.0).astype(jnp.bfloat16),
            jnp.where(low_at == lower, 1.0, 0.0).astype(jnp.bfloat16),
        ).astype(jnp.int32)


def count_buckets(ids):
    tables = ids.shape[0]
    counts = pl.pallas_call(
        count_kernel,
        out_shape=jax.ShapeDtypeStruct((tables, BUCKETS // LOW, LOW), jnp.int32),
        cost_estimate=pl.CostEstimate(flops=3 * 10**9, bytes_accessed=10**6, transcendentals=0),
    )(ids)
    return counts.reshape(tables, BUCKETS)


def norm_parts(values):
    centered = values - jnp.mean(values, axis=-1, keepdims=True)
    spread = jnp.mean(centered * centered, axis=-1, keepdims=True)
    factor = lax.rsqrt(spread + 1e-12)
    return centered * factor, factor


def dot_nn(first, second):
    return jnp.dot(first, second, preferred_element_type=jnp.float32)


def dot_nt(first, second):
    return lax.dot_general(
        first, second, (((1,), (1,)), ((), ())), preferred_element_type=jnp.float32
    )


def flip_axes(matrix):
    return matrix.T


def attend_kernel(plan, count, me_ref, x_ref, seg_ref, *rest):
    pieces = rest[:count]
    qkv_ref, expo_ref, inv_ref, mixed_ref, ht_ref, o_ref, vec_ref, w_ref, sems = rest[count:]
    length, width = x_ref.shape[1:]
    head_dim = width // H

    @pl.when(pl.program_id(0) == 0)
    def _():
        for copy in load_pieces(pieces, plan, me_ref[0], width // BLOCKS, w_ref, sems):
            copy.wait()
        vec_ref[...] = w_ref[:, 3 * width :].astype(jnp.float32).T[:8]

    normed, _ = norm_parts(x_ref[0].astype(jnp.float32))
    h_one = (normed * vec_ref[0:1] + vec_ref[1:2]).astype(jnp.bfloat16)
    ht_ref[0] = flip_axes(h_one)
    qkv = dot_nn(h_one, w_ref[:, : 3 * width]).astype(jnp.bfloat16)
    qkv_ref[0, :, :width] = qkv[:, :width] * (1.0 / head_dim**0.5)
    qkv_ref[0, :, width:] = qkv[:, width:]
    lane = lax.broadcasted_iota(jnp.int32, (length, 128), 1)
    seg = jnp.broadcast_to(seg_ref[0], (128, length)).T.astype(jnp.int32)
    key_seg = jnp.where(seg == lane, 1.0, 0.0).astype(jnp.bfloat16)
    query_seg = jnp.where(seg == lane, 0.0, -1e30).astype(jnp.bfloat16)
    for pair in range(H // 2):
        cols = slice(pair * 128, pair * 128 + 128)
        queries = qkv_ref[0, :, cols]
        keys = qkv_ref[0, :, width + pair * 128 : width + pair * 128 + 128]
        values = qkv_ref[0, :, 2 * width + pair * 128 : 2 * width + pair * 128 + 128]
        key_wide = jnp.concatenate([keys, key_seg], axis=1)
        values_t = flip_axes(values)
        parts = []
        for half in range(2):
            inside = (lane < head_dim) if half == 0 else (lane >= head_dim)
            query_half = jnp.where(inside, queries, jnp.zeros_like(queries))
            scores = dot_nt(key_wide, jnp.concatenate([query_half, query_seg], axis=1))
            top = jnp.max(scores, axis=0, keepdims=True)
            expo = jnp.exp(scores - top)
            inverse = 1.0 / jnp.sum(expo, axis=0, keepdims=True)
            expo = expo.astype(jnp.bfloat16)
            expo_ref[0, 2 * pair + half] = expo
            inv_ref[0, 2 * pair + half] = inverse
            out = dot_nn(values_t, expo)
            parts.append(out[half * head_dim : (half + 1) * head_dim] * inverse)
        mixed = jnp.concatenate(parts, axis=0)
        mixed_ref[0, cols, :] = mixed.astype(jnp.bfloat16)
        o_ref[0, :, cols] = mixed.T.astype(jnp.bfloat16)


def whole_spec(shape):
    zeros = (0,) * len(shape)
    return pl.BlockSpec(shape, lambda *_: zeros, pipeline_mode=pl.Buffered(1))


def row_spec(shape):
    rest = (0,) * (len(shape) - 1)
    return pl.BlockSpec((1,) + shape[1:], lambda r, *_: (r,) + rest)


def any_specs(pieces):
    return [pl.BlockSpec(memory_space=pl.ANY) for _ in pieces]


def kernel_params(mebibytes):
    return pltpu.CompilerParams(vmem_limit_bytes=mebibytes * 1024 * 1024)


def attend(tokens, segments, me, pieces, plan):
    rows, length, width = tokens.shape
    shapes = (
        jax.ShapeDtypeStruct((rows, length, 3 * width), jnp.bfloat16),
        jax.ShapeDtypeStruct((rows, H, length, length), jnp.bfloat16),
        jax.ShapeDtypeStruct((rows, H, 1, length), jnp.float32),
        jax.ShapeDtypeStruct((rows, width, length), jnp.bfloat16),
        jax.ShapeDtypeStruct((rows, width, length), jnp.bfloat16),
        jax.ShapeDtypeStruct((rows, length, width), jnp.bfloat16),
        jax.ShapeDtypeStruct((8, width), jnp.float32),
    )
    return list(pl.pallas_call(
        functools.partial(attend_kernel, plan, len(pieces)),
        grid=(rows,),
        in_specs=[
            pl.BlockSpec(memory_space=pltpu.SMEM),
            row_spec(tokens.shape),
            row_spec(segments.shape),
        ]
        + any_specs(pieces),
        out_specs=[row_spec(s.shape) for s in shapes[:-1]] + [whole_spec((8, width))],
        out_shape=shapes,
        scratch_shapes=[
            pltpu.VMEM((width, 3 * width + 128), jnp.bfloat16),
            pltpu.SemaphoreType.DMA((BLOCKS,)),
        ],
        compiler_params=kernel_params(58),
        cost_estimate=pl.CostEstimate(
            flops=10**9, bytes_accessed=10**6, transcendentals=0
        ),
    )(me, tokens, segments, *pieces))


def split_blocks(source, me, block, keep_ref, send_ref):
    for place, bits in enumerate(PLACES):
        start = pl.multiple_of((me ^ bits) * block, 16)
        keep_ref[place] = source[pl.ds(start, block), :].astype(jnp.bfloat16)
        start = pl.multiple_of((me ^ bits ^ CORE) * block, 16)
        send_ref[place] = source[pl.ds(start, block), :].astype(jnp.bfloat16)


def split_shapes(block, columns):
    return [jax.ShapeDtypeStruct((4, block, columns), jnp.bfloat16)] * 2


def forward_kernel(
    plan, count, me_ref, x_ref, o_ref, cot_ref, vec_ref, *rest
):
    pieces = rest[:count]
    (
        y_ref, ht_ref, keep_ref, send_ref, rise_ref, act_ref, h_ref, w_ref, sems,
    ) = rest[count:]
    step = pl.program_id(0)
    width = y_ref.shape[1]
    chunk = act_ref.shape[1]
    hidden = w_ref.shape[1] - width

    @pl.when(step == 0)
    def _():
        for copy in load_pieces(pieces, plan, me_ref[0], width // BLOCKS, w_ref, sems):
            copy.wait()
        y_ref[...] = x_ref[...].astype(jnp.float32) + dot_nn(o_ref[...], w_ref[:, hidden:])
        normed, _ = norm_parts(y_ref[...])
        h_ref[...] = (normed * vec_ref[2:3] + vec_ref[3:4]).astype(jnp.bfloat16)
        ht_ref[...] = flip_axes(h_ref[...])

    span = pl.ds(pl.multiple_of(step * chunk, chunk), chunk)
    slope = (2.0 / 3.141592653589793) ** 0.5
    upper = dot_nn(h_ref[...], w_ref[:, span])
    square = upper * upper
    half = 0.5 + 0.5 * jnp.tanh(upper * (slope + (slope * 0.044715) * square))
    active = upper * half
    inner = (2.0 * slope) + (6.0 * 0.044715 * slope) * square
    rise_ref[...] = (half + active * (1.0 - half) * inner).astype(jnp.bfloat16)
    active = active.astype(jnp.bfloat16)
    act_ref[...] = active
    down_grad = dot_nn(flip_axes(active), cot_ref[...]).astype(jnp.bfloat16)
    block = keep_ref.shape[1]
    for odd in range(2):

        @pl.when((me_ref[0] & 1) == odd)
        def _():
            keep_ref[0] = down_grad[odd * block : (odd + 1) * block]
            send_ref[0] = down_grad[(1 - odd) * block : (2 - odd) * block]


def feed_forward(tokens, mixed, cotangent, vec, me, pieces, plan):
    count, width = cotangent.shape
    hidden = pieces[0].shape[2] - width
    chunk = hidden // 4
    shapes = (
        jax.ShapeDtypeStruct((count, width), jnp.float32),
        jax.ShapeDtypeStruct((width, count), jnp.bfloat16),
        *split_shapes(hidden // BLOCKS, width),
        jax.ShapeDtypeStruct((count, hidden), jnp.bfloat16),
        jax.ShapeDtypeStruct((count, hidden), jnp.bfloat16),
    )
    half_spec = pl.BlockSpec((1, hidden // BLOCKS, width), lambda j, me: (j ^ (me[0] // 2), 0, 0))
    return pl.pallas_call(
        functools.partial(forward_kernel, plan, len(pieces)),
        grid_spec=pltpu.PrefetchScalarGridSpec(
            num_scalar_prefetch=1,
            grid=(hidden // chunk,),
            in_specs=[whole_spec((count, width))] * 3
            + [whole_spec(vec.shape)]
            + any_specs(pieces),
            out_specs=[whole_spec(s.shape) for s in shapes[:2]]
            + [half_spec] * 2
            + [pl.BlockSpec((count, chunk), lambda j, me: (0, j))] * 2,
            scratch_shapes=[
                pltpu.VMEM((count, width), jnp.bfloat16),
                pltpu.VMEM((width, hidden + width), jnp.bfloat16),
                pltpu.SemaphoreType.DMA((BLOCKS,)),
            ],
        ),
        out_shape=shapes,
        compiler_params=kernel_params(60),
        cost_estimate=pl.CostEstimate(flops=10**9, bytes_accessed=10**6, transcendentals=0),
    )(me, tokens, mixed, cotangent, vec, *pieces)


def norm_back(back, normed, factor, gain):
    scaled = back * gain
    inner = scaled - jnp.mean(scaled, axis=-1, keepdims=True)
    inner = inner - normed * jnp.mean(scaled * normed, axis=-1, keepdims=True)
    gain_grad = jnp.sum(back * normed, axis=0, keepdims=True)
    return factor * inner, gain_grad, jnp.sum(back, axis=0, keepdims=True)


def return_kernel(
    plan, count, plan_down, count_down, me_ref, y_hbm, cot_ref, vec_ref, ht_ref, mixed_hbm,
    rise_ref, act_ref, *rest
):
    pieces = rest[:count]
    down_pieces = rest[count : count + count_down]
    (
        grad_ref, out_ref, keep_ref, send_ref, sums_ref,
        acc_ref, du_ref, w_ref, wd_ref, part_ref, out_grad_ref, y_ref, mixed_ref,
        sems, down_sems, late_sems,
    ) = rest[count + count_down :]
    step = pl.program_id(0)
    width = cot_ref.shape[1]
    chunk = act_ref.shape[1]
    block = width // BLOCKS
    copies = [
        pltpu.make_async_copy(*pair)
        for pair in piece_pairs(pieces, plan, me_ref[0], block, w_ref, sems)
    ]
    copies.append(pltpu.make_async_copy(y_hbm, y_ref, late_sems.at[0]))
    copies.append(pltpu.make_async_copy(mixed_hbm, mixed_ref, late_sems.at[1]))

    @pl.when(step == 0)
    def _():
        down_copies = load_pieces(
            down_pieces, plan_down, me_ref[0], wd_ref.shape[0] // BLOCKS, wd_ref, down_sems
        )
        for copy in copies:
            copy.start()
        acc_ref[...] = jnp.zeros_like(acc_ref)
        out_grad_ref[...] = jnp.zeros_like(out_grad_ref)
        sums_ref[...] = jnp.zeros_like(sums_ref)
        for copy in down_copies:
            copy.wait()

    @pl.when(step < pl.num_programs(0) - 1)
    def _():
        start = pl.multiple_of(step * chunk, chunk)
        down = wd_ref[pl.ds(start, chunk), :]
        grad_upper = (
            dot_nt(cot_ref[...], down) * rise_ref[...].astype(jnp.float32)
        ).astype(jnp.bfloat16)
        du_ref[:, pl.ds(start, chunk)] = grad_upper
        acc_ref[...] += dot_nn(act_ref[...], down)
        part_ref[...] = dot_nn(ht_ref[...], grad_upper)
        split_blocks(part_ref, me_ref[0], block, keep_ref, send_ref)

    @pl.when(step == pl.num_programs(0) - 1)
    def _():
        for copy in copies:
            copy.wait()
        out_ref[...] = (y_ref[...] + acc_ref[...]).astype(jnp.bfloat16)
        size = mixed_ref.shape[2]

        def body(place, carry):
            rows = pl.ds(pl.multiple_of(place * size, size), size)
            back = dot_nt(du_ref[rows, :], w_ref[...])
            normed, factor = norm_parts(y_ref[rows, :])
            through, gain_grad, bias_grad = norm_back(back, normed, factor, vec_ref[2:3])
            sums_ref[0:1] += gain_grad
            sums_ref[1:2] += bias_grad
            grad = cot_ref[rows, :].astype(jnp.float32) + through
            grad_ref[rows, :] = grad
            out_grad_ref[...] += dot_nn(mixed_ref[place], grad.astype(jnp.bfloat16))
            return carry

        lax.fori_loop(0, mixed_ref.shape[0], body, 0)
        split_blocks(out_grad_ref, me_ref[0], block, keep_ref, send_ref)


def feed_return(y_one, cotangent, vec, h_t, mixed, rise, active, me, pieces, plan, down_pieces, plan_down):
    count, width = cotangent.shape
    hidden = active.shape[1]
    chunk = hidden // 4
    shapes = (
        jax.ShapeDtypeStruct((count, width), jnp.float32),
        jax.ShapeDtypeStruct((count, width), jnp.bfloat16),
        *split_shapes(width // BLOCKS, hidden + width),
        jax.ShapeDtypeStruct((8, width), jnp.float32),
    )
    return pl.pallas_call(
        functools.partial(
            return_kernel, plan, len(pieces), plan_down, len(down_pieces)
        ),
        grid=(hidden // chunk + 1,),
        in_specs=[pl.BlockSpec(memory_space=pltpu.SMEM)]
        + any_specs([y_one])
        + [whole_spec(v.shape) for v in (cotangent, vec, h_t)]
        + any_specs([mixed])
        + [
            pl.BlockSpec((count, chunk), lambda j: (0, jnp.minimum(j, 3))),
            pl.BlockSpec((count, chunk), lambda j: (0, jnp.minimum(j, 3))),
        ]
        + any_specs(pieces)
        + any_specs(down_pieces),
        out_specs=[whole_spec(s.shape) for s in shapes[:2]]
        + [pl.BlockSpec((4, width // BLOCKS, width), lambda j: (0, 0, j))] * 2
        + [whole_spec((8, width))],
        out_shape=shapes,
        scratch_shapes=[
            pltpu.VMEM((count, width), jnp.float32),
            pltpu.VMEM((count, hidden), jnp.bfloat16),
            pltpu.VMEM((width, hidden), jnp.bfloat16),
            pltpu.VMEM((hidden, width), jnp.bfloat16),
            pltpu.VMEM((width, chunk), jnp.float32),
            pltpu.VMEM((width, width), jnp.float32),
            pltpu.VMEM((count, width), jnp.float32),
            pltpu.VMEM(mixed.shape, jnp.bfloat16),
            pltpu.SemaphoreType.DMA((BLOCKS,)),
            pltpu.SemaphoreType.DMA((BLOCKS,)),
            pltpu.SemaphoreType.DMA((2,)),
        ],
        compiler_params=kernel_params(60),
        cost_estimate=pl.CostEstimate(
            flops=10**9, bytes_accessed=10**6, transcendentals=0
        ),
    )(me, y_one, cotangent, vec, h_t, mixed, rise, active, *pieces, *down_pieces)


def heads_back(queries, keys, values, grads_t, mixed_t, expos, inverses, head_dim):
    length = queries.shape[0]
    lane = lax.broadcasted_iota(jnp.int32, (length, 128), 1)
    inside = lane < head_dim
    one_lane = jnp.where(lane < 2, 1.0, 0.0).astype(jnp.bfloat16)
    pad_rows = jnp.zeros((126, length), jnp.bfloat16)
    gap_rows = jnp.zeros((head_dim, length), jnp.bfloat16)
    keys_t = flip_axes(keys)
    value_wide = jnp.concatenate([values, one_lane], axis=1)
    grad_pair = grads_t.astype(jnp.float32)
    product = grad_pair * mixed_t.astype(jnp.float32)
    spans = [slice(half * head_dim, (half + 1) * head_dim) for half in range(2)]
    scaled = [
        (grad_pair[span] * inverse).astype(jnp.bfloat16)
        for span, inverse in zip(spans, inverses)
    ]
    scaled_pair = jnp.concatenate(scaled, axis=0)
    dv = []
    dk = []
    dq = []
    for half, span in enumerate(spans):
        delta = -jnp.sum(product[span], axis=0, keepdims=True) * inverses[half]
        high = delta.astype(jnp.bfloat16)
        low = (delta - high.astype(jnp.float32)).astype(jnp.bfloat16)
        first = [scaled[0], gap_rows] if half == 0 else [gap_rows, scaled[1]]
        grad_wide = jnp.concatenate(first + [high, low, pad_rows], axis=0)
        expo = expos[half]
        grad_scores = (expo.astype(jnp.float32) * dot_nn(value_wide, grad_wide)).astype(
            jnp.bfloat16
        )
        dv.append(dot_nt(expo, scaled_pair))
        dk.append(dot_nn(grad_scores, queries))
        dq.append(dot_nn(keys_t, grad_scores)[span] * (1.0 / head_dim**0.5))
    return (
        jnp.concatenate(dq, axis=0).T.astype(jnp.bfloat16),
        jnp.where(inside, dk[0], dk[1]).astype(jnp.bfloat16),
        jnp.where(inside, dv[0], dv[1]).astype(jnp.bfloat16),
    )


def backward_kernel(
    plan, count, groups, me_ref, grad_ref, q_ref, k_ref, v_ref, expo_ref, inv_ref, mixed_ref, ht_ref,
    *rest
):
    pieces = rest[:count]
    dqkv_ref, keep_ref, send_ref, dot_ref, acc_ref, wout_ref, sems = rest[count:]
    row = pl.program_id(0)
    group = pl.program_id(1)
    length, width = grad_ref.shape[1:]
    head_dim = width // H
    block = width // BLOCKS
    wide = q_ref.shape[2]
    me = me_ref[0]

    @pl.when((row == 0) & (group == 0))
    def _():
        copies = load_pieces(
            pieces, plan, me, block, wout_ref, sems, pieces[0].shape[2] - width
        )
        acc_ref[...] = jnp.zeros_like(acc_ref)
        for copy in copies:
            copy.wait()

    @pl.when(group == 0)
    def _():
        attn_in = grad_ref[0].astype(jnp.bfloat16)
        dot_ref[...] = dot_nt(wout_ref[...], attn_in).astype(jnp.bfloat16)

    results = []
    for pair in range(wide // 128):
        cols = slice(pair * 128, pair * 128 + 128)
        start = pl.multiple_of(group * wide + pair * 128, 128)
        results.append(
            heads_back(
                q_ref[0, :, cols], k_ref[0, :, cols], v_ref[0, :, cols],
                dot_ref[pl.ds(start, 128), :], mixed_ref[0, cols, :],
                [expo_ref[0, 2 * pair + half] for half in range(2)],
                [inv_ref[0, 2 * pair + half] for half in range(2)],
                head_dim,
            )
        )
    joined = [jnp.concatenate(list(values), axis=1) for values in zip(*results)]
    for place, value in enumerate(joined):
        start = pl.multiple_of(place * width + group * wide, 128)
        acc_ref[:, pl.ds(start, wide)] += dot_nn(ht_ref[0], value)
        dqkv_ref[0, :, pl.ds(start, wide)] = value

    @pl.when((row == pl.num_programs(0) - 1) & (group == groups - 1))
    def _():
        split_blocks(acc_ref, me, block, keep_ref, send_ref)


def backward(grad_y, saved, me, pieces, plan):
    rows, length, width = grad_y.shape
    qkv, expo, inverse, mixed, h_t = saved
    wide = 256
    heads = wide * H // width
    groups = width // wide

    def column_spec(kind):
        return pl.BlockSpec((1, length, wide), lambda r, g: (r, 0, kind * groups + g))

    inputs = [me, grad_y, qkv, qkv, qkv, expo, inverse, mixed, h_t, *pieces]
    in_specs = [
        pl.BlockSpec(memory_space=pltpu.SMEM),
        row_spec(grad_y.shape),
        column_spec(0),
        column_spec(1),
        column_spec(2),
        pl.BlockSpec((1, heads, length, length), lambda r, g: (r, g, 0, 0)),
        pl.BlockSpec((1, heads, 1, length), lambda r, g: (r, g, 0, 0)),
        pl.BlockSpec((1, wide, length), lambda r, g: (r, g, 0)),
        row_spec(h_t.shape),
    ] + any_specs(pieces)
    shapes = [jax.ShapeDtypeStruct((rows, length, 3 * width), jnp.bfloat16)]
    shapes += split_shapes(width // BLOCKS, 3 * width)
    return pl.pallas_call(
        functools.partial(backward_kernel, plan, len(pieces), groups),
        grid=(rows, groups),
        in_specs=in_specs,
        out_specs=[row_spec(shapes[0].shape)] + [whole_spec(s.shape) for s in shapes[1:]],
        out_shape=shapes,
        scratch_shapes=[
            pltpu.VMEM((width, length), jnp.bfloat16),
            pltpu.VMEM((width, 3 * width), jnp.float32),
            pltpu.VMEM((width, width), jnp.bfloat16),
            pltpu.SemaphoreType.DMA((BLOCKS,)),
        ],
        compiler_params=kernel_params(58),
        cost_estimate=pl.CostEstimate(flops=10**9, bytes_accessed=10**6, transcendentals=0),
    )(*inputs)


def finish_kernel(
    plan, count, me_ref, grad_ref, x_ref, dqkv_ref, vec_ref, ffn_sums_ref, *rest
):
    pieces = rest[:count]
    tokens_grad_ref, keep_ref, send_ref, w_ref, vec_acc, sems = rest[count:]
    row = pl.program_id(0)
    block = w_ref.shape[0] // BLOCKS
    normed, factor = norm_parts(x_ref[0].astype(jnp.float32))

    @pl.when(row == 0)
    def _():
        copies = load_pieces(pieces, plan, me_ref[0], block, w_ref, sems)
        vec_acc[...] = jnp.zeros_like(vec_acc)
        vec_acc[2:4] = ffn_sums_ref[0:2]
        for copy in copies:
            copy.wait()

    back = dot_nt(dqkv_ref[0], w_ref[...])
    through, gain_grad, bias_grad = norm_back(back, normed, factor, vec_ref[0:1])
    vec_acc[0:1] += gain_grad
    vec_acc[1:2] += bias_grad
    tokens_grad_ref[0] = (grad_ref[0] + through).astype(jnp.bfloat16)

    @pl.when(row == pl.num_programs(0) - 1)
    def _():
        vec_t = vec_acc[...].T
        vec_acc[...] = jnp.zeros_like(vec_acc)
        w_ref[:, :128] = vec_t.astype(jnp.bfloat16)
        for place, bits in enumerate(PLACES):
            start = pl.multiple_of((me_ref[0] ^ bits) * block, 16)
            keep_ref[place] = w_ref[pl.ds(start, block), :128]
            start = pl.multiple_of((me_ref[0] ^ bits ^ CORE) * block, 16)
            send_ref[place] = w_ref[pl.ds(start, block), :128]


def finish(grad_y, tokens, dqkv, vec, ffn_sums, me, pieces, plan):
    rows, length, width = tokens.shape
    shapes = [jax.ShapeDtypeStruct(tokens.shape, jnp.bfloat16)]
    shapes += split_shapes(width // BLOCKS, 128)
    return pl.pallas_call(
        functools.partial(finish_kernel, plan, len(pieces)),
        grid=(rows,),
        in_specs=[pl.BlockSpec(memory_space=pltpu.SMEM)]
        + [row_spec(v.shape) for v in (grad_y, tokens, dqkv)]
        + [whole_spec(vec.shape), whole_spec(ffn_sums.shape)]
        + any_specs(pieces),
        out_specs=[row_spec(tokens.shape)] + [whole_spec(s.shape) for s in shapes[1:]],
        out_shape=shapes,
        scratch_shapes=[
            pltpu.VMEM((width, 3 * width), jnp.bfloat16),
            pltpu.VMEM((128, width), jnp.float32),
            pltpu.SemaphoreType.DMA((BLOCKS,)),
        ],
        compiler_params=kernel_params(58),
        cost_estimate=pl.CostEstimate(flops=10**9, bytes_accessed=10**6, transcendentals=0),
    )(me, grad_y, tokens, dqkv, vec, ffn_sums, *pieces)


def layer(ranks, inner, tokens, segments, cotangent, me, front, counts):
    rows, length, width = tokens.shape
    flat_shape = (rows * length, width)
    flat_cot = cotangent.reshape(flat_shape)
    first = front[0]
    near = direct(ranks, inner)
    *saved, o, vec = attend(tokens, segments, me, *first)
    if near:
        _, sides, parts, keep, other = front
        *values, o, other = together([*sides, *parts, o, other])
        sides, parts = values[:4], values[4:]
        parts.append(swap_inner(parts[0], inner - 1, inner))
        own_third = jnp.concatenate(by_bits(parts, lax.axis_index("fsdp")), axis=0)
        second = with_core(sides)
        keep, other = halve_tables(keep + other, NEAR_X)
        own_third, second[0][1] = together([own_third, second[0][1]])
        sides = gather_sides(own_third)
    else:
        second, third = front[1:]
    y_one, h_t, *down_parts, rise, active = feed_forward(
        tokens.reshape(flat_shape), o.reshape(flat_shape), flat_cot, vec, me, *second
    )
    if near:
        *sides, y_one, down_parts[1], other = together([*sides, y_one, down_parts[1], other])
        keep, other = halve_tables(keep + other, NEAR_Y)
        third = with_core(sides)
        down_parts = scatter_core(*down_parts)
        y_one, *down_parts = together([y_one, *down_parts])
        down_received = scatter_sides(down_parts)
    grad_y, layer_output, *up_parts, ffn_sums = feed_return(
        y_one, flat_cot, vec, h_t, saved[3], rise, active, me, *second, *third
    )
    if near:
        *down_received, up_parts[1], grad_y, other = together(
            [*down_received, up_parts[1], grad_y, other]
        )
        counts = keep + other
        others = [swap_inner(counts, k, inner) for k in range(1, inner)]
        parts = scatter_core(*up_parts)
        down_mine = add(down_parts[0], *down_received)
        *values, grad_y, down_mine = together([*parts, *others, grad_y, down_mine])
        parts, others = values[:4], values[4:]
        counts = sum(others, counts)
        received = scatter_sides(parts)
        size = down_mine.shape[0] // inner
        pieces = [down_mine[k * size : (k + 1) * size] for k in range(inner)]
        pieces = by_bits(pieces, lax.axis_index("fsdp"))
        down_inner = [swap_inner(pieces[k], k, inner) for k in range(1, inner - 1)]
    grad_y = grad_y.reshape(tokens.shape)
    dqkv, *early = backward(grad_y, saved, me, *second)
    if near:
        *values, dqkv, early[1], piece, counts = together(
            [*received, *down_inner, dqkv, early[1], pieces[-1], counts]
        )
        received, down_inner = values[:3], values[3:]
        other = swap(counts, NEAR_Y)
        down_inner.append(swap_inner(piece, inner - 1, inner))
        early_parts = scatter_core(*early)
        up_mine = add(parts[0], *received)
        size = up_mine.shape[0] // inner
        up_pieces = [up_mine[k * size : (k + 1) * size] for k in range(inner)]
        up_pieces = by_bits(up_pieces, lax.axis_index("fsdp"))
        *values, dqkv, other = together([*early_parts, *down_inner, *up_pieces, dqkv, other])
        early_parts, down_inner = values[:4], values[4 : 3 + inner]
        up_pieces = values[3 + inner :]
        counts = double_tables(counts, other, NEAR_Y)
        other = swap(counts, NEAR_X)
        dqkv, other = together([dqkv, other])
        counts = double_tables(counts, other, NEAR_X)
        down_sum = sum_parts(pieces[:1] + down_inner)
        early_received = scatter_sides(early_parts)
        up_inner = [swap_inner(up_pieces[k], k, inner) for k in range(1, inner - 1)]
    tokens_grad, *late = finish(grad_y, tokens, dqkv, vec, ffn_sums, me, *first)
    if near:
        *up_inner, tokens_grad, late[1], piece, counts = together(
            [*up_inner, tokens_grad, late[1], up_pieces[-1], counts]
        )
        late_parts = scatter_core(*late)
        other = swap(counts, CORE)
        *late_parts, other = together([*late_parts, other])
        counts = double_tables(counts, other, CORE)
        late_received = scatter_sides(late_parts)
        *values, piece = together([*early_received, *late_received, piece])
        early_received, late_received = values[:3], values[3:]
        up_inner.append(swap_inner(piece, inner - 1, inner))
        early_mine = add(early_parts[0], *early_received)
        late_mine = add(late_parts[0], *late_received)
        both = jnp.concatenate([early_mine, late_mine], axis=1)
        both = sum_parts(scatter_inner(both, inner))
        up_sum = sum_parts(up_pieces[:1] + up_inner)
        early_sum, late_sum = both[:, : 3 * width], both[:, 3 * width :]
    else:
        up_sum, down_sum, early_sum, late_sum = [
            scatter_whole(*v) for v in (up_parts, down_parts, early, late)
        ]
    hidden = active.shape[1]
    return (
        layer_output.reshape(tokens.shape),
        tokens_grad,
        early_sum,
        up_sum[:, hidden:],
        up_sum[:, :hidden],
        down_sum,
        late_sum,
        counts,
    )


def per_device(
    ranks,
    inner,
    tokens,
    segment_ids,
    bucket_ids,
    cotangent,
    qkv_weight,
    out_weight,
    up_weight,
    down_weight,
    attn_gain,
    attn_bias,
    ffn_gain,
    ffn_bias,
):
    vectors = jnp.stack([attn_gain, attn_bias, ffn_gain, ffn_bias], axis=1)
    vectors = jnp.pad(vectors, ((0, 0), (0, 124)))
    ids = bucket_ids.reshape(-1, bucket_ids.shape[2]).T
    counts = count_buckets(ids)
    segments = segment_ids.astype(jnp.float32)[:, None, :]
    shards = (
        jnp.concatenate([qkv_weight, vectors], axis=1),
        jnp.concatenate([up_weight, out_weight], axis=1),
        down_weight,
    )
    if direct(ranks, inner):
        me = lax.axis_index("dp").reshape(1).astype(jnp.int32)
        *front, segments = gather_first(shards, inner, counts, segments)
    else:
        me = jnp.zeros((1,), jnp.int32)
        front = [gather_whole(shard) for shard in shards]
        counts = lax.psum(counts, BOTH)
    *results, vec_sums, counts = layer(
        ranks, inner, tokens, segments, cotangent, me, front, counts
    )
    return (*results, *[vec_sums[:, place] for place in range(4)], counts)


def solution(mesh):
    placed = (
        P(("dp", "fsdp"), None, None),
        P(("dp", "fsdp"), None),
        P(("dp", "fsdp"), None, None),
        P(("dp", "fsdp"), None, None),
        P(("dp", "fsdp"), None),
        P(("dp", "fsdp"), None),
        P(("dp", "fsdp"), None),
        P(("dp", "fsdp"), None),
        P(("dp", "fsdp")),
        P(("dp", "fsdp")),
        P(("dp", "fsdp")),
        P(("dp", "fsdp")),
    )
    return jax.shard_map(
        functools.partial(per_device, mesh.shape["dp"], mesh.shape["fsdp"]),
        mesh=mesh,
        in_specs=placed,
        out_specs=(
            P(("dp", "fsdp"), None, None),
            P(("dp", "fsdp"), None, None),
            P(("dp", "fsdp"), None),
            P(("dp", "fsdp"), None),
            P(("dp", "fsdp"), None),
            P(("dp", "fsdp"), None),
            P(("dp", "fsdp")),
            P(("dp", "fsdp")),
            P(("dp", "fsdp")),
            P(("dp", "fsdp")),
            P(),
        ),
        check_vma=False,
    )
```

```python
import functools

import jax
import jax.numpy as jnp
from jax import lax
from jax.experimental import pallas as pl
from jax.experimental.pallas import tpu as pltpu
from jax.sharding import PartitionSpec as P

H = 12
BUCKETS = 16384
LOW = 256
BLOCKS = 8
CORE, NEAR_X, NEAR_Y = 1, 2, 4
PLACES = (0, NEAR_X, NEAR_Y, NEAR_X + NEAR_Y)
BOTH = ("dp", "fsdp")


def swap(value, bit):
    return lax.ppermute(value, "dp", [(i, i ^ bit) for i in range(BLOCKS)])


def swap_inner(value, bit, size):
    return lax.ppermute(value, "fsdp", [(i, i ^ bit) for i in range(size)])


def by_bits(parts, index):
    bit = 1
    while bit < len(parts):
        odd = (index & bit) != 0
        parts = [jnp.where(odd, parts[j ^ bit], parts[j]) for j in range(len(parts))]
        bit *= 2
    return parts


def direct(ranks, inner):
    return ranks == BLOCKS and inner & (inner - 1) == 0


def gather_whole(shard):
    near = lax.all_gather(shard, "fsdp", axis=0, tiled=True)
    whole = lax.all_gather(near, "dp", axis=0, tiled=True)
    whole = whole.reshape(4, 2, -1, whole.shape[1])
    return [whole[:, 0], whole[:, 1]], [0, CORE]


def gather_inner(shard, inner):
    parts = [shard] + [swap_inner(shard, k, inner) for k in range(1, inner)]
    return jnp.concatenate(by_bits(parts, lax.axis_index("fsdp")), axis=0)


def gather_sides(own):
    return [own] + [swap(own, bits) for bits in PLACES[1:]]


def with_core(pieces):
    joined = jnp.stack(pieces)
    return [joined, swap(joined, CORE)], [0, CORE]


def after(value, *others):
    return lax.optimization_barrier((value, *others))[0]


def together(values, *others):
    return list(lax.optimization_barrier((*values, *others)))[: len(values)]


def gather_first(shards, inner, counts, segments):
    own = gather_inner(shards[0], inner)
    own, second, counts, segments = together([own, shards[1], counts, segments])
    sides = gather_sides(own)
    parts = [second] + [swap_inner(second, k, inner) for k in range(1, inner)]
    values = together([*sides, *parts])
    sides, parts = values[:4], values[4:]
    keep, other = halve_tables(counts, CORE)
    own_second = jnp.concatenate(by_bits(parts, lax.axis_index("fsdp")), axis=0)
    first = with_core(sides)
    own_second, third, other = together([own_second, shards[2], other], *first[0])
    parts = [swap_inner(third, k, inner) for k in range(1, inner - 1)]
    return first, gather_sides(own_second), [third] + parts, keep, other, segments


def halve_tables(counts, bit):
    tables = counts.shape[0] // 2
    upper = (lax.axis_index("dp") & bit) != 0
    keep = jnp.where(upper, counts[tables:], counts[:tables])
    send = jnp.where(upper, counts[:tables], counts[tables:])
    return keep, swap(send, bit)


def double_tables(counts, other, bit):
    upper = (lax.axis_index("dp") & bit) != 0
    return jnp.concatenate(
        [jnp.where(upper, other, counts), jnp.where(upper, counts, other)], axis=0
    )


def add(*terms):
    total = terms[0].astype(jnp.float32)
    for term in terms[1:]:
        total = total + term.astype(jnp.float32)
    return total.astype(jnp.bfloat16)


def scatter_core(keep, send):
    other = swap(send, CORE)
    return [add(keep[place], other[place]) for place in range(4)]


def scatter_sides(parts):
    return [swap(part, bits) for part, bits in zip(parts[1:], PLACES[1:])]


def scatter_corner(parts):
    half = parts[3].shape[0] // 2
    return [swap(parts[3][:half], NEAR_Y), swap(parts[3][half:], NEAR_X)]


def scatter_rest(parts, corners):
    half = parts[3].shape[0] // 2
    first, second = corners
    to_x = jnp.concatenate([add(parts[1][:half], first), parts[1][half:]], axis=0)
    to_y = jnp.concatenate([parts[2][:half], add(parts[2][half:], second)], axis=0)
    return [swap(to_x, NEAR_X), swap(to_y, NEAR_Y)]


def scatter_inner(mine, inner):
    part = mine.shape[0] // inner
    parts = [mine[j * part : (j + 1) * part] for j in range(inner)]
    parts = by_bits(parts, lax.axis_index("fsdp"))
    return parts[:1] + [swap_inner(parts[k], k, inner) for k in range(1, inner)]


def sum_parts(parts):
    total = parts[0].astype(jnp.float32)
    for part in parts[1:]:
        total = total + part.astype(jnp.float32)
    return total


def scatter_whole(keep, send):
    whole = jnp.stack([keep, send], axis=1).reshape(-1, keep.shape[2])
    near = lax.psum_scatter(whole, "dp", scatter_dimension=0, tiled=True)
    return lax.psum_scatter(near, "fsdp", scatter_dimension=0, tiled=True).astype(jnp.float32)


def piece_pairs(refs, plan, me, block, target, sems, column=0):
    pairs = []
    for ref, first in zip(refs, plan):
        for place, bits in enumerate(PLACES):
            start = pl.multiple_of((me ^ first ^ bits) * block, 16)
            pairs.append(
                (
                    ref.at[place, :, column : column + target.shape[1]],
                    target.at[pl.ds(start, block), :],
                    sems.at[len(pairs)],
                )
            )
    return pairs


def load_pieces(*details):
    copies = [pltpu.make_async_copy(*pair) for pair in piece_pairs(*details)]
    for copy in copies:
        copy.start()
    return copies


def count_kernel(ids_ref, counts_ref):
    _, high_count, low_count = counts_ref.shape
    tables, length = ids_ref.shape
    high_at = lax.broadcasted_iota(jnp.int32, (high_count, length), 0)
    low_at = lax.broadcasted_iota(jnp.int32, (low_count, length), 0)
    for table in range(tables):
        ids = ids_ref[table : table + 1, :]
        upper = lax.shift_right_logical(ids, 8)
        lower = jnp.bitwise_and(ids, low_count - 1)
        counts_ref[table] = dot_nt(
            jnp.where(high_at == upper, 1.0, 0.0).astype(jnp.bfloat16),
            jnp.where(low_at == lower, 1.0, 0.0).astype(jnp.bfloat16),
        ).astype(jnp.int32)


def count_buckets(ids):
    tables = ids.shape[0]
    counts = pl.pallas_call(
        count_kernel,
        out_shape=jax.ShapeDtypeStruct((tables, BUCKETS // LOW, LOW), jnp.int32),
        cost_estimate=pl.CostEstimate(flops=3 * 10**9, bytes_accessed=10**6, transcendentals=0),
    )(ids)
    return counts.reshape(tables, BUCKETS)


def norm_parts(values):
    centered = values - jnp.mean(values, axis=-1, keepdims=True)
    spread = jnp.mean(centered * centered, axis=-1, keepdims=True)
    factor = lax.rsqrt(spread + 1e-12)
    return centered * factor, factor


def dot_nn(first, second):
    return jnp.dot(first, second, preferred_element_type=jnp.float32)


def dot_nt(first, second):
    return lax.dot_general(
        first, second, (((1,), (1,)), ((), ())), preferred_element_type=jnp.float32
    )


def flip_axes(matrix):
    return matrix.T


def attend_kernel(plan, count, me_ref, x_ref, seg_ref, *rest):
    pieces = rest[:count]
    qkv_ref, expo_ref, inv_ref, mixed_ref, ht_ref, o_ref, vec_ref, w_ref, sems = rest[count:]
    length, width = x_ref.shape[1:]
    head_dim = width // H

    @pl.when(pl.program_id(0) == 0)
    def _():
        for copy in load_pieces(pieces, plan, me_ref[0], width // BLOCKS, w_ref, sems):
            copy.wait()
        vec_ref[...] = w_ref[:, 3 * width :].astype(jnp.float32).T[:8]

    normed, _ = norm_parts(x_ref[0].astype(jnp.float32))
    h_one = (normed * vec_ref[0:1] + vec_ref[1:2]).astype(jnp.bfloat16)
    ht_ref[0] = flip_axes(h_one)
    qkv = dot_nn(h_one, w_ref[:, : 3 * width]).astype(jnp.bfloat16)
    qkv_ref[0, :, :width] = qkv[:, :width] * (1.0 / head_dim**0.5)
    qkv_ref[0, :, width:] = qkv[:, width:]
    lane = lax.broadcasted_iota(jnp.int32, (length, 128), 1)
    seg = jnp.broadcast_to(seg_ref[0], (128, length)).T.astype(jnp.int32)
    key_seg = jnp.where(seg == lane, 1.0, 0.0).astype(jnp.bfloat16)
    query_seg = jnp.where(seg == lane, 0.0, -1e30).astype(jnp.bfloat16)
    for pair in range(H // 2):
        cols = slice(pair * 128, pair * 128 + 128)
        queries = qkv_ref[0, :, cols]
        keys = qkv_ref[0, :, width + pair * 128 : width + pair * 128 + 128]
        values = qkv_ref[0, :, 2 * width + pair * 128 : 2 * width + pair * 128 + 128]
        key_wide = jnp.concatenate([keys, key_seg], axis=1)
        values_t = flip_axes(values)
        parts = []
        for half in range(2):
            inside = (lane < head_dim) if half == 0 else (lane >= head_dim)
            query_half = jnp.where(inside, queries, jnp.zeros_like(queries))
            scores = dot_nt(key_wide, jnp.concatenate([query_half, query_seg], axis=1))
            top = jnp.max(scores, axis=0, keepdims=True)
            expo = jnp.exp(scores - top)
            inverse = 1.0 / jnp.sum(expo, axis=0, keepdims=True)
            expo = expo.astype(jnp.bfloat16)
            expo_ref[0, 2 * pair + half] = expo
            inv_ref[0, 2 * pair + half] = inverse
            out = dot_nn(values_t, expo)
            parts.append(out[half * head_dim : (half + 1) * head_dim] * inverse)
        mixed = jnp.concatenate(parts, axis=0)
        mixed_ref[0, cols, :] = mixed.astype(jnp.bfloat16)
        o_ref[0, :, cols] = mixed.T.astype(jnp.bfloat16)


def whole_spec(shape):
    zeros = (0,) * len(shape)
    return pl.BlockSpec(shape, lambda *_: zeros, pipeline_mode=pl.Buffered(1))


def row_spec(shape):
    rest = (0,) * (len(shape) - 1)
    return pl.BlockSpec((1,) + shape[1:], lambda r, *_: (r,) + rest)


def any_specs(pieces):
    return [pl.BlockSpec(memory_space=pl.ANY) for _ in pieces]


def kernel_params(mebibytes):
    return pltpu.CompilerParams(vmem_limit_bytes=mebibytes * 1024 * 1024)


def attend(tokens, segments, me, pieces, plan):
    rows, length, width = tokens.shape
    shapes = (
        jax.ShapeDtypeStruct((rows, length, 3 * width), jnp.bfloat16),
        jax.ShapeDtypeStruct((rows, H, length, length), jnp.bfloat16),
        jax.ShapeDtypeStruct((rows, H, 1, length), jnp.float32),
        jax.ShapeDtypeStruct((rows, width, length), jnp.bfloat16),
        jax.ShapeDtypeStruct((rows, width, length), jnp.bfloat16),
        jax.ShapeDtypeStruct((rows, length, width), jnp.bfloat16),
        jax.ShapeDtypeStruct((8, width), jnp.float32),
    )
    return list(pl.pallas_call(
        functools.partial(attend_kernel, plan, len(pieces)),
        grid=(rows,),
        in_specs=[
            pl.BlockSpec(memory_space=pltpu.SMEM),
            row_spec(tokens.shape),
            row_spec(segments.shape),
        ]
        + any_specs(pieces),
        out_specs=[row_spec(s.shape) for s in shapes[:-1]] + [whole_spec((8, width))],
        out_shape=shapes,
        scratch_shapes=[
            pltpu.VMEM((width, 3 * width + 128), jnp.bfloat16),
            pltpu.SemaphoreType.DMA((BLOCKS,)),
        ],
        compiler_params=kernel_params(58),
        cost_estimate=pl.CostEstimate(
            flops=10**9, bytes_accessed=10**6, transcendentals=0
        ),
    )(me, tokens, segments, *pieces))


def split_blocks(source, me, block, keep_ref, send_ref):
    for place, bits in enumerate(PLACES):
        start = pl.multiple_of((me ^ bits) * block, 16)
        keep_ref[place] = source[pl.ds(start, block), :].astype(jnp.bfloat16)
        start = pl.multiple_of((me ^ bits ^ CORE) * block, 16)
        send_ref[place] = source[pl.ds(start, block), :].astype(jnp.bfloat16)


def split_shapes(block, columns):
    return [jax.ShapeDtypeStruct((4, block, columns), jnp.bfloat16)] * 2


def forward_kernel(
    plan, count, me_ref, x_ref, o_ref, cot_ref, vec_ref, *rest
):
    pieces = rest[:count]
    (
        y_ref, ht_ref, keep_ref, send_ref, rise_ref, act_ref, h_ref, w_ref, sems,
    ) = rest[count:]
    step = pl.program_id(0)
    width = y_ref.shape[1]
    chunk = act_ref.shape[1]
    hidden = w_ref.shape[1] - width

    @pl.when(step == 0)
    def _():
        for copy in load_pieces(pieces, plan, me_ref[0], width // BLOCKS, w_ref, sems):
            copy.wait()
        y_ref[...] = x_ref[...].astype(jnp.float32) + dot_nn(o_ref[...], w_ref[:, hidden:])
        normed, _ = norm_parts(y_ref[...])
        h_ref[...] = (normed * vec_ref[2:3] + vec_ref[3:4]).astype(jnp.bfloat16)
        ht_ref[...] = flip_axes(h_ref[...])

    span = pl.ds(pl.multiple_of(step * chunk, chunk), chunk)
    slope = (2.0 / 3.141592653589793) ** 0.5
    upper = dot_nn(h_ref[...], w_ref[:, span])
    square = upper * upper
    half = 0.5 + 0.5 * jnp.tanh(upper * (slope + (slope * 0.044715) * square))
    active = upper * half
    inner = (2.0 * slope) + (6.0 * 0.044715 * slope) * square
    rise_ref[...] = (half + active * (1.0 - half) * inner).astype(jnp.bfloat16)
    active = active.astype(jnp.bfloat16)
    act_ref[...] = active
    down_grad = dot_nn(flip_axes(active), cot_ref[...]).astype(jnp.bfloat16)
    block = keep_ref.shape[1]
    for odd in range(2):

        @pl.when((me_ref[0] & 1) == odd)
        def _():
            keep_ref[0] = down_grad[odd * block : (odd + 1) * block]
            send_ref[0] = down_grad[(1 - odd) * block : (2 - odd) * block]


def feed_forward(tokens, mixed, cotangent, vec, me, pieces, plan):
    count, width = cotangent.shape
    hidden = pieces[0].shape[2] - width
    chunk = hidden // 4
    shapes = (
        jax.ShapeDtypeStruct((count, width), jnp.float32),
        jax.ShapeDtypeStruct((width, count), jnp.bfloat16),
        *split_shapes(hidden // BLOCKS, width),
        jax.ShapeDtypeStruct((count, hidden), jnp.bfloat16),
        jax.ShapeDtypeStruct((count, hidden), jnp.bfloat16),
    )
    half_spec = pl.BlockSpec((1, hidden // BLOCKS, width), lambda j, me: (j ^ (me[0] // 2), 0, 0))
    return pl.pallas_call(
        functools.partial(forward_kernel, plan, len(pieces)),
        grid_spec=pltpu.PrefetchScalarGridSpec(
            num_scalar_prefetch=1,
            grid=(hidden // chunk,),
            in_specs=[whole_spec((count, width))] * 3
            + [whole_spec(vec.shape)]
            + any_specs(pieces),
            out_specs=[whole_spec(s.shape) for s in shapes[:2]]
            + [half_spec] * 2
            + [pl.BlockSpec((count, chunk), lambda j, me: (0, j))] * 2,
            scratch_shapes=[
                pltpu.VMEM((count, width), jnp.bfloat16),
                pltpu.VMEM((width, hidden + width), jnp.bfloat16),
                pltpu.SemaphoreType.DMA((BLOCKS,)),
            ],
        ),
        out_shape=shapes,
        compiler_params=kernel_params(60),
        cost_estimate=pl.CostEstimate(flops=10**9, bytes_accessed=10**6, transcendentals=0),
    )(me, tokens, mixed, cotangent, vec, *pieces)


def norm_back(back, normed, factor, gain):
    scaled = back * gain
    inner = scaled - jnp.mean(scaled, axis=-1, keepdims=True)
    inner = inner - normed * jnp.mean(scaled * normed, axis=-1, keepdims=True)
    gain_grad = jnp.sum(back * normed, axis=0, keepdims=True)
    return factor * inner, gain_grad, jnp.sum(back, axis=0, keepdims=True)


def return_kernel(
    plan, count, plan_down, count_down, me_ref, y_hbm, cot_ref, vec_ref, ht_ref, mixed_hbm,
    rise_ref, act_hbm, *rest
):
    pieces = rest[:count]
    down_pieces = rest[count : count + count_down]
    (
        grad_ref, out_ref, keep_ref, send_ref, sums_ref,
        act_ref, du_ref, w_ref, wd_ref, part_ref, out_grad_ref, y_ref, mixed_ref,
        sems, down_sems, late_sems,
    ) = rest[count + count_down :]
    step = pl.program_id(0)
    width = cot_ref.shape[1]
    chunk = rise_ref.shape[1]
    block = width // BLOCKS
    copies = [
        pltpu.make_async_copy(*pair)
        for pair in piece_pairs(pieces, plan, me_ref[0], block, w_ref, sems)
    ]
    copies.append(pltpu.make_async_copy(y_hbm, y_ref, late_sems.at[0]))
    copies.append(pltpu.make_async_copy(mixed_hbm, mixed_ref, late_sems.at[1]))
    copies.append(pltpu.make_async_copy(act_hbm, act_ref, late_sems.at[2]))

    @pl.when(step == 0)
    def _():
        down_copies = load_pieces(
            down_pieces, plan_down, me_ref[0], wd_ref.shape[0] // BLOCKS, wd_ref, down_sems
        )
        for copy in copies:
            copy.start()
        out_grad_ref[...] = jnp.zeros_like(out_grad_ref)
        sums_ref[...] = jnp.zeros_like(sums_ref)
        for copy in down_copies:
            copy.wait()

    @pl.when(step < pl.num_programs(0) - 1)
    def _():
        start = pl.multiple_of(step * chunk, chunk)
        down = wd_ref[pl.ds(start, chunk), :]
        grad_upper = (
            dot_nt(cot_ref[...], down) * rise_ref[...].astype(jnp.float32)
        ).astype(jnp.bfloat16)
        du_ref[:, pl.ds(start, chunk)] = grad_upper
        part_ref[...] = dot_nn(ht_ref[...], grad_upper)
        split_blocks(part_ref, me_ref[0], block, keep_ref, send_ref)

    @pl.when(step == pl.num_programs(0) - 1)
    def _():
        for copy in copies:
            copy.wait()
        size = mixed_ref.shape[2]

        def body(place, carry):
            rows = pl.ds(pl.multiple_of(place * size, size), size)
            total = y_ref[rows, :] + dot_nn(act_ref[rows, :], wd_ref[...])
            out_ref[rows, :] = total.astype(jnp.bfloat16)
            back = dot_nt(du_ref[rows, :], w_ref[...])
            normed, factor = norm_parts(y_ref[rows, :])
            through, gain_grad, bias_grad = norm_back(back, normed, factor, vec_ref[2:3])
            sums_ref[0:1] += gain_grad
            sums_ref[1:2] += bias_grad
            grad = cot_ref[rows, :].astype(jnp.float32) + through
            grad_ref[rows, :] = grad
            out_grad_ref[...] += dot_nn(mixed_ref[place], grad.astype(jnp.bfloat16))
            return carry

        lax.fori_loop(0, mixed_ref.shape[0], body, 0)
        split_blocks(out_grad_ref, me_ref[0], block, keep_ref, send_ref)


def feed_return(y_one, cotangent, vec, h_t, mixed, rise, active, me, pieces, plan, down_pieces, plan_down):
    count, width = cotangent.shape
    hidden = active.shape[1]
    chunk = hidden // 4
    shapes = (
        jax.ShapeDtypeStruct((count, width), jnp.float32),
        jax.ShapeDtypeStruct((count, width), jnp.bfloat16),
        *split_shapes(width // BLOCKS, hidden + width),
        jax.ShapeDtypeStruct((8, width), jnp.float32),
    )
    return pl.pallas_call(
        functools.partial(
            return_kernel, plan, len(pieces), plan_down, len(down_pieces)
        ),
        grid=(hidden // chunk + 1,),
        in_specs=[pl.BlockSpec(memory_space=pltpu.SMEM)]
        + any_specs([y_one])
        + [whole_spec(v.shape) for v in (cotangent, vec, h_t)]
        + any_specs([mixed])
        + [
            pl.BlockSpec((count, chunk), lambda j: (0, jnp.minimum(j, 3))),
            pl.BlockSpec(memory_space=pl.ANY),
        ]
        + any_specs(pieces)
        + any_specs(down_pieces),
        out_specs=[whole_spec(s.shape) for s in shapes[:2]]
        + [pl.BlockSpec((4, width // BLOCKS, width), lambda j: (0, 0, j))] * 2
        + [whole_spec((8, width))],
        out_shape=shapes,
        scratch_shapes=[
            pltpu.VMEM((count, hidden), jnp.bfloat16),
            pltpu.VMEM((count, hidden), jnp.bfloat16),
            pltpu.VMEM((width, hidden), jnp.bfloat16),
            pltpu.VMEM((hidden, width), jnp.bfloat16),
            pltpu.VMEM((width, chunk), jnp.float32),
            pltpu.VMEM((width, width), jnp.float32),
            pltpu.VMEM((count, width), jnp.float32),
            pltpu.VMEM(mixed.shape, jnp.bfloat16),
            pltpu.SemaphoreType.DMA((BLOCKS,)),
            pltpu.SemaphoreType.DMA((BLOCKS,)),
            pltpu.SemaphoreType.DMA((3,)),
        ],
        compiler_params=kernel_params(60),
        cost_estimate=pl.CostEstimate(
            flops=10**9, bytes_accessed=10**6, transcendentals=0
        ),
    )(me, y_one, cotangent, vec, h_t, mixed, rise, active, *pieces, *down_pieces)


def heads_back(queries, keys, values, grads_t, mixed_t, expos, inverses, head_dim):
    length = queries.shape[0]
    lane = lax.broadcasted_iota(jnp.int32, (length, 128), 1)
    inside = lane < head_dim
    one_lane = jnp.where(lane < 2, 1.0, 0.0).astype(jnp.bfloat16)
    pad_rows = jnp.zeros((126, length), jnp.bfloat16)
    gap_rows = jnp.zeros((head_dim, length), jnp.bfloat16)
    keys_t = flip_axes(keys)
    value_wide = jnp.concatenate([values, one_lane], axis=1)
    grad_pair = grads_t.astype(jnp.float32)
    product = grad_pair * mixed_t.astype(jnp.float32)
    spans = [slice(half * head_dim, (half + 1) * head_dim) for half in range(2)]
    scaled = [
        (grad_pair[span] * inverse).astype(jnp.bfloat16)
        for span, inverse in zip(spans, inverses)
    ]
    scaled_pair = jnp.concatenate(scaled, axis=0)
    dv = []
    dk = []
    dq = []
    for half, span in enumerate(spans):
        delta = -jnp.sum(product[span], axis=0, keepdims=True) * inverses[half]
        high = delta.astype(jnp.bfloat16)
        low = (delta - high.astype(jnp.float32)).astype(jnp.bfloat16)
        first = [scaled[0], gap_rows] if half == 0 else [gap_rows, scaled[1]]
        grad_wide = jnp.concatenate(first + [high, low, pad_rows], axis=0)
        expo = expos[half]
        grad_scores = (expo.astype(jnp.float32) * dot_nn(value_wide, grad_wide)).astype(
            jnp.bfloat16
        )
        dv.append(dot_nt(expo, scaled_pair))
        dk.append(dot_nn(grad_scores, queries))
        dq.append(dot_nn(keys_t, grad_scores)[span] * (1.0 / head_dim**0.5))
    return (
        jnp.concatenate(dq, axis=0).T.astype(jnp.bfloat16),
        jnp.where(inside, dk[0], dk[1]).astype(jnp.bfloat16),
        jnp.where(inside, dv[0], dv[1]).astype(jnp.bfloat16),
    )


def backward_kernel(
    plan, count, groups, me_ref, grad_ref, q_ref, k_ref, v_ref, expo_ref, inv_ref, mixed_ref, ht_ref,
    *rest
):
    pieces = rest[:count]
    dqkv_ref, keep_ref, send_ref, dot_ref, acc_ref, wout_ref, sems = rest[count:]
    row = pl.program_id(0)
    group = pl.program_id(1)
    length, width = grad_ref.shape[1:]
    head_dim = width // H
    block = width // BLOCKS
    wide = q_ref.shape[2]
    me = me_ref[0]

    @pl.when((row == 0) & (group == 0))
    def _():
        copies = load_pieces(
            pieces, plan, me, block, wout_ref, sems, pieces[0].shape[2] - width
        )
        acc_ref[...] = jnp.zeros_like(acc_ref)
        for copy in copies:
            copy.wait()

    @pl.when(group == 0)
    def _():
        attn_in = grad_ref[0].astype(jnp.bfloat16)
        dot_ref[...] = dot_nt(wout_ref[...], attn_in).astype(jnp.bfloat16)

    results = []
    for pair in range(wide // 128):
        cols = slice(pair * 128, pair * 128 + 128)
        start = pl.multiple_of(group * wide + pair * 128, 128)
        results.append(
            heads_back(
                q_ref[0, :, cols], k_ref[0, :, cols], v_ref[0, :, cols],
                dot_ref[pl.ds(start, 128), :], mixed_ref[0, cols, :],
                [expo_ref[0, 2 * pair + half] for half in range(2)],
                [inv_ref[0, 2 * pair + half] for half in range(2)],
                head_dim,
            )
        )
    joined = [jnp.concatenate(list(values), axis=1) for values in zip(*results)]
    for place, value in enumerate(joined):
        start = pl.multiple_of(place * width + group * wide, 128)
        acc_ref[:, pl.ds(start, wide)] += dot_nn(ht_ref[0], value)
        dqkv_ref[0, :, pl.ds(start, wide)] = value

    @pl.when((row == pl.num_programs(0) - 1) & (group == groups - 1))
    def _():
        split_blocks(acc_ref, me, block, keep_ref, send_ref)


def backward(grad_y, saved, me, pieces, plan):
    rows, length, width = grad_y.shape
    qkv, expo, inverse, mixed, h_t = saved
    wide = 256
    heads = wide * H // width
    groups = width // wide

    def column_spec(kind):
        return pl.BlockSpec((1, length, wide), lambda r, g: (r, 0, kind * groups + g))

    inputs = [me, grad_y, qkv, qkv, qkv, expo, inverse, mixed, h_t, *pieces]
    in_specs = [
        pl.BlockSpec(memory_space=pltpu.SMEM),
        row_spec(grad_y.shape),
        column_spec(0),
        column_spec(1),
        column_spec(2),
        pl.BlockSpec((1, heads, length, length), lambda r, g: (r, g, 0, 0)),
        pl.BlockSpec((1, heads, 1, length), lambda r, g: (r, g, 0, 0)),
        pl.BlockSpec((1, wide, length), lambda r, g: (r, g, 0)),
        row_spec(h_t.shape),
    ] + any_specs(pieces)
    shapes = [jax.ShapeDtypeStruct((rows, length, 3 * width), jnp.bfloat16)]
    shapes += split_shapes(width // BLOCKS, 3 * width)
    return pl.pallas_call(
        functools.partial(backward_kernel, plan, len(pieces), groups),
        grid=(rows, groups),
        in_specs=in_specs,
        out_specs=[row_spec(shapes[0].shape)] + [whole_spec(s.shape) for s in shapes[1:]],
        out_shape=shapes,
        scratch_shapes=[
            pltpu.VMEM((width, length), jnp.bfloat16),
            pltpu.VMEM((width, 3 * width), jnp.float32),
            pltpu.VMEM((width, width), jnp.bfloat16),
            pltpu.SemaphoreType.DMA((BLOCKS,)),
        ],
        compiler_params=kernel_params(58),
        cost_estimate=pl.CostEstimate(flops=10**9, bytes_accessed=10**6, transcendentals=0),
    )(*inputs)


def finish_kernel(
    plan, count, me_ref, grad_ref, x_ref, dqkv_ref, vec_ref, ffn_sums_ref, *rest
):
    pieces = rest[:count]
    tokens_grad_ref, keep_ref, send_ref, w_ref, vec_acc, sems = rest[count:]
    row = pl.program_id(0)
    block = w_ref.shape[0] // BLOCKS
    normed, factor = norm_parts(x_ref[0].astype(jnp.float32))

    @pl.when(row == 0)
    def _():
        copies = load_pieces(pieces, plan, me_ref[0], block, w_ref, sems)
        vec_acc[...] = jnp.zeros_like(vec_acc)
        vec_acc[2:4] = ffn_sums_ref[0:2]
        for copy in copies:
            copy.wait()

    back = dot_nt(dqkv_ref[0], w_ref[...])
    through, gain_grad, bias_grad = norm_back(back, normed, factor, vec_ref[0:1])
    vec_acc[0:1] += gain_grad
    vec_acc[1:2] += bias_grad
    tokens_grad_ref[0] = (grad_ref[0] + through).astype(jnp.bfloat16)

    @pl.when(row == pl.num_programs(0) - 1)
    def _():
        vec_t = vec_acc[...].T
        vec_acc[...] = jnp.zeros_like(vec_acc)
        w_ref[:, :128] = vec_t.astype(jnp.bfloat16)
        for place, bits in enumerate(PLACES):
            start = pl.multiple_of((me_ref[0] ^ bits) * block, 16)
            keep_ref[place] = w_ref[pl.ds(start, block), :128]
            start = pl.multiple_of((me_ref[0] ^ bits ^ CORE) * block, 16)
            send_ref[place] = w_ref[pl.ds(start, block), :128]


def finish(grad_y, tokens, dqkv, vec, ffn_sums, me, pieces, plan):
    rows, length, width = tokens.shape
    shapes = [jax.ShapeDtypeStruct(tokens.shape, jnp.bfloat16)]
    shapes += split_shapes(width // BLOCKS, 128)
    return pl.pallas_call(
        functools.partial(finish_kernel, plan, len(pieces)),
        grid=(rows,),
        in_specs=[pl.BlockSpec(memory_space=pltpu.SMEM)]
        + [row_spec(v.shape) for v in (grad_y, tokens, dqkv)]
        + [whole_spec(vec.shape), whole_spec(ffn_sums.shape)]
        + any_specs(pieces),
        out_specs=[row_spec(tokens.shape)] + [whole_spec(s.shape) for s in shapes[1:]],
        out_shape=shapes,
        scratch_shapes=[
            pltpu.VMEM((width, 3 * width), jnp.bfloat16),
            pltpu.VMEM((128, width), jnp.float32),
            pltpu.SemaphoreType.DMA((BLOCKS,)),
        ],
        compiler_params=kernel_params(58),
        cost_estimate=pl.CostEstimate(flops=10**9, bytes_accessed=10**6, transcendentals=0),
    )(me, grad_y, tokens, dqkv, vec, ffn_sums, *pieces)


def layer(ranks, inner, tokens, segments, cotangent, me, front, counts):
    rows, length, width = tokens.shape
    flat_shape = (rows * length, width)
    flat_cot = cotangent.reshape(flat_shape)
    first = front[0]
    near = direct(ranks, inner)
    *saved, o, vec = attend(tokens, segments, me, *first)
    if near:
        _, sides, parts, keep, other = front
        *values, o, other = together([*sides, *parts, o, other])
        sides, parts = values[:4], values[4:]
        parts.append(swap_inner(parts[0], inner - 1, inner))
        own_third = jnp.concatenate(by_bits(parts, lax.axis_index("fsdp")), axis=0)
        second = with_core(sides)
        keep, other = halve_tables(keep + other, NEAR_X)
        own_third, second[0][1] = together([own_third, second[0][1]])
        sides = gather_sides(own_third)
    else:
        second, third = front[1:]
    y_one, h_t, *down_parts, rise, active = feed_forward(
        tokens.reshape(flat_shape), o.reshape(flat_shape), flat_cot, vec, me, *second
    )
    if near:
        *sides, y_one, down_parts[1], other = together([*sides, y_one, down_parts[1], other])
        keep, other = halve_tables(keep + other, NEAR_Y)
        third = with_core(sides)
        down_parts = scatter_core(*down_parts)
        y_one, *down_parts = together([y_one, *down_parts])
        down_received = scatter_sides(down_parts)
    grad_y, layer_output, *up_parts, ffn_sums = feed_return(
        y_one, flat_cot, vec, h_t, saved[3], rise, active, me, *second, *third
    )
    if near:
        *down_received, up_parts[1], grad_y, other = together(
            [*down_received, up_parts[1], grad_y, other]
        )
        counts = keep + other
        others = [swap_inner(counts, k, inner) for k in range(1, inner)]
        parts = scatter_core(*up_parts)
        down_mine = add(down_parts[0], *down_received)
        *values, grad_y, down_mine = together([*parts, *others, grad_y, down_mine])
        parts, others = values[:4], values[4:]
        counts = sum(others, counts)
        received = scatter_sides(parts)
        size = down_mine.shape[0] // inner
        pieces = [down_mine[k * size : (k + 1) * size] for k in range(inner)]
        pieces = by_bits(pieces, lax.axis_index("fsdp"))
        down_inner = [swap_inner(pieces[k], k, inner) for k in range(1, inner - 1)]
    grad_y = grad_y.reshape(tokens.shape)
    dqkv, *early = backward(grad_y, saved, me, *second)
    if near:
        *values, dqkv, early[1], piece, counts = together(
            [*received, *down_inner, dqkv, early[1], pieces[-1], counts]
        )
        received, down_inner = values[:3], values[3:]
        other = swap(counts, NEAR_Y)
        down_inner.append(swap_inner(piece, inner - 1, inner))
        early_parts = scatter_core(*early)
        up_mine = add(parts[0], *received)
        size = up_mine.shape[0] // inner
        up_pieces = [up_mine[k * size : (k + 1) * size] for k in range(inner)]
        up_pieces = by_bits(up_pieces, lax.axis_index("fsdp"))
        *values, dqkv, other = together([*early_parts, *down_inner, *up_pieces, dqkv, other])
        early_parts, down_inner = values[:4], values[4 : 3 + inner]
        up_pieces = values[3 + inner :]
        counts = double_tables(counts, other, NEAR_Y)
        other = swap(counts, NEAR_X)
        dqkv, other = together([dqkv, other])
        counts = double_tables(counts, other, NEAR_X)
        down_sum = sum_parts(pieces[:1] + down_inner)
        early_received = scatter_sides(early_parts)
        up_inner = [swap_inner(up_pieces[k], k, inner) for k in range(1, inner - 1)]
    tokens_grad, *late = finish(grad_y, tokens, dqkv, vec, ffn_sums, me, *first)
    if near:
        *up_inner, tokens_grad, late[1], piece, counts = together(
            [*up_inner, tokens_grad, late[1], up_pieces[-1], counts]
        )
        late_parts = scatter_core(*late)
        other = swap(counts, CORE)
        *late_parts, other, piece = together([*late_parts, other, piece])
        up_inner.append(swap_inner(piece, inner - 1, inner))
        counts = double_tables(counts, other, CORE)
        late_received = scatter_sides(late_parts)
        values = together([*early_received, *late_received])
        early_received, late_received = values[:3], values[3:]
        early_mine = add(early_parts[0], *early_received)
        late_mine = add(late_parts[0], *late_received)
        both = jnp.concatenate([early_mine, late_mine], axis=1)
        both = sum_parts(scatter_inner(both, inner))
        up_sum = sum_parts(up_pieces[:1] + up_inner)
        early_sum, late_sum = both[:, : 3 * width], both[:, 3 * width :]
    else:
        up_sum, down_sum, early_sum, late_sum = [
            scatter_whole(*v) for v in (up_parts, down_parts, early, late)
        ]
    hidden = active.shape[1]
    return (
        layer_output.reshape(tokens.shape),
        tokens_grad,
        early_sum,
        up_sum[:, hidden:],
        up_sum[:, :hidden],
        down_sum,
        late_sum,
        counts,
    )


def per_device(
    ranks,
    inner,
    tokens,
    segment_ids,
    bucket_ids,
    cotangent,
    qkv_weight,
    out_weight,
    up_weight,
    down_weight,
    attn_gain,
    attn_bias,
    ffn_gain,
    ffn_bias,
):
    vectors = jnp.stack([attn_gain, attn_bias, ffn_gain, ffn_bias], axis=1)
    vectors = jnp.pad(vectors, ((0, 0), (0, 124)))
    ids = bucket_ids.reshape(-1, bucket_ids.shape[2]).T
    counts = count_buckets(ids)
    segments = segment_ids.astype(jnp.float32)[:, None, :]
    shards = (
        jnp.concatenate([qkv_weight, vectors], axis=1),
        jnp.concatenate([up_weight, out_weight], axis=1),
        down_weight,
    )
    if direct(ranks, inner):
        me = lax.axis_index("dp").reshape(1).astype(jnp.int32)
        *front, segments = gather_first(shards, inner, counts, segments)
    else:
        me = jnp.zeros((1,), jnp.int32)
        front = [gather_whole(shard) for shard in shards]
        counts = lax.psum(counts, BOTH)
    *results, vec_sums, counts = layer(
        ranks, inner, tokens, segments, cotangent, me, front, counts
    )
    return (*results, *[vec_sums[:, place] for place in range(4)], counts)


def solution(mesh):
    placed = (
        P(("dp", "fsdp"), None, None),
        P(("dp", "fsdp"), None),
        P(("dp", "fsdp"), None, None),
        P(("dp", "fsdp"), None, None),
        P(("dp", "fsdp"), None),
        P(("dp", "fsdp"), None),
        P(("dp", "fsdp"), None),
        P(("dp", "fsdp"), None),
        P(("dp", "fsdp")),
        P(("dp", "fsdp")),
        P(("dp", "fsdp")),
        P(("dp", "fsdp")),
    )
    return jax.shard_map(
        functools.partial(per_device, mesh.shape["dp"], mesh.shape["fsdp"]),
        mesh=mesh,
        in_specs=placed,
        out_specs=(
            P(("dp", "fsdp"), None, None),
            P(("dp", "fsdp"), None, None),
            P(("dp", "fsdp"), None),
            P(("dp", "fsdp"), None),
            P(("dp", "fsdp"), None),
            P(("dp", "fsdp"), None),
            P(("dp", "fsdp")),
            P(("dp", "fsdp")),
            P(("dp", "fsdp")),
            P(("dp", "fsdp")),
            P(),
        ),
        check_vma=False,
    )
```
